256 devices in a mesh: seq: 32 (over x, z), mp: 8 (over y, core).
Axes of the slice: x: 4, y: 4, z: 8, core: 2. Of those that a mesh axis runs over, the one named last changes fastest.
Arguments:
- queries: bfloat16 [16384, 3072], P(('seq', 'mp')), may hold values from -128 to 128
- keys: bfloat16 [16384, 3072], P(('seq', 'mp')), may hold values from -4 to 4
- values: bfloat16 [16384, 3072], P(('seq', 'mp')), may hold values from -6 to 6
- out_grad: bfloat16 [16384, 3072], P(('seq', 'mp')), may hold values from -6 to 6
- window_lists: int32 [256, 27], P('seq'), may hold values from -1 to 255, as said below
- valid_counts: int32 [256], replicated, may hold values from 1 to 64, as said below
Outputs:
- attended: bfloat16 [16384, 3072], P(('seq', 'mp'))
- grad_queries: bfloat16 [16384, 3072], P(('seq', 'mp'))
- grad_keys: bfloat16 [16384, 3072], P(('seq', 'mp'))
- grad_values: bfloat16 [16384, 3072], P(('seq', 'mp'))
The draws below stay inside these ranges and needn't reach their ends.
Inputs may be any that keep to these rules, and one draw needn't show every extreme that they name: `window_lists`: each tile's list holds the tile itself and some of the other tiles of its 3 x 3 x 3 block of tiles inside the grid of 8 x 8 x 4 tiles, each at most once, and -1 in the other slots. `valid_counts`: tiles that are not in the last tile layer or the last tile row hold 64 valid tokens.
All inputs are finite; a program needn't handle non-finite values.
Results may differ from the reference program's by a relative error of at most 0.006.
Values may be sent and summed in bfloat16 or wider, within the bound.
A program may use at most 128 MiB of HBM per device.

```python
import math
import jax
import jax.numpy as jnp
import numpy as np
from jax import lax

HEADS = 24
HEAD_DIM = 128
D = 3072
TILE = 64
WINDOW = 27
TLAYERS = 8
TW = 4
NH = 8
TILES = 256
TOKENS = 16384


def shared_keys(key):
    return jnp.clip(jax.random.normal(key, (TOKENS, D), jnp.float32), -4.0, 4.0)


def draw_keys(key, part):
    base = shared_keys(key)
    return base.astype(jnp.bfloat16)


def draw_queries(key, part):
    key = jax.random.fold_in(key, 12)
    fresh = jnp.clip(jax.random.normal(jax.random.fold_in(key, 1), (TOKENS, D), jnp.float32), -4.0, 4.0)
    return fresh.astype(jnp.bfloat16)


def grid_places():
    ids = jnp.arange(TILES, dtype=jnp.int32)
    layer = ids // (NH * TW)
    row = ids // TW % NH
    column = ids % TW
    return (layer, row, column)


def draw_window_lists(key, part):
    key = jax.random.fold_in(key, 13)
    layer, row, column = grid_places()
    steps = np.array([(a, b, c) for a in (-1, 0, 1) for b in (-1, 0, 1) for c in (-1, 0, 1)], dtype=np.int32)
    next_layer = layer[:, None] + steps[None, :, 0]
    next_row = row[:, None] + steps[None, :, 1]
    next_column = column[:, None] + steps[None, :, 2]
    inside = (next_layer >= 0) & (next_layer < TLAYERS) & (next_row >= 0) & (next_row < NH) & (next_column >= 0) & (next_column < TW)
    itself = (steps[:, 0] == 0) & (steps[:, 1] == 0) & (steps[:, 2] == 0)
    keep = (jax.random.randint(key, (TILES, WINDOW), 0, 4) != 0) | itself[None, :]
    target = (next_layer * NH + next_row) * TW + next_column
    return jnp.where(inside & keep, target, -1).astype(jnp.int32)


def draw_valid_counts(key, part):
    key = jax.random.fold_in(key, 14)
    layer, row, column = grid_places()
    border = (layer == TLAYERS - 1) | (row == NH - 1)
    partial_value = jax.random.randint(key, (TILES,), 1, TILE + 1)
    return jnp.where(border, partial_value, TILE).astype(jnp.int32)


def steps_of(rng, shape, shards, least, top_value):
    def one(position, parts):
        draws = jax.random.uniform(jax.random.fold_in(jax.random.fold_in(rng, 6), position), (parts,), jnp.float32, least / len(shards), top_value / len(shards))
        return jnp.repeat(jnp.exp(draws), shape[position] // parts).reshape((-1,) + (1,) * (len(shape) - position - 1))

    factor_of = one(*shards[0])
    for cut in shards[1:]:
        factor_of = factor_of * one(*cut)
    return factor_of


def gaussian(key, shape, deviation, most, split=(), kind=jnp.bfloat16):
    result = deviation * jax.random.normal(key, shape, jnp.float32)
    if split:
        result = result * steps_of(key, shape, split, -0.22, 0.18)
    return jnp.clip(result, -most, most).astype(kind)


def setup_inputs(seed: int = 0) -> dict:
    key_of = jax.random.split(jax.random.key(seed), 7)
    return {
        "queries": draw_queries(jax.random.fold_in(key_of[6], 71), 0),
        "keys": draw_keys(jax.random.fold_in(key_of[6], 71), 0),
        "values": gaussian(key_of[2], (TOKENS, D), 1.0, 6.0, ((0, 256),)),
        "out_grad": gaussian(key_of[3], (TOKENS, D), 1.0, 6.0, ((0, 256),)),
        "window_lists": draw_window_lists(jax.random.fold_in(key_of[6], 71), 0),
        "valid_counts": draw_valid_counts(jax.random.fold_in(key_of[6], 71), 0),
    }


def reference(queries, keys, values, out_grad, window_lists, valid_counts):
    scale = 1.0 / math.sqrt(HEAD_DIM)
    live = window_lists >= 0
    safe = jnp.maximum(window_lists, 0).astype(jnp.int32)
    places = jnp.arange(TILE, dtype=jnp.int32)
    key_count = valid_counts[safe]
    key_ok = (live[:, :, None] & (places[None, None, :] < key_count[:, :, None])).reshape(TILES, WINDOW * TILE)
    query_ok = places[None, :] < valid_counts[:, None]
    query_mask = query_ok.astype(jnp.float32)[:, :, None]
    q_all = queries.reshape(TILES, TILE, HEADS, HEAD_DIM)
    k_all = keys.reshape(TILES, TILE, HEADS, HEAD_DIM)
    v_all = values.reshape(TILES, TILE, HEADS, HEAD_DIM)
    g_all = out_grad.reshape(TILES, TILE, HEADS, HEAD_DIM)

    def one_head(head):
        q = lax.dynamic_index_in_dim(q_all, head, 2, keepdims=False)
        k = lax.dynamic_index_in_dim(k_all, head, 2, keepdims=False)
        v = lax.dynamic_index_in_dim(v_all, head, 2, keepdims=False)
        g = lax.dynamic_index_in_dim(g_all, head, 2, keepdims=False)
        g = g * query_ok[:, :, None].astype(jnp.bfloat16)
        k_win = k[safe].reshape(TILES, WINDOW * TILE, HEAD_DIM).astype(jnp.float32)
        v_win = v[safe].reshape(TILES, WINDOW * TILE, HEAD_DIM).astype(jnp.float32)
        scores = jnp.einsum('tqd,tkd->tqk', q.astype(jnp.float32), k_win) * scale
        scores = jnp.where(key_ok[:, None, :], scores, -1e+30)
        top = lax.optimization_barrier(jnp.max(scores, axis=-1, keepdims=True))
        expo = jnp.exp(scores - top)
        probs = expo / lax.optimization_barrier(jnp.sum(expo, axis=-1, keepdims=True))
        probs_low = probs.astype(jnp.bfloat16)
        attended = jnp.einsum('tqk,tkd->tqd', probs_low.astype(jnp.float32), v_win) * query_mask
        attended = attended.astype(jnp.bfloat16)
        delta = lax.optimization_barrier(jnp.sum(g.astype(jnp.float32) * attended.astype(jnp.float32), axis=-1))
        dprobs = jnp.einsum('tqd,tkd->tqk', g.astype(jnp.float32), v_win)
        dscores = (probs * (dprobs - delta[:, :, None]) * scale).astype(jnp.bfloat16)
        grad_q = jnp.einsum('tqk,tkd->tqd', dscores.astype(jnp.float32), k_win).astype(jnp.bfloat16)
        grad_kw = jnp.einsum('tqk,tqd->tkd', dscores.astype(jnp.float32), q.astype(jnp.float32))
        grad_vw = jnp.einsum('tqk,tqd->tkd', probs_low.astype(jnp.float32), g.astype(jnp.float32))
        slot_mask = live.astype(jnp.float32)[:, :, None, None]
        grad_kw = grad_kw.reshape(TILES, WINDOW, TILE, HEAD_DIM) * slot_mask
        grad_vw = grad_vw.reshape(TILES, WINDOW, TILE, HEAD_DIM) * slot_mask
        grad_k = jnp.zeros((TILES, TILE, HEAD_DIM), jnp.float32).at[safe.reshape(-1)].add(grad_kw.reshape(TILES * WINDOW, TILE, HEAD_DIM))
        grad_v = jnp.zeros((TILES, TILE, HEAD_DIM), jnp.float32).at[safe.reshape(-1)].add(grad_vw.reshape(TILES * WINDOW, TILE, HEAD_DIM))
        return (attended, grad_q, grad_k.astype(jnp.bfloat16), grad_v.astype(jnp.bfloat16))
    stacked = lax.map(one_head, jnp.arange(HEADS, dtype=jnp.int32))

    def relay(block):
        return jnp.transpose(block, (1, 2, 0, 3)).reshape(TOKENS, D)
    return (relay(stacked[0]), relay(stacked[1]), relay(stacked[2]), relay(stacked[3]))
```

```python
import functools
import math

import jax
import jax.numpy as jnp
from jax import lax
from jax.experimental import pallas as pl
from jax.experimental.pallas import tpu as pltpu
from jax.sharding import PartitionSpec as P

HEADS = 24
HEAD_DIM = 128
D = HEADS * HEAD_DIM
TILE = 64
TLAYERS = 8
NH = 8
TW = 4
NX = 4
NZ = 8
NM = 8
NEG = -1e30
SCALE = 1.0 / math.sqrt(HEAD_DIM)
EXP2_SCALE = SCALE / math.log(2.0)
MESH = pl.DeviceIdType.MESH
BF16 = jnp.bfloat16
F32 = jnp.float32


def place():
    seat = lax.axis_index("seq")
    m = lax.axis_index("mp")
    x = seat // NZ
    z = lax.rem(seat, NZ)
    return x, z, m


def worker_of(part, head):
    rest_a = head - 8
    z_a = jnp.where(
        head < 8, 3 + 4 * lax.rem(head, 2), 2 + lax.rem(rest_a + 8, 2) + 4 * (lax.rem(rest_a + 8, 4) // 2)
    )
    m_a = jnp.where(head < 8, head // 2, 2 + head // 4)
    z_b = jnp.where(head < 16, lax.rem(head, 2) + 4 * (lax.rem(head, 4) // 2), 4 * lax.rem(head, 2))
    m_b = jnp.where(head < 16, head // 4, head // 2 - 4)
    return jnp.where(part == 0, z_a, z_b), jnp.where(part == 0, m_a, m_b)


def work_of(z, m):
    zq = lax.rem(z, 4)
    zh = z // 4
    part = jnp.where(zq >= 2, 0, 1)
    head_a = jnp.where(m < 4, 2 * m + zh, 4 * m - 8 + 2 * zh + (zq - 2))
    head_b = jnp.where(m < 4, 4 * m + 2 * zh + zq, 2 * m + 8 + zh)
    active = jnp.where(m < 4, zq != 2, zq != 1)
    return part, jnp.where(part == 0, head_a, head_b), active


def greet_plane(x, z, m):
    barrier = pltpu.get_barrier_semaphore()

    def greet(i, carry):
        zz = i // NM
        mm = lax.rem(i, NM)

        @pl.when(jnp.logical_or(zz != z, mm != m))
        def _():
            pl.semaphore_signal(barrier, inc=1, device_id=(x * NZ + zz, mm), device_id_type=MESH)

        return carry

    lax.fori_loop(0, NZ * NM, greet, 0)

    @pl.when(x > 0)
    def _():
        pl.semaphore_signal(barrier, inc=1, device_id=((x - 1) * NZ + z, m), device_id_type=MESH)

    @pl.when(x < NX - 1)
    def _():
        pl.semaphore_signal(barrier, inc=1, device_id=((x + 1) * NZ + z, m), device_id_type=MESH)

    peers = NZ * NM - 1 + jnp.where(x > 0, 1, 0) + jnp.where(x < NX - 1, 1, 0)
    pl.semaphore_wait(barrier, peers)


def wait_for(ref, sem):
    pltpu.make_async_copy(ref, ref, sem).wait()


def spread_kernel(
    q_ref, k_ref, v_ref, g_ref, flag_ref,
    qg_out, pool_out, flag_out,
    blank, send_sem, extra_sem, flag_send, kv_sem, qg_sem, flag_sem, halo_send, halo_sem, blank_sem,
):
    x, z, m = place()
    zh = z // 4
    zl = lax.rem(z, 4)
    h = 2 * zl + m // 4
    w = lax.rem(m, 4)
    own = zl // 2
    part, _, active = work_of(z, m)
    row0 = jnp.where(part == 0, 1, 0)
    blank[...] = jnp.zeros_like(blank)
    greet_plane(x, z, m)

    unused = jnp.where(part == 0, 0, 5)
    for layer in range(4):
        pltpu.make_async_copy(blank, pool_out.at[layer, pl.ds(unused, 1)], blank_sem.at[layer]).start()

    def blank_layer(layer, begin):
        copies = [
            pltpu.make_async_copy(blank, pool_out.at[layer, pl.ds(row0 + r, 1)], blank_sem.at[4 + r])
            for r in range(5)
        ]
        for c in copies:
            c.start() if begin else c.wait()

    @pl.when(x == 0)
    def _():
        blank_layer(0, True)

    @pl.when(x == NX - 1)
    def _():
        blank_layer(3, True)

    first = lax.rem(m * 3 + z * 5, HEADS)
    two = jnp.logical_or(h == 3, h == 4)
    other_row = jnp.where(h == 3, 0, 5)
    own_row = lax.rem(h, 4) + 1
    half = pl.ds(pl.multiple_of(lax.rem(w, 2) * TILE, TILE), TILE)

    def send_kv(j, carry):
        head = lax.rem(j + first, HEADS)
        columns = pl.ds(pl.multiple_of(head * HEAD_DIM, HEAD_DIM), HEAD_DIM)
        wz, wm = worker_of(own, head)
        for i, ref in ((0, k_ref), (1, v_ref)):
            pltpu.make_async_remote_copy(
                src_ref=ref.at[:, columns],
                dst_ref=pool_out.at[1 + zh, own_row, i, w // 2, half, :],
                send_sem=send_sem.at[i],
                recv_sem=kv_sem.at[zh, own_row],
                device_id=(x * NZ + wz, wm),
                device_id_type=MESH,
            ).start()

        @pl.when(two)
        def _():
            oz, om = worker_of(1 - own, head)
            for i, ref in ((0, k_ref), (1, v_ref)):
                pltpu.make_async_remote_copy(
                    src_ref=ref.at[:, columns],
                    dst_ref=pool_out.at[1 + zh, other_row, i, w // 2, half, :],
                    send_sem=extra_sem.at[i],
                    recv_sem=kv_sem.at[zh, other_row],
                    device_id=(x * NZ + oz, om),
                    device_id_type=MESH,
                ).start()

        return carry

    lax.fori_loop(0, HEADS, send_kv, 0)

    def send_flags(j, carry):
        wz, wm = worker_of(own, m * 3 + j)
        pltpu.make_async_remote_copy(
            src_ref=flag_ref.at[0],
            dst_ref=flag_out.at[zh, lax.rem(zl, 2)],
            send_sem=flag_send.at[j],
            recv_sem=flag_sem.at[zh, lax.rem(zl, 2)],
            device_id=(x * NZ + wz, wm),
            device_id_type=MESH,
        ).start()
        return carry

    lax.fori_loop(0, 3, send_flags, 0)

    def send_qg(j, carry):
        head = lax.rem(j + first, HEADS)
        columns = pl.ds(pl.multiple_of(head * HEAD_DIM, HEAD_DIM), HEAD_DIM)
        wz, wm = worker_of(own, head)
        for i, ref in ((0, q_ref), (1, g_ref)):
            pltpu.make_async_remote_copy(
                src_ref=ref.at[:, columns],
                dst_ref=qg_out.at[i, zh, lax.rem(h, 4), pl.ds(pl.multiple_of(w * TILE, TILE), TILE), :],
                send_sem=send_sem.at[2 + i],
                recv_sem=qg_sem,
                device_id=(x * NZ + wz, wm),
                device_id_type=MESH,
            ).start()
        return carry

    lax.fori_loop(0, HEADS, send_qg, 0)

    @pl.when(active)
    def _():
        def forward(r, carry):
            row = row0 + r
            wait_for(pool_out.at[1, row], kv_sem.at[0, row])

            @pl.when(x > 0)
            def _():
                pltpu.make_async_remote_copy(
                    src_ref=pool_out.at[1, row],
                    dst_ref=pool_out.at[3, row],
                    send_sem=halo_send.at[0],
                    recv_sem=halo_sem.at[1],
                    device_id=((x - 1) * NZ + z, m),
                    device_id_type=MESH,
                ).start()

            wait_for(pool_out.at[2, row], kv_sem.at[1, row])

            @pl.when(x < NX - 1)
            def _():
                pltpu.make_async_remote_copy(
                    src_ref=pool_out.at[2, row],
                    dst_ref=pool_out.at[0, row],
                    send_sem=halo_send.at[1],
                    recv_sem=halo_sem.at[0],
                    device_id=((x + 1) * NZ + z, m),
                    device_id_type=MESH,
                ).start()

            return carry

        lax.fori_loop(0, 5, forward, 0)
        wait_for(qg_out, qg_sem)
        for a in range(2):
            for b in range(2):
                wait_for(flag_out.at[a, b], flag_sem.at[a, b])

        @pl.when(x > 0)
        def _():
            wait_for(pool_out.at[1, pl.ds(row0, 5)], halo_send.at[0])
            wait_for(pool_out.at[0, pl.ds(row0, 5)], halo_sem.at[0])

        @pl.when(x < NX - 1)
        def _():
            wait_for(pool_out.at[2, pl.ds(row0, 5)], halo_send.at[1])
            wait_for(pool_out.at[3, pl.ds(row0, 5)], halo_sem.at[1])

    for i, ref in enumerate((k_ref, v_ref, q_ref, g_ref)):
        wait_for(ref, send_sem.at[i])

    @pl.when(two)
    def _():
        wait_for(k_ref, extra_sem.at[0])
        wait_for(v_ref, extra_sem.at[1])

    for j in range(3):
        wait_for(flag_ref.at[0], flag_send.at[j])
    for layer in range(4):
        pltpu.make_async_copy(blank, pool_out.at[layer, pl.ds(unused, 1)], blank_sem.at[layer]).wait()

    @pl.when(x == 0)
    def _():
        blank_layer(0, False)

    @pl.when(x == NX - 1)
    def _():
        blank_layer(3, False)


def spread(q, k, v, g, flags):
    any_space = pl.BlockSpec(memory_space=pl.ANY)
    return pl.pallas_call(
        spread_kernel,
        out_shape=(
            jax.ShapeDtypeStruct((2, 2, 4, 4 * TILE, HEAD_DIM), BF16),
            jax.ShapeDtypeStruct((4, 6, 2, 2, 2 * TILE, HEAD_DIM), BF16),
            jax.ShapeDtypeStruct((2, 2, 8, 128), F32),
        ),
        in_specs=[any_space] * 5,
        out_specs=(any_space,) * 3,
        scratch_shapes=[
            pltpu.VMEM((1, 2, 2, 2 * TILE, HEAD_DIM), BF16),
            pltpu.SemaphoreType.DMA((4,)),
            pltpu.SemaphoreType.DMA((2,)),
            pltpu.SemaphoreType.DMA((3,)),
            pltpu.SemaphoreType.DMA((2, 6)),
            pltpu.SemaphoreType.DMA,
            pltpu.SemaphoreType.DMA((2, 2)),
            pltpu.SemaphoreType.DMA((2,)),
            pltpu.SemaphoreType.DMA((2,)),
            pltpu.SemaphoreType.DMA((9,)),
        ],
        compiler_params=pltpu.CompilerParams(collective_id=0, has_side_effects=True),
        name="spread",
    )(q, k, v, g, flags)


def dot(a, b, dims):
    return lax.dot_general(a, b, (dims, ((), ())), preferred_element_type=F32)


def attend_kernel(qg_ref, pool_ref, flag_ref, place_ref, valid_ref, out_ref, mid_ref, halo_ref, acc):
    acc[...] = jnp.zeros_like(acc)

    def strip(s, carry):
        zh = s // 4
        r = lax.rem(s, 4)
        q = qg_ref[0, zh, r]
        g = qg_ref[1, zh, r]
        flags = flag_ref[zh, r // 2].astype(BF16)
        odd = lax.rem(r, 2) == 1
        scores, keys, values = [], [], []
        for pair in range(2):
            rows = slice(pair * TILE, pair * TILE + 3 * TILE)
            key = [pool_ref[zh + a, pl.ds(r, 3), 0, pair].reshape(384, HEAD_DIM) for a in range(3)]
            value = [pool_ref[zh + a, pl.ds(r, 3), 1, pair].reshape(384, HEAD_DIM) for a in range(3)]
            keys.append(jnp.concatenate(key, axis=0))
            values.append(jnp.concatenate(value, axis=0))
            live = dot(flags, place_ref[pair], ((1,), (0,)))
            live = jnp.where(odd, live[4:8], live[0:4])
            ok = jnp.concatenate(
                [valid_ref[zh + a, r + b, pair : pair + 1] for a in range(3) for b in range(3)], axis=1
            )
            bias = (live * ok - 1.0) * (-NEG)
            bias = jnp.concatenate(
                [jnp.broadcast_to(bias[pair + j : pair + j + 1], (TILE, 1152)) for j in range(3)], axis=0
            )
            scores.append(dot(q[rows], keys[pair], ((1,), (1,))) + bias)
        tops = [jnp.max(sc, axis=1, keepdims=True) for sc in scores]
        middle = jnp.maximum(tops[0][TILE:], tops[1][: 2 * TILE])
        top0 = jnp.concatenate([tops[0][:TILE], middle], axis=0)
        top1 = jnp.concatenate([middle, tops[1][2 * TILE :]], axis=0)
        expo = [jnp.exp2((sc - t) * EXP2_SCALE) for sc, t in zip(scores, (top0, top1))]
        sums = [jnp.sum(e, axis=1, keepdims=True) for e in expo]
        middle = sums[0][TILE:] + sums[1][: 2 * TILE]
        inv0 = 1.0 / jnp.concatenate([sums[0][:TILE], middle], axis=0)
        inv1 = 1.0 / jnp.concatenate([middle, sums[1][2 * TILE :]], axis=0)
        probs = [expo[0] * inv0, expo[1] * inv1]
        low = [p.astype(BF16) for p in probs]

        def join(a, b):
            return jnp.concatenate([a[:TILE], a[TILE:] + b[: 2 * TILE], b[2 * TILE :]], axis=0)

        attended = join(*[dot(low[i], values[i], ((1,), (0,))) for i in range(2)]).astype(BF16)
        out_ref[0, zh, r] = attended
        delta = jnp.sum(g.astype(F32) * attended.astype(F32), axis=1, keepdims=True)
        grads = []
        for pair in range(2):
            rows = slice(pair * TILE, pair * TILE + 3 * TILE)
            dprobs = dot(g[rows], values[pair], ((1,), (1,)))
            dscores = (probs[pair] * (dprobs - delta[rows])).astype(BF16)
            grads.append(dot(dscores, keys[pair], ((1,), (0,))))
            grad_k = dot(dscores, q[rows], ((0,), (0,))).reshape(3, 3, 2 * TILE, HEAD_DIM)
            grad_v = dot(low[pair], g[rows], ((0,), (0,))).reshape(3, 3, 2 * TILE, HEAD_DIM)
            for a in range(3):
                acc[zh + a, pl.ds(r, 3), 0, pair] += grad_k[a]
                acc[zh + a, pl.ds(r, 3), 1, pair] += grad_v[a]
        out_ref[1, zh, r] = (join(*grads) * SCALE).astype(BF16)
        return carry

    lax.fori_loop(0, 8, strip, 0)
    for i, factor in ((0, SCALE), (1, 1.0)):
        mid_ref[:, :, i] = acc[1:3, :, i] * factor
        halo_ref[0, :, i] = (acc[0, :, i] * factor).astype(BF16)
        halo_ref[1, :, i] = (acc[3, :, i] * factor).astype(BF16)


def attend(qg, pool, flags, places, valid):
    vmem = pl.BlockSpec(memory_space=pltpu.VMEM)
    return pl.pallas_call(
        attend_kernel,
        out_shape=(
            jax.ShapeDtypeStruct((2, 2, 4, 4 * TILE, HEAD_DIM), BF16),
            jax.ShapeDtypeStruct((2, 6, 2, 2, 2 * TILE, HEAD_DIM), F32),
            jax.ShapeDtypeStruct((2, 6, 2, 2, 2 * TILE, HEAD_DIM), BF16),
        ),
        in_specs=[vmem] * 5,
        out_specs=(vmem,) * 3,
        scratch_shapes=[pltpu.VMEM((4, 6, 2, 2, 2 * TILE, HEAD_DIM), F32)],
        compiler_params=pltpu.CompilerParams(vmem_limit_bytes=56 * 1024 * 1024),
        cost_estimate=pl.CostEstimate(flops=5_400_000_000, bytes_accessed=14_000_000, transcendentals=3_600_000),
        name="attend",
    )(qg, pool, flags, places, valid)


def collect_kernel(
    out_ref, mid_ref, halo_ref,
    token_out, extra_out,
    came, total, send_sem, kv_send, halo_send, halo_sem, token_sem, extra_sem,
):
    x, z, m = place()
    zl = lax.rem(z, 4)
    h = 2 * zl + m // 4
    part, head, active = work_of(z, m)
    row0 = jnp.where(part == 0, 1, 0)
    two = jnp.logical_or(h == 3, h == 4)
    columns = pl.ds(pl.multiple_of(head * HEAD_DIM, HEAD_DIM), HEAD_DIM)
    greet_plane(x, z, m)

    @pl.when(active)
    def _():
        def send_halo(r, carry):
            row = row0 + r

            @pl.when(x > 0)
            def _():
                pltpu.make_async_remote_copy(
                    src_ref=halo_ref.at[0, row],
                    dst_ref=came.at[1, row],
                    send_sem=halo_send.at[0],
                    recv_sem=halo_sem.at[1, row],
                    device_id=((x - 1) * NZ + z, m),
                    device_id_type=MESH,
                ).start()

            @pl.when(x < NX - 1)
            def _():
                pltpu.make_async_remote_copy(
                    src_ref=halo_ref.at[1, row],
                    dst_ref=came.at[0, row],
                    send_sem=halo_send.at[1],
                    recv_sem=halo_sem.at[0, row],
                    device_id=((x + 1) * NZ + z, m),
                    device_id_type=MESH,
                ).start()

            return carry

        lax.fori_loop(0, 5, send_halo, 0)

        def send_tokens(j, carry):
            j = lax.rem(j + head, 32)
            layer = j // 16
            r = lax.rem(j // 4, 4)
            w = lax.rem(j, 4)
            there = part * 4 + r
            oz = layer * 4 + there // 2
            om = lax.rem(there, 2) * 4 + w
            for i in range(2):
                pltpu.make_async_remote_copy(
                    src_ref=out_ref.at[i, layer, r, pl.ds(pl.multiple_of(w * TILE, TILE), TILE), :],
                    dst_ref=token_out.at[i, :, columns],
                    send_sem=send_sem,
                    recv_sem=token_sem.at[i],
                    device_id=(x * NZ + oz, om),
                    device_id_type=MESH,
                ).start()
            return carry

        lax.fori_loop(0, 32, send_tokens, 0)

        def send_grads(j, carry):
            layer = j // 5
            row = row0 + lax.rem(j, 5)
            there = part * 4 + row - 1
            here = jnp.where(layer == 0, x > 0, x < NX - 1)

            @pl.when(here)
            def _():
                wait_for(came.at[layer, row], halo_sem.at[layer, row])
                total[layer, row] = (mid_ref[layer, row] + came[layer, row].astype(F32)).astype(BF16)

            @pl.when(jnp.logical_not(here))
            def _():
                total[layer, row] = mid_ref[layer, row].astype(BF16)

            oz = layer * 4 + there // 2
            mine = there // 4 == part

            def send(w, carry):
                om = lax.rem(there, 2) * 4 + w
                half = pl.ds(pl.multiple_of(lax.rem(w, 2) * TILE, TILE), TILE)

                for i in range(2):
                    @pl.when(mine)
                    def _():
                        pltpu.make_async_remote_copy(
                            src_ref=total.at[layer, row, i, w // 2, half, :],
                            dst_ref=token_out.at[2 + i, :, columns],
                            send_sem=kv_send,
                            recv_sem=token_sem.at[2 + i],
                            device_id=(x * NZ + oz, om),
                            device_id_type=MESH,
                        ).start()

                    @pl.when(jnp.logical_not(mine))
                    def _():
                        pltpu.make_async_remote_copy(
                            src_ref=total.at[layer, row, i, w // 2, half, :],
                            dst_ref=extra_out.at[i, :, columns],
                            send_sem=kv_send,
                            recv_sem=extra_sem.at[i],
                            device_id=(x * NZ + oz, om),
                            device_id_type=MESH,
                        ).start()

                return carry

            return lax.fori_loop(0, 4, send, carry)

        lax.fori_loop(0, 10, send_grads, 0)
        wait_for(out_ref, send_sem)
        wait_for(total.at[:, pl.ds(row0, 5)], kv_send)

        @pl.when(x > 0)
        def _():
            wait_for(halo_ref.at[0, pl.ds(row0, 5)], halo_send.at[0])

        @pl.when(x < NX - 1)
        def _():
            wait_for(halo_ref.at[1, pl.ds(row0, 5)], halo_send.at[1])

    for i in range(4):
        wait_for(token_out.at[i], token_sem.at[i])

    @pl.when(two)
    def _():
        for i in range(2):
            wait_for(extra_out.at[i], extra_sem.at[i])


def collect(out, mid, halo):
    any_space = pl.BlockSpec(memory_space=pl.ANY)
    vmem = pl.BlockSpec(memory_space=pltpu.VMEM)
    shape = (2, 6, 2, 2, 2 * TILE, HEAD_DIM)
    return pl.pallas_call(
        collect_kernel,
        out_shape=(
            jax.ShapeDtypeStruct((4, TILE, D), BF16),
            jax.ShapeDtypeStruct((2, TILE, D), BF16),
        ),
        in_specs=[any_space, vmem, any_space],
        out_specs=(any_space,) * 2,
        scratch_shapes=[
            pltpu.VMEM(shape, BF16),
            pltpu.VMEM(shape, BF16),
            pltpu.SemaphoreType.DMA,
            pltpu.SemaphoreType.DMA,
            pltpu.SemaphoreType.DMA((2,)),
            pltpu.SemaphoreType.DMA((2, 6)),
            pltpu.SemaphoreType.DMA((4,)),
            pltpu.SemaphoreType.DMA((2,)),
        ],
        compiler_params=pltpu.CompilerParams(
            collective_id=1, has_side_effects=True, vmem_limit_bytes=32 * 1024 * 1024
        ),
        name="collect",
    )(out, mid, halo)


def on_device(queries, keys, values, out_grad, window_lists, valid_counts):
    x, z, m = place()
    zl = lax.rem(z, 4)
    t = 2 * x + z // 4
    h = 2 * zl + m // 4
    w = lax.rem(m, 4)
    part, _, _ = work_of(z, m)
    count = lax.dynamic_index_in_dim(valid_counts, (t * NH + h) * TW + w, keepdims=False)
    valid = jnp.arange(TILE, dtype=jnp.int32)[:, None] < count
    cot = jnp.where(valid, out_grad, jnp.zeros_like(out_grad))

    spot = jnp.arange(128, dtype=jnp.int32)[None, :]
    mine = jnp.arange(8, dtype=jnp.int32)[:, None]
    near_t = t + spot // 12 - 1
    near_h = 2 * zl + mine // 4 + spot // 4 % 3 - 1
    near = (near_t * NH + near_h) * TW + spot % 4
    inside = (spot < 36) & (near_t >= 0) & (near_t < TLAYERS) & (near_h >= 0) & (near_h < NH)
    listed = jnp.any(window_lists[:, :, None] == near[:, None, :], axis=1)
    flags = (inside & listed).astype(F32)[None]

    counts = jnp.pad(valid_counts.reshape(TLAYERS, NH, TW), ((1, 1), (1, 1), (0, 0)))
    counts = lax.dynamic_slice(counts, (2 * x, 4 * part, 0), (4, 6, TW))
    key_ok = jnp.arange(TILE, dtype=jnp.int32) < counts[..., None]
    key_ok = key_ok.astype(F32).reshape(4, 6, 2, 2 * TILE)

    key = jnp.arange(1152, dtype=jnp.int32)[None, None, :]
    pair = jnp.arange(2, dtype=jnp.int32)[:, None, None]
    wanted = key // 128 * 4 + pair * 2 + key % 128 // TILE
    places = (wanted == jnp.arange(128, dtype=jnp.int32)[None, :, None]).astype(BF16)

    qg, pool, flag_pool = spread(queries, keys, values, cot, flags)
    out, mid, halo = attend(qg, pool, flag_pool, places, key_ok)
    tokens, extra = collect(out, mid, halo)
    attended = jnp.where(valid, tokens[0], jnp.zeros_like(tokens[0]))
    two = jnp.logical_or(h == 3, h == 4)

    def joined(a, b):
        return jnp.where(two, (a.astype(F32) + b.astype(F32)).astype(BF16), a)

    return attended, tokens[1], joined(tokens[2], extra[0]), joined(tokens[3], extra[1])


def solution(mesh):
    rows = P(("seq", "mp"), None)
    return jax.shard_map(
        on_device,
        mesh=mesh,
        in_specs=(rows, rows, rows, rows, P("seq", None), P()),
        out_specs=(rows, rows, rows, rows),
        check_vma=False,
    )
```

```python
import math

import jax
import jax.numpy as jnp
from jax import lax
from jax.experimental import pallas as pl
from jax.experimental.pallas import tpu as pltpu
from jax.sharding import PartitionSpec as P

HEADS = 24
HEAD_DIM = 128
D = HEADS * HEAD_DIM
TILE = 64
WINDOW = 27
TLAYERS = 8
NH = 8
TW = 4
TILES = TLAYERS * NH * TW
NX = 4
NZ = 8
NM = 8
WAVES = 3
KEYS = 9 * 2 * TILE
BIG = 1e30
SCALE = 1.0 / math.sqrt(HEAD_DIM)
EXP2_SCALE = SCALE / math.log(2.0)
MESH = pl.DeviceIdType.MESH
BF16 = jnp.bfloat16
F32 = jnp.float32


def place():
    seat = lax.axis_index("seq")
    m = lax.axis_index("mp")
    return seat // NZ, lax.rem(seat, NZ), m


def worker_z(part, m, wave):
    u = lax.rem(wave + m // 2, 2)
    v = lax.rem(m + wave // 2, 2)
    return jnp.where(part == 0, 3 - u + 4 * v, lax.rem(4 - 3 * u + 4 * v, NZ))


def work_of(z, m):
    zq = lax.rem(z, 4)
    zh = z // 4
    part = jnp.where(zq >= 2, 0, 1)
    u = jnp.where(part == 0, 3 - zq, zq)
    v = jnp.where(jnp.logical_and(part == 1, u == 0), 1 - zh, zh)
    same_v = v == lax.rem(m, 2)
    same_u = u == lax.rem(m // 2, 2)
    wave = jnp.where(same_u, jnp.where(same_v, 0, 2), 1)
    return part, wave, jnp.logical_or(same_u, same_v)


def greet_plane(x, z, m):
    barrier = pltpu.get_barrier_semaphore()

    def greet(i, carry):
        zz = i // NM
        mm = lax.rem(i, NM)

        @pl.when(jnp.logical_or(zz != z, mm != m))
        def _():
            pl.semaphore_signal(barrier, inc=1, device_id=(x * NZ + zz, mm), device_id_type=MESH)

        return carry

    lax.fori_loop(0, NZ * NM, greet, 0)

    @pl.when(x > 0)
    def _():
        pl.semaphore_signal(barrier, inc=1, device_id=((x - 1) * NZ + z, m), device_id_type=MESH)

    @pl.when(x < NX - 1)
    def _():
        pl.semaphore_signal(barrier, inc=1, device_id=((x + 1) * NZ + z, m), device_id_type=MESH)

    peers = NZ * NM - 1 + jnp.where(x > 0, 1, 0) + jnp.where(x < NX - 1, 1, 0)
    pl.semaphore_wait(barrier, peers)


def wait_for(ref, sem):
    pltpu.make_async_copy(ref, ref, sem).wait()


def send(src, dst, send_sem, recv_sem, seat, m):
    pltpu.make_async_remote_copy(
        src_ref=src, dst_ref=dst, send_sem=send_sem, recv_sem=recv_sem,
        device_id=(seat, m), device_id_type=MESH,
    ).start()


def dot(a, b, dims):
    return lax.dot_general(a, b, (dims, ((), ())), preferred_element_type=F32)


def tile_rows(w):
    return pl.ds(pl.multiple_of(w * TILE, TILE), TILE)


def head_columns(head):
    return pl.ds(pl.multiple_of(head * HEAD_DIM, HEAD_DIM), HEAD_DIM)


def kernel(
    q_ref, k_ref, v_ref, g_ref, list_ref, count_ref,
    att_out, gq_out, gk_out, gv_out,
    pool, qg, out, acc, edge, came, passed, total, flag_mine, flag_all, places, valid, bias,
    send_sem, kv_sem, qg_sem, flag_send, flag_sem, xsend, xsem, zsend, zsem,
    out_send, token_sem, edge_send, edge_sem, part_send, part_sem, total_send,
):
    x, z, m = place()
    zh = z // 4
    zl = lax.rem(z, 4)
    h = 2 * zl + m // 4
    w = lax.rem(m, 4)
    t = 2 * x + zh
    own = zl // 2
    part, wave, active = work_of(z, m)
    head = 3 * m + wave
    has_low = x > 0
    has_high = x < NX - 1
    low_seat = (x - 1) * NZ + z
    high_seat = (x + 1) * NZ + z
    other_seat = x * NZ + worker_z(1 - part, m, wave)

    spot = lax.broadcasted_iota(jnp.int32, (8, 128), 1)
    mine = lax.broadcasted_iota(jnp.int32, (8, 128), 0)
    near_t = t + spot // 12 - 1
    near_h = 2 * zl + mine // 4 + lax.rem(spot // 4, 3) - 1
    near = (near_t * NH + near_h) * TW + lax.rem(spot, 4)
    inside = (spot < 36) & (near_t >= 0) & (near_t < TLAYERS) & (near_h >= 0) & (near_h < NH)
    near = jnp.where(inside, near, -2)
    listed = jnp.zeros((8, 128), F32)
    for j in range(WINDOW):
        listed = jnp.where(list_ref[:, j : j + 1] == near, 1.0, listed)
    flag_mine[...] = listed
    pool[...] = jnp.zeros_like(pool)
    greet_plane(x, z, m)

    my_rows = tile_rows(lax.rem(w, 2))

    def send_wave(number, carry):
        def send_kv(j, carry):
            wm = lax.rem(j + m + z, NM)
            seat = x * NZ + worker_z(own, wm, number)
            columns = head_columns(3 * wm + number)
            row = lax.rem(h, 4)
            for i, ref in ((0, k_ref), (1, v_ref)):
                send(
                    ref.at[:, columns], pool.at[1 + zh, 1 + row, i, w // 2, my_rows, :],
                    send_sem.at[i], kv_sem.at[zh, row], seat, wm,
                )
            return carry

        def send_qg(j, carry):
            wm = lax.rem(j + m + z, NM)
            seat = x * NZ + worker_z(own, wm, number)
            columns = head_columns(3 * wm + number)
            row = lax.rem(h, 4)
            for i, ref in ((0, q_ref), (1, g_ref)):
                send(
                    ref.at[:, columns], qg.at[zh, row, i, tile_rows(w), :],
                    send_sem.at[2 + i], qg_sem.at[zh, row], seat, wm,
                )
            return carry

        lax.fori_loop(0, NM, send_kv, 0)
        send(
            flag_mine, flag_all.at[zh, lax.rem(zl, 2)],
            flag_send.at[number], flag_sem.at[zh, lax.rem(zl, 2)],
            x * NZ + worker_z(own, m, number), m,
        )
        lax.fori_loop(0, NM, send_qg, 0)
        return carry

    lax.fori_loop(0, WAVES, send_wave, 0)

    def row_of(i):
        return jnp.where(part == 0, 5 - i, i)

    def work():
        acc[...] = jnp.zeros_like(acc)
        lane = lax.broadcasted_iota(jnp.int32, (1, 128), 1)

        def mark(i, carry):
            layer = i // 6
            row = lax.rem(i, 6)
            key_t = 2 * x - 1 + layer
            key_h = 4 * part - 1 + row
            real = (key_t >= 0) & (key_t < TLAYERS) & (key_h >= 0) & (key_h < NH)
            first = jnp.where(real, (key_t * NH + key_h) * TW, 0)
            for pair in range(2):
                counts = [jnp.where(real, count_ref[first + 2 * pair + j], 0) for j in range(2)]
                until = jnp.where(lane < TILE, counts[0], counts[1] + TILE)
                valid[layer, row, pair : pair + 1, :] = jnp.where(lane < until, 1.0, 0.0)
            return carry

        lax.fori_loop(0, 24, mark, 0)

        key = lax.broadcasted_iota(jnp.int32, (128, KEYS), 1)
        flag = lax.broadcasted_iota(jnp.int32, (128, KEYS), 0)
        for pair in range(2):
            wanted = key // 128 * 4 + pair * 2 + lax.rem(key, 128) // TILE
            places[pair] = jnp.where(wanted == flag, 1.0, 0.0).astype(BF16)

        def forward(i, carry):
            row = row_of(i)
            for side in range(2):
                @pl.when(i > 0)
                def _():
                    wait_for(pool.at[1 + side, row], kv_sem.at[side, jnp.maximum(row, 1) - 1])

                @pl.when(i == 0)
                def _():
                    wait_for(pool.at[1 + side, row], zsem.at[side])

                @pl.when(i == 1)
                def _():
                    send(
                        pool.at[1 + side, row], pool.at[1 + side, jnp.where(part == 0, 0, 5)],
                        zsend.at[side], zsem.at[side], other_seat, m,
                    )

            @pl.when(has_low)
            def _():
                send(pool.at[1, row], pool.at[3, row], xsend.at[0], xsem.at[1, row], low_seat, m)

            @pl.when(has_high)
            def _():
                send(pool.at[2, row], pool.at[0, row], xsend.at[1], xsem.at[0, row], high_seat, m)

            return carry

        lax.fori_loop(1, 5, forward, 0)
        forward(0, 0)

        def make_bias(layer, carry):
            for a in range(2):
                wait_for(flag_all.at[layer, a], flag_sem.at[layer, a])
            for pair in range(2):
                for r in range(4):
                    if r % 2 == 0:
                        live = dot(flag_all[layer, r // 2].astype(BF16), places[pair], ((1,), (0,)))
                    ok = jnp.concatenate(
                        [valid[layer + a, r + b, pair : pair + 1, :] for a in range(3) for b in range(3)], axis=1
                    )
                    tiles = live[(r % 2) * 4 : (r % 2) * 4 + 4]
                    bias[layer, r, pair, 0:4, :] = (tiles * ok - 1.0) * BIG
            return carry

        lax.fori_loop(0, 2, make_bias, 0)

        def arrive(i, carry):
            row = row_of(i)

            @pl.when(has_low)
            def _():
                wait_for(pool.at[0, row], xsem.at[0, row])

            @pl.when(has_high)
            def _():
                wait_for(pool.at[3, row], xsem.at[1, row])

            return carry

        lax.fori_loop(0, 5, arrive, 0)

        position = lax.broadcasted_iota(jnp.int32, (TILE, HEAD_DIM), 0)

        def strip(layer, r):
            wait_for(qg.at[layer, r], qg_sem.at[layer, r])
            tile0 = ((2 * x + layer) * NH + 4 * part + r) * TW
            token_ok = jnp.concatenate([position < count_ref[tile0 + j] for j in range(TW)], axis=0)
            q = qg[layer, r, 0]
            g = qg[layer, r, 1]
            g = jnp.where(token_ok, g.astype(F32), 0.0).astype(BF16)
            scores, keys, values = [], [], []
            for pair in range(2):
                rows = slice(pair * TILE, pair * TILE + 3 * TILE)
                key = [pool[layer + a, pl.ds(r, 3), 0, pair].reshape(384, HEAD_DIM) for a in range(3)]
                value = [pool[layer + a, pl.ds(r, 3), 1, pair].reshape(384, HEAD_DIM) for a in range(3)]
                keys.append(jnp.concatenate(key, axis=0))
                values.append(jnp.concatenate(value, axis=0))
                out_of = jnp.concatenate(
                    [
                        jnp.broadcast_to(bias[layer, r, pair, pair + j : pair + j + 1, :], (TILE, KEYS))
                        for j in range(3)
                    ],
                    axis=0,
                )
                scores.append(dot(q[rows], keys[pair], ((1,), (1,))) + out_of)
            tops = [jnp.max(sc, axis=1, keepdims=True) for sc in scores]
            middle = jnp.maximum(tops[0][TILE:], tops[1][: 2 * TILE])
            top0 = jnp.concatenate([tops[0][:TILE], middle], axis=0)
            top1 = jnp.concatenate([middle, tops[1][2 * TILE :]], axis=0)
            expo = [jnp.exp2((sc - top) * EXP2_SCALE) for sc, top in zip(scores, (top0, top1))]
            sums = [jnp.sum(e, axis=1, keepdims=True) for e in expo]
            middle = sums[0][TILE:] + sums[1][: 2 * TILE]
            inv0 = 1.0 / jnp.concatenate([sums[0][:TILE], middle], axis=0)
            inv1 = 1.0 / jnp.concatenate([middle, sums[1][2 * TILE :]], axis=0)
            probs = [expo[0] * inv0, expo[1] * inv1]
            low = [p.astype(BF16) for p in probs]

            def join(a, b):
                return jnp.concatenate([a[:TILE], a[TILE:] + b[: 2 * TILE], b[2 * TILE :]], axis=0)

            attended = join(*[dot(low[i], values[i], ((1,), (0,))) for i in range(2)])
            attended = jnp.where(token_ok, attended, 0.0).astype(BF16)
            out[layer, r, 0] = attended
            delta = jnp.sum(g.astype(F32) * attended.astype(F32), axis=1, keepdims=True)
            grads = []
            for pair in range(2):
                rows = slice(pair * TILE, pair * TILE + 3 * TILE)
                dprobs = dot(g[rows], values[pair], ((1,), (1,)))
                dscores = (probs[pair] * (dprobs - delta[rows])).astype(BF16)
                grads.append(dot(dscores, keys[pair], ((1,), (0,))))
                grad_k = dot(dscores, q[rows], ((0,), (0,))).reshape(3, 3, 2 * TILE, HEAD_DIM)
                grad_v = dot(low[pair], g[rows], ((0,), (0,))).reshape(3, 3, 2 * TILE, HEAD_DIM)
                for a in range(3):
                    acc[layer + a, pl.ds(r, 3), 0, pair] += grad_k[a]
                    acc[layer + a, pl.ds(r, 3), 1, pair] += grad_v[a]
            out[layer, r, 1] = (join(*grads) * SCALE).astype(BF16)

        columns = head_columns(head)

        def seat_of(layer, row):
            return x * NZ + layer * 4 + (4 * part + row) // 2, lax.rem(row, 2) * 4

        def send_strip(layer, r):
            seat, m0 = seat_of(layer, r)

            def send_tile(j, carry):
                for i, ref in ((0, att_out), (1, gq_out)):
                    send(
                        out.at[layer, r, i, tile_rows(j), :], ref.at[:, columns],
                        out_send, token_sem.at[i], seat, m0 + j,
                    )
                return carry

            lax.fori_loop(0, TW, send_tile, 0)

        def scaled(layer, row, i):
            return acc[layer, row, i] * (SCALE if i == 0 else 1.0)

        def send_edge(i):
            row = row_of(i)

            @pl.when(has_low)
            def _():
                for j in range(2):
                    edge[0, i, j] = scaled(0, row, j).astype(BF16)
                send(edge.at[0, i], came.at[1, i], edge_send.at[0], edge_sem.at[1, i], low_seat, m)

            @pl.when(has_high)
            def _():
                for j in range(2):
                    edge[1, i, j] = scaled(3, row, j).astype(BF16)
                send(edge.at[1, i], came.at[0, i], edge_send.at[1], edge_sem.at[0, i], high_seat, m)

        def add_edge(side, i, row):
            @pl.when(has_high if side else has_low)
            def _():
                wait_for(came.at[side, i], edge_sem.at[side, i])
                for j in range(2):
                    total[side, i, j] = (scaled(1 + side, row, j) + came[side, i, j].astype(F32)).astype(BF16)

            @pl.when(jnp.logical_not(has_high if side else has_low))
            def _():
                for j in range(2):
                    total[side, i, j] = scaled(1 + side, row, j).astype(BF16)

        def finish(i):
            row = row_of(i)
            for side in (1, 0):
                add_edge(side, i, row)

                @pl.when(i == 0)
                def _():
                    send(
                        total.at[side, i], passed.at[side],
                        part_send.at[side], part_sem.at[side], other_seat, m,
                    )

                @pl.when(i == 1)
                def _():
                    wait_for(passed.at[side], part_sem.at[side])
                    total[side, i] = (total[side, i].astype(F32) + passed[side].astype(F32)).astype(BF16)

                @pl.when(i > 0)
                def _():
                    seat, m0 = seat_of(side, row - 1)

                    def send_tile(j, carry):
                        for n, ref in ((0, gk_out), (1, gv_out)):
                            send(
                                total.at[side, i, n, j // 2, tile_rows(lax.rem(j, 2)), :], ref.at[:, columns],
                                total_send, token_sem.at[2 + n], seat, m0 + j,
                            )
                        return carry

                    lax.fori_loop(0, TW, send_tile, 0)

        def step(i, carry):
            r = jnp.where(part == 0, 3 - i, i)

            def one(layer, carry):
                strip(layer, r)
                send_strip(layer, r)
                return carry

            lax.fori_loop(0, 2, one, 0)
            send_edge(i)

            @pl.when(i > 0)
            def _():
                finish(i - 1)

            return carry

        lax.fori_loop(0, 4, step, 0)
        send_edge(4)

        def last(i, carry):
            finish(i)
            return carry

        lax.fori_loop(3, 5, last, 0)

        wait_for(out, out_send)
        wait_for(total.at[:, pl.ds(1, 4)], total_send)
        for side in range(2):
            wait_for(pool.at[0, 0], zsend.at[side])
            wait_for(total.at[side, 0], part_send.at[side])

            @pl.when(has_high if side else has_low)
            def _():
                wait_for(pool.at[0, pl.ds(0, 5)], xsend.at[side])
                wait_for(edge.at[side], edge_send.at[side])

    pl.when(active)(work)

    for i, ref in enumerate((k_ref, v_ref, q_ref, g_ref)):
        wait_for(ref, send_sem.at[i])
    for i in range(WAVES):
        wait_for(flag_mine, flag_send.at[i])
    for i, ref in enumerate((att_out, gq_out, gk_out, gv_out)):
        wait_for(ref, token_sem.at[i])


def on_device(queries, keys, values, out_grad, window_lists, valid_counts):
    any_space = pl.BlockSpec(memory_space=pl.ANY)
    dma = pltpu.SemaphoreType.DMA
    row = (2, 2, 2 * TILE, HEAD_DIM)
    return pl.pallas_call(
        kernel,
        out_shape=(jax.ShapeDtypeStruct((TILE, D), BF16),) * 4,
        in_specs=[any_space] * 4
        + [pl.BlockSpec(memory_space=pltpu.VMEM), pl.BlockSpec(memory_space=pltpu.SMEM)],
        out_specs=(any_space,) * 4,
        scratch_shapes=[
            pltpu.VMEM((4, 6) + row, BF16),
            pltpu.VMEM((2, 4, 2, TW * TILE, HEAD_DIM), BF16),
            pltpu.VMEM((2, 4, 2, TW * TILE, HEAD_DIM), BF16),
            pltpu.VMEM((4, 6) + row, F32),
            pltpu.VMEM((2, 5) + row, BF16),
            pltpu.VMEM((2, 5) + row, BF16),
            pltpu.VMEM((2,) + row, BF16),
            pltpu.VMEM((2, 5) + row, BF16),
            pltpu.VMEM((8, 128), F32),
            pltpu.VMEM((2, 2, 8, 128), F32),
            pltpu.VMEM((2, 128, KEYS), BF16),
            pltpu.VMEM((4, 6, 2, 128), F32),
            pltpu.VMEM((2, 4, 2, 4, KEYS), F32),
            dma((4,)), dma((2, 4)), dma((2, 4)), dma((WAVES,)), dma((2, 2)),
            dma((2,)), dma((2, 6)), dma((2,)), dma((2,)),
            dma, dma((4,)), dma((2,)), dma((2, 5)), dma((2,)), dma((2,)), dma,
        ],
        compiler_params=pltpu.CompilerParams(
            collective_id=0, has_side_effects=True, vmem_limit_bytes=56 * 1024 * 1024
        ),
        cost_estimate=pl.CostEstimate(flops=5_400_000_000, bytes_accessed=6_000_000, transcendentals=3_600_000),
        name="window_attention",
    )(queries, keys, values, out_grad, window_lists, valid_counts)


def solution(mesh):
    rows = P(("seq", "mp"), None)
    return jax.shard_map(
        on_device,
        mesh=mesh,
        in_specs=(rows, rows, rows, rows, P("seq", None), P()),
        out_specs=(rows, rows, rows, rows),
        check_vma=False,
    )
```

```python
import math

import jax
import jax.numpy as jnp
from jax import lax
from jax.experimental import pallas as pl
from jax.experimental.pallas import tpu as pltpu
from jax.sharding import PartitionSpec as P

HEADS = 24
HEAD_DIM = 128
D = HEADS * HEAD_DIM
TILE = 64
WINDOW = 27
TLAYERS = 8
NH = 8
TW = 4
TILES = TLAYERS * NH * TW
NX = 4
NZ = 8
NM = 8
WAVES = 3
KEYS = 9 * 2 * TILE
BIG = 1e30
SCALE = 1.0 / math.sqrt(HEAD_DIM)
EXP2_SCALE = SCALE / math.log(2.0)
MESH = pl.DeviceIdType.MESH
BF16 = jnp.bfloat16
F32 = jnp.float32


def place():
    seat = lax.axis_index("seq")
    m = lax.axis_index("mp")
    return seat // NZ, lax.rem(seat, NZ), m


def worker_z(part, m, wave):
    u = lax.rem(wave + m // 2, 2)
    v = lax.rem(m + wave // 2, 2)
    return jnp.where(part == 0, 3 - u + 4 * v, lax.rem(4 - 3 * u + 4 * v, NZ))


def work_of(z, m):
    zq = lax.rem(z, 4)
    zh = z // 4
    part = jnp.where(zq >= 2, 0, 1)
    u = jnp.where(part == 0, 3 - zq, zq)
    v = jnp.where(jnp.logical_and(part == 1, u == 0), 1 - zh, zh)
    same_v = v == lax.rem(m, 2)
    same_u = u == lax.rem(m // 2, 2)
    wave = jnp.where(same_u, jnp.where(same_v, 0, 2), 1)
    return part, wave, jnp.logical_or(same_u, same_v)


def greet_plane(x, z, m):
    barrier = pltpu.get_barrier_semaphore()

    def greet(i, carry):
        zz = i // NM
        mm = lax.rem(i, NM)

        @pl.when(jnp.logical_or(zz != z, mm != m))
        def _():
            pl.semaphore_signal(barrier, inc=1, device_id=(x * NZ + zz, mm), device_id_type=MESH)

        return carry

    lax.fori_loop(0, NZ * NM, greet, 0)

    @pl.when(x > 0)
    def _():
        pl.semaphore_signal(barrier, inc=1, device_id=((x - 1) * NZ + z, m), device_id_type=MESH)

    @pl.when(x < NX - 1)
    def _():
        pl.semaphore_signal(barrier, inc=1, device_id=((x + 1) * NZ + z, m), device_id_type=MESH)

    peers = NZ * NM - 1 + jnp.where(x > 0, 1, 0) + jnp.where(x < NX - 1, 1, 0)
    pl.semaphore_wait(barrier, peers)


def wait_for(ref, sem):
    pltpu.make_async_copy(ref, ref, sem).wait()


def send(src, dst, send_sem, recv_sem, seat, m):
    pltpu.make_async_remote_copy(
        src_ref=src, dst_ref=dst, send_sem=send_sem, recv_sem=recv_sem,
        device_id=(seat, m), device_id_type=MESH,
    ).start()


def dot(a, b, dims):
    return lax.dot_general(a, b, (dims, ((), ())), preferred_element_type=F32)


def tile_rows(w):
    return pl.ds(pl.multiple_of(w * TILE, TILE), TILE)


def head_columns(head):
    return pl.ds(pl.multiple_of(head * HEAD_DIM, HEAD_DIM), HEAD_DIM)


def kernel(
    q_ref, k_ref, v_ref, g_ref, list_ref, count_ref,
    att_out, gq_out, gk_out, gv_out,
    pool, qg, out, acc, edge, came, passed, total, flag_mine, flag_all, places, valid, bias,
    send_sem, kv_sem, qg_sem, flag_send, flag_sem, xsend, xsem, zsend, zsem,
    out_send, token_sem, edge_send, edge_sem, part_send, part_sem, total_send,
):
    x, z, m = place()
    zh = z // 4
    zl = lax.rem(z, 4)
    h = 2 * zl + m // 4
    w = lax.rem(m, 4)
    t = 2 * x + zh
    own = zl // 2
    part, wave, active = work_of(z, m)
    head = 3 * m + wave
    has_low = x > 0
    has_high = x < NX - 1
    low_seat = (x - 1) * NZ + z
    high_seat = (x + 1) * NZ + z
    other_seat = x * NZ + worker_z(1 - part, m, wave)

    spot = lax.broadcasted_iota(jnp.int32, (8, 128), 1)
    mine = lax.broadcasted_iota(jnp.int32, (8, 128), 0)
    near_t = t + spot // 12 - 1
    near_h = 2 * zl + mine // 4 + lax.rem(spot // 4, 3) - 1
    near = (near_t * NH + near_h) * TW + lax.rem(spot, 4)
    inside = (spot < 36) & (near_t >= 0) & (near_t < TLAYERS) & (near_h >= 0) & (near_h < NH)
    near = jnp.where(inside, near, -2)
    listed = jnp.zeros((8, 128), F32)
    for j in range(WINDOW):
        listed = jnp.where(list_ref[:, j : j + 1] == near, 1.0, listed)
    flag_mine[...] = listed
    pool[...] = jnp.zeros_like(pool)
    greet_plane(x, z, m)

    my_rows = tile_rows(lax.rem(w, 2))

    def send_kv(number):
        def one(j, carry):
            wm = lax.rem(j + m + z, NM)
            seat = x * NZ + worker_z(own, wm, number)
            columns = head_columns(3 * wm + number)
            row = lax.rem(h, 4)
            for i, ref in ((0, k_ref), (1, v_ref)):
                send(
                    ref.at[:, columns], pool.at[1 + zh, 1 + row, i, w // 2, my_rows, :],
                    send_sem.at[i], kv_sem.at[zh, row], seat, wm,
                )
            return carry

        lax.fori_loop(0, NM, one, 0)

    def send_qg(number):
        send(
            flag_mine, flag_all.at[zh, lax.rem(zl, 2)],
            flag_send.at[number], flag_sem.at[zh, lax.rem(zl, 2)],
            x * NZ + worker_z(own, m, number), m,
        )

        def one(j, carry):
            wm = lax.rem(j + m + z, NM)
            seat = x * NZ + worker_z(own, wm, number)
            columns = head_columns(3 * wm + number)
            row = lax.rem(h, 4)
            for i, ref in ((0, q_ref), (1, g_ref)):
                send(
                    ref.at[:, columns], qg.at[zh, row, i, tile_rows(w), :],
                    send_sem.at[2 + i], qg_sem.at[zh, row], seat, wm,
                )
            return carry

        lax.fori_loop(0, NM, one, 0)

    def row_of(i):
        return jnp.where(part == 0, 5 - i, i)

    def forward(i, carry):
        row = row_of(i)
        for side in range(2):
            @pl.when(i > 0)
            def _():
                wait_for(pool.at[1 + side, row], kv_sem.at[side, jnp.maximum(row, 1) - 1])

            @pl.when(i == 0)
            def _():
                wait_for(pool.at[1 + side, row], zsem.at[side])

            @pl.when(i == 1)
            def _():
                send(
                    pool.at[1 + side, row], pool.at[1 + side, jnp.where(part == 0, 0, 5)],
                    zsend.at[side], zsem.at[side], other_seat, m,
                )

        @pl.when(has_low)
        def _():
            send(pool.at[1, row], pool.at[3, row], xsend.at[0], xsem.at[1, row], low_seat, m)

        @pl.when(has_high)
        def _():
            send(pool.at[2, row], pool.at[0, row], xsend.at[1], xsem.at[0, row], high_seat, m)

        return carry

    def send_wave(number, carry):
        send_kv(number)
        send_qg(number)

        @pl.when(jnp.logical_and(active, wave == number))
        def _():
            lax.fori_loop(1, 5, forward, 0)
            forward(0, 0)

        return carry

    lax.fori_loop(0, WAVES, send_wave, 0)

    def work():
        acc[...] = jnp.zeros_like(acc)
        lane = lax.broadcasted_iota(jnp.int32, (1, 128), 1)

        def mark(i, carry):
            layer = i // 6
            row = lax.rem(i, 6)
            key_t = 2 * x - 1 + layer
            key_h = 4 * part - 1 + row
            real = (key_t >= 0) & (key_t < TLAYERS) & (key_h >= 0) & (key_h < NH)
            first = jnp.where(real, (key_t * NH + key_h) * TW, 0)
            for pair in range(2):
                counts = [jnp.where(real, count_ref[first + 2 * pair + j], 0) for j in range(2)]
                until = jnp.where(lane < TILE, counts[0], counts[1] + TILE)
                valid[layer, row, pair : pair + 1, :] = jnp.where(lane < until, 1.0, 0.0)
            return carry

        lax.fori_loop(0, 24, mark, 0)

        key = lax.broadcasted_iota(jnp.int32, (128, KEYS), 1)
        flag = lax.broadcasted_iota(jnp.int32, (128, KEYS), 0)
        for pair in range(2):
            wanted = key // 128 * 4 + pair * 2 + lax.rem(key, 128) // TILE
            places[pair] = jnp.where(wanted == flag, 1.0, 0.0).astype(BF16)

        def make_bias(layer, carry):
            for a in range(2):
                wait_for(flag_all.at[layer, a], flag_sem.at[layer, a])
            for pair in range(2):
                for r in range(4):
                    if r % 2 == 0:
                        live = dot(flag_all[layer, r // 2].astype(BF16), places[pair], ((1,), (0,)))
                    ok = jnp.concatenate(
                        [valid[layer + a, r + b, pair : pair + 1, :] for a in range(3) for b in range(3)], axis=1
                    )
                    tiles = live[(r % 2) * 4 : (r % 2) * 4 + 4]
                    bias[layer, r, pair, 0:4, :] = (tiles * ok - 1.0) * BIG
            return carry

        lax.fori_loop(0, 2, make_bias, 0)

        def arrive(i, carry):
            row = row_of(i)

            @pl.when(has_low)
            def _():
                wait_for(pool.at[0, row], xsem.at[0, row])

            @pl.when(has_high)
            def _():
                wait_for(pool.at[3, row], xsem.at[1, row])

            return carry

        lax.fori_loop(0, 5, arrive, 0)

        position = lax.broadcasted_iota(jnp.int32, (TILE, HEAD_DIM), 0)

        def strip(layer, r):
            wait_for(qg.at[layer, r], qg_sem.at[layer, r])
            tile0 = ((2 * x + layer) * NH + 4 * part + r) * TW
            token_ok = jnp.concatenate([position < count_ref[tile0 + j] for j in range(TW)], axis=0)
            q = qg[layer, r, 0]
            g = qg[layer, r, 1]
            g = jnp.where(token_ok, g.astype(F32), 0.0).astype(BF16)
            scores, keys, values = [], [], []
            for pair in range(2):
                rows = slice(pair * TILE, pair * TILE + 3 * TILE)
                key = [pool[layer + a, pl.ds(r, 3), 0, pair].reshape(384, HEAD_DIM) for a in range(3)]
                value = [pool[layer + a, pl.ds(r, 3), 1, pair].reshape(384, HEAD_DIM) for a in range(3)]
                keys.append(jnp.concatenate(key, axis=0))
                values.append(jnp.concatenate(value, axis=0))
                out_of = jnp.concatenate(
                    [
                        jnp.broadcast_to(bias[layer, r, pair, pair + j : pair + j + 1, :], (TILE, KEYS))
                        for j in range(3)
                    ],
                    axis=0,
                )
                scores.append(dot(q[rows], keys[pair], ((1,), (1,))) + out_of)
            tops = [jnp.max(sc, axis=1, keepdims=True) for sc in scores]
            middle = jnp.maximum(tops[0][TILE:], tops[1][: 2 * TILE])
            top0 = jnp.concatenate([tops[0][:TILE], middle], axis=0)
            top1 = jnp.concatenate([middle, tops[1][2 * TILE :]], axis=0)
            expo = [jnp.exp2((sc - top) * EXP2_SCALE) for sc, top in zip(scores, (top0, top1))]
            sums = [jnp.sum(e, axis=1, keepdims=True) for e in expo]
            middle = sums[0][TILE:] + sums[1][: 2 * TILE]
            inv0 = 1.0 / jnp.concatenate([sums[0][:TILE], middle], axis=0)
            inv1 = 1.0 / jnp.concatenate([middle, sums[1][2 * TILE :]], axis=0)
            probs = [expo[0] * inv0, expo[1] * inv1]
            low = [p.astype(BF16) for p in probs]

            def join(a, b):
                return jnp.concatenate([a[:TILE], a[TILE:] + b[: 2 * TILE], b[2 * TILE :]], axis=0)

            attended = join(*[dot(low[i], values[i], ((1,), (0,))) for i in range(2)])
            attended = jnp.where(token_ok, attended, 0.0).astype(BF16)
            out[layer, r, 0] = attended
            delta = jnp.sum(g.astype(F32) * attended.astype(F32), axis=1, keepdims=True)
            grads = []
            for pair in range(2):
                rows = slice(pair * TILE, pair * TILE + 3 * TILE)
                dprobs = dot(g[rows], values[pair], ((1,), (1,)))
                dscores = (probs[pair] * (dprobs - delta[rows])).astype(BF16)
                grads.append(dot(dscores, keys[pair], ((1,), (0,))))
                grad_k = dot(dscores, q[rows], ((0,), (0,))).reshape(3, 3, 2 * TILE, HEAD_DIM)
                grad_v = dot(low[pair], g[rows], ((0,), (0,))).reshape(3, 3, 2 * TILE, HEAD_DIM)
                for a in range(3):
                    acc[layer + a, pl.ds(r, 3), 0, pair] += grad_k[a]
                    acc[layer + a, pl.ds(r, 3), 1, pair] += grad_v[a]
            out[layer, r, 1] = (join(*grads) * SCALE).astype(BF16)

        columns = head_columns(head)

        def seat_of(layer, row):
            return x * NZ + layer * 4 + (4 * part + row) // 2, lax.rem(row, 2) * 4

        def send_strip(layer, r):
            seat, m0 = seat_of(layer, r)

            def send_tile(j, carry):
                for i, ref in ((0, att_out), (1, gq_out)):
                    send(
                        out.at[layer, r, i, tile_rows(j), :], ref.at[:, columns],
                        out_send, token_sem.at[i], seat, m0 + j,
                    )
                return carry

            lax.fori_loop(0, TW, send_tile, 0)

        def scaled(layer, row, i):
            return acc[layer, row, i] * (SCALE if i == 0 else 1.0)

        def send_edge(i):
            row = row_of(i)

            @pl.when(has_low)
            def _():
                for j in range(2):
                    edge[0, i, j] = scaled(0, row, j).astype(BF16)
                send(edge.at[0, i], came.at[1, i], edge_send.at[0], edge_sem.at[1, i], low_seat, m)

            @pl.when(has_high)
            def _():
                for j in range(2):
                    edge[1, i, j] = scaled(3, row, j).astype(BF16)
                send(edge.at[1, i], came.at[0, i], edge_send.at[1], edge_sem.at[0, i], high_seat, m)

        def add_edge(side, i, row):
            @pl.when(has_high if side else has_low)
            def _():
                wait_for(came.at[side, i], edge_sem.at[side, i])
                for j in range(2):
                    total[side, i, j] = (scaled(1 + side, row, j) + came[side, i, j].astype(F32)).astype(BF16)

            @pl.when(jnp.logical_not(has_high if side else has_low))
            def _():
                for j in range(2):
                    total[side, i, j] = scaled(1 + side, row, j).astype(BF16)

        def finish(i):
            row = row_of(i)
            for side in (1, 0):
                add_edge(side, i, row)

                @pl.when(i == 0)
                def _():
                    send(
                        total.at[side, i], passed.at[side],
                        part_send.at[side], part_sem.at[side], other_seat, m,
                    )

                @pl.when(i == 1)
                def _():
                    wait_for(passed.at[side], part_sem.at[side])
                    total[side, i] = (total[side, i].astype(F32) + passed[side].astype(F32)).astype(BF16)

                @pl.when(i > 0)
                def _():
                    seat, m0 = seat_of(side, row - 1)

                    def send_tile(j, carry):
                        for n, ref in ((0, gk_out), (1, gv_out)):
                            send(
                                total.at[side, i, n, j // 2, tile_rows(lax.rem(j, 2)), :], ref.at[:, columns],
                                total_send, token_sem.at[2 + n], seat, m0 + j,
                            )
                        return carry

                    lax.fori_loop(0, TW, send_tile, 0)

        def step(i, carry):
            r = jnp.where(part == 0, 3 - i, i)

            def one(layer, carry):
                strip(layer, r)
                send_strip(layer, r)
                return carry

            lax.fori_loop(0, 2, one, 0)
            send_edge(i)

            @pl.when(i > 0)
            def _():
                finish(i - 1)

            return carry

        lax.fori_loop(0, 4, step, 0)
        send_edge(4)

        def last(i, carry):
            finish(i)
            return carry

        lax.fori_loop(3, 5, last, 0)

        wait_for(out, out_send)
        wait_for(total.at[:, pl.ds(1, 4)], total_send)
        for side in range(2):
            wait_for(pool.at[0, 0], zsend.at[side])
            wait_for(total.at[side, 0], part_send.at[side])

            @pl.when(has_high if side else has_low)
            def _():
                wait_for(pool.at[0, pl.ds(0, 5)], xsend.at[side])
                wait_for(edge.at[side], edge_send.at[side])

    pl.when(active)(work)

    for i, ref in enumerate((k_ref, v_ref, q_ref, g_ref)):
        wait_for(ref, send_sem.at[i])
    for i in range(WAVES):
        wait_for(flag_mine, flag_send.at[i])
    for i, ref in enumerate((att_out, gq_out, gk_out, gv_out)):
        wait_for(ref, token_sem.at[i])


def on_device(queries, keys, values, out_grad, window_lists, valid_counts):
    any_space = pl.BlockSpec(memory_space=pl.ANY)
    dma = pltpu.SemaphoreType.DMA
    row = (2, 2, 2 * TILE, HEAD_DIM)
    return pl.pallas_call(
        kernel,
        out_shape=(jax.ShapeDtypeStruct((TILE, D), BF16),) * 4,
        in_specs=[any_space] * 4
        + [pl.BlockSpec(memory_space=pltpu.VMEM), pl.BlockSpec(memory_space=pltpu.SMEM)],
        out_specs=(any_space,) * 4,
        scratch_shapes=[
            pltpu.VMEM((4, 6) + row, BF16),
            pltpu.VMEM((2, 4, 2, TW * TILE, HEAD_DIM), BF16),
            pltpu.VMEM((2, 4, 2, TW * TILE, HEAD_DIM), BF16),
            pltpu.VMEM((4, 6) + row, F32),
            pltpu.VMEM((2, 5) + row, BF16),
            pltpu.VMEM((2, 5) + row, BF16),
            pltpu.VMEM((2,) + row, BF16),
            pltpu.VMEM((2, 5) + row, BF16),
            pltpu.VMEM((8, 128), F32),
            pltpu.VMEM((2, 2, 8, 128), F32),
            pltpu.VMEM((2, 128, KEYS), BF16),
            pltpu.VMEM((4, 6, 2, 128), F32),
            pltpu.VMEM((2, 4, 2, 4, KEYS), F32),
            dma((4,)), dma((2, 4)), dma((2, 4)), dma((WAVES,)), dma((2, 2)),
            dma((2,)), dma((2, 6)), dma((2,)), dma((2,)),
            dma, dma((4,)), dma((2,)), dma((2, 5)), dma((2,)), dma((2,)), dma,
        ],
        compiler_params=pltpu.CompilerParams(
            collective_id=0, has_side_effects=True, vmem_limit_bytes=56 * 1024 * 1024
        ),
        cost_estimate=pl.CostEstimate(flops=5_400_000_000, bytes_accessed=6_000_000, transcendentals=3_600_000),
        name="window_attention",
    )(queries, keys, values, out_grad, window_lists, valid_counts)


def solution(mesh):
    rows = P(("seq", "mp"), None)
    return jax.shard_map(
        on_device,
        mesh=mesh,
        in_specs=(rows, rows, rows, rows, P("seq", None), P()),
        out_specs=(rows, rows, rows, rows),
        check_vma=False,
    )
```

```python
import math

import jax
import jax.numpy as jnp
from jax import lax
from jax.experimental import pallas as pl
from jax.experimental.pallas import tpu as pltpu
from jax.sharding import PartitionSpec as P

HEADS = 24
HEAD_DIM = 128
D = HEADS * HEAD_DIM
TILE = 64
WINDOW = 27
TLAYERS = 8
NH = 8
TW = 4
TILES = TLAYERS * NH * TW
NX = 4
NZ = 8
NM = 8
WAVES = 3
KEYS = 9 * 2 * TILE
BIG = 1e30
SCALE = 1.0 / math.sqrt(HEAD_DIM)
EXP2_SCALE = SCALE / math.log(2.0)
MESH = pl.DeviceIdType.MESH
BF16 = jnp.bfloat16
F32 = jnp.float32


def place():
    seat = lax.axis_index("seq")
    m = lax.axis_index("mp")
    return seat // NZ, lax.rem(seat, NZ), m


def worker_z(part, m, wave):
    u = lax.rem(wave + m // 2, 2)
    v = lax.rem(m + wave // 2, 2)
    return jnp.where(part == 0, 3 - u + 4 * v, lax.rem(4 - 3 * u + 4 * v, NZ))


def work_of(z, m):
    zq = lax.rem(z, 4)
    zh = z // 4
    part = jnp.where(zq >= 2, 0, 1)
    u = jnp.where(part == 0, 3 - zq, zq)
    v = jnp.where(jnp.logical_and(part == 1, u == 0), 1 - zh, zh)
    same_v = v == lax.rem(m, 2)
    same_u = u == lax.rem(m // 2, 2)
    wave = jnp.where(same_u, jnp.where(same_v, 0, 2), 1)
    return part, wave, jnp.logical_or(same_u, same_v)


def greet_plane(x, z, m):
    barrier = pltpu.get_barrier_semaphore()

    def greet(i, carry):
        zz = i // NM
        mm = lax.rem(i, NM)

        @pl.when(jnp.logical_or(zz != z, mm != m))
        def _():
            pl.semaphore_signal(barrier, inc=1, device_id=(x * NZ + zz, mm), device_id_type=MESH)

        return carry

    lax.fori_loop(0, NZ * NM, greet, 0)

    @pl.when(x > 0)
    def _():
        pl.semaphore_signal(barrier, inc=1, device_id=((x - 1) * NZ + z, m), device_id_type=MESH)

    @pl.when(x < NX - 1)
    def _():
        pl.semaphore_signal(barrier, inc=1, device_id=((x + 1) * NZ + z, m), device_id_type=MESH)

    peers = NZ * NM - 1 + jnp.where(x > 0, 1, 0) + jnp.where(x < NX - 1, 1, 0)
    pl.semaphore_wait(barrier, peers)


def wait_for(ref, sem):
    pltpu.make_async_copy(ref, ref, sem).wait()


def send(src, dst, send_sem, recv_sem, seat, m):
    pltpu.make_async_remote_copy(
        src_ref=src, dst_ref=dst, send_sem=send_sem, recv_sem=recv_sem,
        device_id=(seat, m), device_id_type=MESH,
    ).start()


def dot(a, b, dims):
    return lax.dot_general(a, b, (dims, ((), ())), preferred_element_type=F32)


def tile_rows(w):
    return pl.ds(pl.multiple_of(w * TILE, TILE), TILE)


def head_columns(head):
    return pl.ds(pl.multiple_of(head * HEAD_DIM, HEAD_DIM), HEAD_DIM)


def kernel(
    q_ref, k_ref, v_ref, g_ref, list_ref, count_ref,
    att_out, gq_out, gk_out, gv_out,
    pool, qg, out, acc, edge, came, passed, total, flag_mine, flag_all, places, valid, bias,
    send_sem, kv_sem, qg_sem, flag_send, flag_sem, xsend, xsem, zsend, zsem,
    out_send, token_sem, edge_send, edge_sem, part_send, part_sem, total_send,
):
    x, z, m = place()
    zh = z // 4
    zl = lax.rem(z, 4)
    h = 2 * zl + m // 4
    w = lax.rem(m, 4)
    t = 2 * x + zh
    own = zl // 2
    part, wave, active = work_of(z, m)
    head = 3 * m + wave
    has_low = x > 0
    has_high = x < NX - 1
    low_seat = (x - 1) * NZ + z
    high_seat = (x + 1) * NZ + z
    other_seat = x * NZ + worker_z(1 - part, m, wave)

    spot = lax.broadcasted_iota(jnp.int32, (8, 128), 1)
    mine = lax.broadcasted_iota(jnp.int32, (8, 128), 0)
    near_t = t + spot // 12 - 1
    near_h = 2 * zl + mine // 4 + lax.rem(spot // 4, 3) - 1
    near = (near_t * NH + near_h) * TW + lax.rem(spot, 4)
    inside = (spot < 36) & (near_t >= 0) & (near_t < TLAYERS) & (near_h >= 0) & (near_h < NH)
    near = jnp.where(inside, near, -2)
    listed = jnp.zeros((8, 128), F32)
    for j in range(WINDOW):
        listed = jnp.where(list_ref[:, j : j + 1] == near, 1.0, listed)
    flag_mine[...] = listed
    pool[...] = jnp.zeros_like(pool)
    greet_plane(x, z, m)

    my_rows = tile_rows(lax.rem(w, 2))

    def send_kv(number, start, stop):
        def one(j, carry):
            wm = lax.rem(j + m + z, NM)
            seat = x * NZ + worker_z(own, wm, number)
            columns = head_columns(3 * wm + number)
            row = lax.rem(h, 4)
            for i, ref in ((0, k_ref), (1, v_ref)):
                send(
                    ref.at[:, columns], pool.at[1 + zh, 1 + row, i, w // 2, my_rows, :],
                    send_sem.at[i], kv_sem.at[zh, row], seat, wm,
                )
            return carry

        lax.fori_loop(start, stop, one, 0)

    def send_flags(number):
        send(
            flag_mine, flag_all.at[zh, lax.rem(zl, 2)],
            flag_send.at[number], flag_sem.at[zh, lax.rem(zl, 2)],
            x * NZ + worker_z(own, m, number), m,
        )

    def send_qg(number, start, stop):
        def one(j, carry):
            wm = lax.rem(j + m + z, NM)
            seat = x * NZ + worker_z(own, wm, number)
            columns = head_columns(3 * wm + number)
            row = lax.rem(h, 4)
            for i, ref in ((0, q_ref), (1, g_ref)):
                send(
                    ref.at[:, columns], qg.at[zh, row, i, tile_rows(w), :],
                    send_sem.at[2 + i], qg_sem.at[zh, row], seat, wm,
                )
            return carry

        lax.fori_loop(start, stop, one, 0)

    def row_of(i):
        return jnp.where(part == 0, 5 - i, i)

    def forward(i, carry):
        row = row_of(i)
        for side in range(2):
            @pl.when(i > 0)
            def _():
                wait_for(pool.at[1 + side, row], kv_sem.at[side, jnp.maximum(row, 1) - 1])

            @pl.when(i == 0)
            def _():
                wait_for(pool.at[1 + side, row], zsem.at[side])

            @pl.when(i == 1)
            def _():
                send(
                    pool.at[1 + side, row], pool.at[1 + side, jnp.where(part == 0, 0, 5)],
                    zsend.at[side], zsem.at[side], other_seat, m,
                )

        @pl.when(has_low)
        def _():
            send(pool.at[1, row], pool.at[3, row], xsend.at[0], xsem.at[1, row], low_seat, m)

        @pl.when(has_high)
        def _():
            send(pool.at[2, row], pool.at[0, row], xsend.at[1], xsem.at[0, row], high_seat, m)

        return carry

    def forward_own(number):
        @pl.when(jnp.logical_and(active, wave == number))
        def _():
            lax.fori_loop(1, 5, forward, 0)

    def forward_other(number):
        @pl.when(jnp.logical_and(active, wave == number))
        def _():
            forward(0, 0)

    send_flags(0)
    send_kv(0, 0, 8)
    send_flags(1)
    send_kv(1, 0, 8)
    send_flags(2)
    send_kv(2, 0, 8)
    send_qg(0, 0, 4)
    forward_own(0)
    send_qg(0, 4, 8)
    forward_own(1)
    send_qg(1, 0, 4)
    forward_other(0)
    send_qg(1, 4, 8)
    forward_own(2)
    send_qg(2, 0, 4)
    forward_other(1)
    send_qg(2, 4, 8)
    forward_other(2)

    def work():
        acc[...] = jnp.zeros_like(acc)
        lane = lax.broadcasted_iota(jnp.int32, (1, 128), 1)

        def mark(i, carry):
            layer = i // 6
            row = lax.rem(i, 6)
            key_t = 2 * x - 1 + layer
            key_h = 4 * part - 1 + row
            real = (key_t >= 0) & (key_t < TLAYERS) & (key_h >= 0) & (key_h < NH)
            first = jnp.where(real, (key_t * NH + key_h) * TW, 0)
            for pair in range(2):
                counts = [jnp.where(real, count_ref[first + 2 * pair + j], 0) for j in range(2)]
                until = jnp.where(lane < TILE, counts[0], counts[1] + TILE)
                valid[layer, row, pair : pair + 1, :] = jnp.where(lane < until, 1.0, 0.0)
            return carry

        lax.fori_loop(0, 24, mark, 0)

        key = lax.broadcasted_iota(jnp.int32, (128, KEYS), 1)
        flag = lax.broadcasted_iota(jnp.int32, (128, KEYS), 0)
        for pair in range(2):
            wanted = key // 128 * 4 + pair * 2 + lax.rem(key, 128) // TILE
            places[pair] = jnp.where(wanted == flag, 1.0, 0.0).astype(BF16)

        def make_bias(layer, carry):
            for a in range(2):
                wait_for(flag_all.at[layer, a], flag_sem.at[layer, a])
            for pair in range(2):
                for r in range(4):
                    if r % 2 == 0:
                        live = dot(flag_all[layer, r // 2].astype(BF16), places[pair], ((1,), (0,)))
                    ok = jnp.concatenate(
                        [valid[layer + a, r + b, pair : pair + 1, :] for a in range(3) for b in range(3)], axis=1
                    )
                    tiles = live[(r % 2) * 4 : (r % 2) * 4 + 4]
                    bias[layer, r, pair, 0:4, :] = (tiles * ok - 1.0) * BIG
            return carry

        lax.fori_loop(0, 2, make_bias, 0)

        def arrive(i, carry):
            row = row_of(i)

            @pl.when(has_low)
            def _():
                wait_for(pool.at[0, row], xsem.at[0, row])

            @pl.when(has_high)
            def _():
                wait_for(pool.at[3, row], xsem.at[1, row])

            return carry

        lax.fori_loop(0, 5, arrive, 0)

        position = lax.broadcasted_iota(jnp.int32, (TILE, HEAD_DIM), 0)

        def strip(layer, r):
            wait_for(qg.at[layer, r], qg_sem.at[layer, r])
            tile0 = ((2 * x + layer) * NH + 4 * part + r) * TW
            token_ok = jnp.concatenate([position < count_ref[tile0 + j] for j in range(TW)], axis=0)
            q = qg[layer, r, 0]
            g = qg[layer, r, 1]
            g = jnp.where(token_ok, g.astype(F32), 0.0).astype(BF16)
            scores, keys, values = [], [], []
            for pair in range(2):
                rows = slice(pair * TILE, pair * TILE + 3 * TILE)
                key = [pool[layer + a, pl.ds(r, 3), 0, pair].reshape(384, HEAD_DIM) for a in range(3)]
                value = [pool[layer + a, pl.ds(r, 3), 1, pair].reshape(384, HEAD_DIM) for a in range(3)]
                keys.append(jnp.concatenate(key, axis=0))
                values.append(jnp.concatenate(value, axis=0))
                out_of = jnp.concatenate(
                    [
                        jnp.broadcast_to(bias[layer, r, pair, pair + j : pair + j + 1, :], (TILE, KEYS))
                        for j in range(3)
                    ],
                    axis=0,
                )
                scores.append(dot(q[rows], keys[pair], ((1,), (1,))) + out_of)
            tops = [jnp.max(sc, axis=1, keepdims=True) for sc in scores]
            middle = jnp.maximum(tops[0][TILE:], tops[1][: 2 * TILE])
            top0 = jnp.concatenate([tops[0][:TILE], middle], axis=0)
            top1 = jnp.concatenate([middle, tops[1][2 * TILE :]], axis=0)
            expo = [jnp.exp2((sc - top) * EXP2_SCALE) for sc, top in zip(scores, (top0, top1))]
            sums = [jnp.sum(e, axis=1, keepdims=True) for e in expo]
            middle = sums[0][TILE:] + sums[1][: 2 * TILE]
            inv0 = 1.0 / jnp.concatenate([sums[0][:TILE], middle], axis=0)
            inv1 = 1.0 / jnp.concatenate([middle, sums[1][2 * TILE :]], axis=0)
            probs = [expo[0] * inv0, expo[1] * inv1]
            low = [p.astype(BF16) for p in probs]

            def join(a, b):
                return jnp.concatenate([a[:TILE], a[TILE:] + b[: 2 * TILE], b[2 * TILE :]], axis=0)

            attended = join(*[dot(low[i], values[i], ((1,), (0,))) for i in range(2)])
            attended = jnp.where(token_ok, attended, 0.0).astype(BF16)
            out[layer, r, 0] = attended
            delta = jnp.sum(g.astype(F32) * attended.astype(F32), axis=1, keepdims=True)
            grads = []
            for pair in range(2):
                rows = slice(pair * TILE, pair * TILE + 3 * TILE)
                dprobs = dot(g[rows], values[pair], ((1,), (1,)))
                dscores = (probs[pair] * (dprobs - delta[rows])).astype(BF16)
                grads.append(dot(dscores, keys[pair], ((1,), (0,))))
                grad_k = dot(dscores, q[rows], ((0,), (0,))).reshape(3, 3, 2 * TILE, HEAD_DIM)
                grad_v = dot(low[pair], g[rows], ((0,), (0,))).reshape(3, 3, 2 * TILE, HEAD_DIM)
                for a in range(3):
                    acc[layer + a, pl.ds(r, 3), 0, pair] += grad_k[a]
                    acc[layer + a, pl.ds(r, 3), 1, pair] += grad_v[a]
            out[layer, r, 1] = (join(*grads) * SCALE).astype(BF16)

        columns = head_columns(head)

        def seat_of(layer, row):
            return x * NZ + layer * 4 + (4 * part + row) // 2, lax.rem(row, 2) * 4

        def send_strip(layer, r):
            seat, m0 = seat_of(layer, r)

            def send_tile(j, carry):
                for i, ref in ((0, att_out), (1, gq_out)):
                    send(
                        out.at[layer, r, i, tile_rows(j), :], ref.at[:, columns],
                        out_send, token_sem.at[i], seat, m0 + j,
                    )
                return carry

            lax.fori_loop(0, TW, send_tile, 0)

        def scaled(layer, row, i):
            return acc[layer, row, i] * (SCALE if i == 0 else 1.0)

        def send_edge(i):
            row = row_of(i)

            @pl.when(has_low)
            def _():
                for j in range(2):
                    edge[0, i, j] = scaled(0, row, j).astype(BF16)
                send(edge.at[0, i], came.at[1, i], edge_send.at[0], edge_sem.at[1, i], low_seat, m)

            @pl.when(has_high)
            def _():
                for j in range(2):
                    edge[1, i, j] = scaled(3, row, j).astype(BF16)
                send(edge.at[1, i], came.at[0, i], edge_send.at[1], edge_sem.at[0, i], high_seat, m)

        def add_edge(side, i, row):
            @pl.when(has_high if side else has_low)
            def _():
                wait_for(came.at[side, i], edge_sem.at[side, i])
                for j in range(2):
                    total[side, i, j] = (scaled(1 + side, row, j) + came[side, i, j].astype(F32)).astype(BF16)

            @pl.when(jnp.logical_not(has_high if side else has_low))
            def _():
                for j in range(2):
                    total[side, i, j] = scaled(1 + side, row, j).astype(BF16)

        def finish(i):
            row = row_of(i)
            for side in (1, 0):
                add_edge(side, i, row)

                @pl.when(i == 0)
                def _():
                    send(
                        total.at[side, i], passed.at[side],
                        part_send.at[side], part_sem.at[side], other_seat, m,
                    )

                @pl.when(i == 1)
                def _():
                    wait_for(passed.at[side], part_sem.at[side])
                    total[side, i] = (total[side, i].astype(F32) + passed[side].astype(F32)).astype(BF16)

                @pl.when(i > 0)
                def _():
                    seat, m0 = seat_of(side, row - 1)

                    def send_tile(j, carry):
                        for n, ref in ((0, gk_out), (1, gv_out)):
                            send(
                                total.at[side, i, n, j // 2, tile_rows(lax.rem(j, 2)), :], ref.at[:, columns],
                                total_send, token_sem.at[2 + n], seat, m0 + j,
                            )
                        return carry

                    lax.fori_loop(0, TW, send_tile, 0)

        def step(i, carry):
            r = jnp.where(part == 0, 3 - i, i)

            def one(layer, carry):
                strip(layer, r)
                send_strip(layer, r)
                return carry

            lax.fori_loop(0, 2, one, 0)
            send_edge(i)

            @pl.when(i > 0)
            def _():
                finish(i - 1)

            return carry

        lax.fori_loop(0, 4, step, 0)
        send_edge(4)

        def last(i, carry):
            finish(i)
            return carry

        lax.fori_loop(3, 5, last, 0)

        wait_for(out, out_send)
        wait_for(total.at[:, pl.ds(1, 4)], total_send)
        for side in range(2):
            wait_for(pool.at[0, 0], zsend.at[side])
            wait_for(total.at[side, 0], part_send.at[side])

            @pl.when(has_high if side else has_low)
            def _():
                wait_for(pool.at[0, pl.ds(0, 5)], xsend.at[side])
                wait_for(edge.at[side], edge_send.at[side])

    pl.when(active)(work)

    for i, ref in enumerate((k_ref, v_ref, q_ref, g_ref)):
        wait_for(ref, send_sem.at[i])
    for i in range(WAVES):
        wait_for(flag_mine, flag_send.at[i])
    for i, ref in enumerate((att_out, gq_out, gk_out, gv_out)):
        wait_for(ref, token_sem.at[i])


def on_device(queries, keys, values, out_grad, window_lists, valid_counts):
    any_space = pl.BlockSpec(memory_space=pl.ANY)
    dma = pltpu.SemaphoreType.DMA
    row = (2, 2, 2 * TILE, HEAD_DIM)
    return pl.pallas_call(
        kernel,
        out_shape=(jax.ShapeDtypeStruct((TILE, D), BF16),) * 4,
        in_specs=[any_space] * 4
        + [pl.BlockSpec(memory_space=pltpu.VMEM), pl.BlockSpec(memory_space=pltpu.SMEM)],
        out_specs=(any_space,) * 4,
        scratch_shapes=[
            pltpu.VMEM((4, 6) + row, BF16),
            pltpu.VMEM((2, 4, 2, TW * TILE, HEAD_DIM), BF16),
            pltpu.VMEM((2, 4, 2, TW * TILE, HEAD_DIM), BF16),
            pltpu.VMEM((4, 6) + row, F32),
            pltpu.VMEM((2, 5) + row, BF16),
            pltpu.VMEM((2, 5) + row, BF16),
            pltpu.VMEM((2,) + row, BF16),
            pltpu.VMEM((2, 5) + row, BF16),
            pltpu.VMEM((8, 128), F32),
            pltpu.VMEM((2, 2, 8, 128), F32),
            pltpu.VMEM((2, 128, KEYS), BF16),
            pltpu.VMEM((4, 6, 2, 128), F32),
            pltpu.VMEM((2, 4, 2, 4, KEYS), F32),
            dma((4,)), dma((2, 4)), dma((2, 4)), dma((WAVES,)), dma((2, 2)),
            dma((2,)), dma((2, 6)), dma((2,)), dma((2,)),
            dma, dma((4,)), dma((2,)), dma((2, 5)), dma((2,)), dma((2,)), dma,
        ],
        compiler_params=pltpu.CompilerParams(
            collective_id=0, has_side_effects=True, vmem_limit_bytes=56 * 1024 * 1024
        ),
        cost_estimate=pl.CostEstimate(flops=5_400_000_000, bytes_accessed=6_000_000, transcendentals=3_600_000),
        name="window_attention",
    )(queries, keys, values, out_grad, window_lists, valid_counts)


def solution(mesh):
    rows = P(("seq", "mp"), None)
    return jax.shard_map(
        on_device,
        mesh=mesh,
        in_specs=(rows, rows, rows, rows, P("seq", None), P()),
        out_specs=(rows, rows, rows, rows),
        check_vma=False,
    )
```

```python
import math

import jax
import jax.numpy as jnp
from jax import lax
from jax.experimental import pallas as pl
from jax.experimental.pallas import tpu as pltpu
from jax.sharding import PartitionSpec as P

HEADS = 24
HEAD_DIM = 128
D = HEADS * HEAD_DIM
TILE = 64
WINDOW = 27
TLAYERS = 8
NH = 8
TW = 4
TILES = TLAYERS * NH * TW
NX = 4
NZ = 8
NM = 8
WAVES = 3
KEYS = 9 * 2 * TILE
BIG = 1e30
SCALE = 1.0 / math.sqrt(HEAD_DIM)
EXP2_SCALE = SCALE / math.log(2.0)
MESH = pl.DeviceIdType.MESH
BF16 = jnp.bfloat16
F32 = jnp.float32


def place():
    seat = lax.axis_index("seq")
    m = lax.axis_index("mp")
    return seat // NZ, lax.rem(seat, NZ), m


def worker_z(part, m, wave):
    u = lax.rem(wave + m // 2, 2)
    v = lax.rem(m + wave // 2, 2)
    return jnp.where(part == 0, 3 - u + 4 * v, lax.rem(4 - 3 * u + 4 * v, NZ))


def work_of(z, m):
    zq = lax.rem(z, 4)
    zh = z // 4
    part = jnp.where(zq >= 2, 0, 1)
    u = jnp.where(part == 0, 3 - zq, zq)
    v = jnp.where(jnp.logical_and(part == 1, u == 0), 1 - zh, zh)
    same_v = v == lax.rem(m, 2)
    same_u = u == lax.rem(m // 2, 2)
    wave = jnp.where(same_u, jnp.where(same_v, 0, 2), 1)
    return part, wave, jnp.logical_or(same_u, same_v)


def greet_plane(x, z, m):
    barrier = pltpu.get_barrier_semaphore()

    def greet(i, carry):
        zz = i // NM
        mm = lax.rem(i, NM)

        @pl.when(jnp.logical_or(zz != z, mm != m))
        def _():
            pl.semaphore_signal(barrier, inc=1, device_id=(x * NZ + zz, mm), device_id_type=MESH)

        return carry

    lax.fori_loop(0, NZ * NM, greet, 0)

    @pl.when(x > 0)
    def _():
        pl.semaphore_signal(barrier, inc=1, device_id=((x - 1) * NZ + z, m), device_id_type=MESH)

    @pl.when(x < NX - 1)
    def _():
        pl.semaphore_signal(barrier, inc=1, device_id=((x + 1) * NZ + z, m), device_id_type=MESH)

    peers = NZ * NM - 1 + jnp.where(x > 0, 1, 0) + jnp.where(x < NX - 1, 1, 0)
    pl.semaphore_wait(barrier, peers)


def wait_for(ref, sem):
    pltpu.make_async_copy(ref, ref, sem).wait()


def send(src, dst, send_sem, recv_sem, seat, m):
    pltpu.make_async_remote_copy(
        src_ref=src, dst_ref=dst, send_sem=send_sem, recv_sem=recv_sem,
        device_id=(seat, m), device_id_type=MESH,
    ).start()


def dot(a, b, dims):
    return lax.dot_general(a, b, (dims, ((), ())), preferred_element_type=F32)


def tile_rows(w):
    return pl.ds(pl.multiple_of(w * TILE, TILE), TILE)


def head_columns(head):
    return pl.ds(pl.multiple_of(head * HEAD_DIM, HEAD_DIM), HEAD_DIM)


def kernel(
    q_ref, k_ref, v_ref, g_ref, list_ref, count_ref,
    tokens,
    pool, qg, out, acc, edge, came, passed, total, flag_mine, flag_all, places, valid, bias,
    send_sem, kv_sem, qg_sem, flag_send, flag_sem, xsend, xsem, zsend, zsem,
    out_send, token_sem, edge_send, edge_sem, part_send, part_sem, total_send,
):
    x, z, m = place()
    zh = z // 4
    zl = lax.rem(z, 4)
    h = 2 * zl + m // 4
    w = lax.rem(m, 4)
    t = 2 * x + zh
    own = zl // 2
    part, wave, active = work_of(z, m)
    head = 3 * m + wave
    has_low = x > 0
    has_high = x < NX - 1
    low_seat = (x - 1) * NZ + z
    high_seat = (x + 1) * NZ + z
    other_seat = x * NZ + worker_z(1 - part, m, wave)

    spot = lax.broadcasted_iota(jnp.int32, (8, 128), 1)
    mine = lax.broadcasted_iota(jnp.int32, (8, 128), 0)
    near_t = t + spot // 12 - 1
    near_h = 2 * zl + mine // 4 + lax.rem(spot // 4, 3) - 1
    near = (near_t * NH + near_h) * TW + lax.rem(spot, 4)
    inside = (spot < 36) & (near_t >= 0) & (near_t < TLAYERS) & (near_h >= 0) & (near_h < NH)
    near = jnp.where(inside, near, -2)
    listed = jnp.zeros((8, 128), F32)
    for j in range(WINDOW):
        listed = jnp.where(list_ref[:, j : j + 1] == near, 1.0, listed)
    flag_mine[...] = listed
    pool[...] = jnp.zeros_like(pool)
    greet_plane(x, z, m)

    my_rows = tile_rows(lax.rem(w, 2))

    def send_kv(number, start, stop):
        def one(j, carry):
            wm = lax.rem(j + m + z, NM)
            seat = x * NZ + worker_z(own, wm, number)
            columns = head_columns(3 * wm + number)
            row = lax.rem(h, 4)
            for i, ref in ((0, k_ref), (1, v_ref)):
                send(
                    ref.at[:, columns], pool.at[1 + zh, 1 + row, i, w // 2, my_rows, :],
                    send_sem.at[i], kv_sem.at[zh, row], seat, wm,
                )
            return carry

        lax.fori_loop(start, stop, one, 0)

    def send_flags(number):
        send(
            flag_mine, flag_all.at[zh, lax.rem(zl, 2)],
            flag_send.at[number], flag_sem.at[zh, lax.rem(zl, 2)],
            x * NZ + worker_z(own, m, number), m,
        )

    def send_qg(number, start, stop):
        def one(j, carry):
            wm = lax.rem(j + m + z, NM)
            seat = x * NZ + worker_z(own, wm, number)
            columns = head_columns(3 * wm + number)
            row = lax.rem(h, 4)
            for i, ref in ((0, q_ref), (1, g_ref)):
                send(
                    ref.at[:, columns], qg.at[zh, row, i, tile_rows(w), :],
                    send_sem.at[2 + i], qg_sem.at[zh, row], seat, wm,
                )
            return carry

        lax.fori_loop(start, stop, one, 0)

    def row_of(i):
        return jnp.where(part == 0, 5 - i, i)

    def forward(i, carry):
        row = row_of(i)
        for side in range(2):
            @pl.when(i > 0)
            def _():
                wait_for(pool.at[1 + side, row], kv_sem.at[side, jnp.maximum(row, 1) - 1])

            @pl.when(i == 0)
            def _():
                wait_for(pool.at[1 + side, row], zsem.at[side])

            @pl.when(i == 1)
            def _():
                send(
                    pool.at[1 + side, row], pool.at[1 + side, jnp.where(part == 0, 0, 5)],
                    zsend.at[side], zsem.at[side], other_seat, m,
                )

        @pl.when(has_low)
        def _():
            send(pool.at[1, row], pool.at[3, row], xsend.at[0], xsem.at[1, row], low_seat, m)

        @pl.when(has_high)
        def _():
            send(pool.at[2, row], pool.at[0, row], xsend.at[1], xsem.at[0, row], high_seat, m)

        return carry

    def forward_own(number):
        @pl.when(jnp.logical_and(active, wave == number))
        def _():
            lax.fori_loop(1, 5, forward, 0)

    def forward_other(number):
        @pl.when(jnp.logical_and(active, wave == number))
        def _():
            forward(0, 0)

    send_flags(0)
    send_kv(0, 0, 8)
    send_flags(1)
    send_kv(1, 0, 8)
    send_flags(2)
    send_kv(2, 0, 4)
    forward_own(0)
    send_kv(2, 4, 8)
    send_qg(0, 0, 4)
    forward_own(1)
    send_qg(0, 4, 8)
    forward_other(0)
    forward_own(2)
    send_qg(1, 0, 4)
    forward_other(1)
    send_qg(1, 4, 8)
    forward_other(2)
    send_qg(2, 0, 8)

    def work():
        acc[...] = jnp.zeros_like(acc)
        lane = lax.broadcasted_iota(jnp.int32, (1, 128), 1)

        def mark(i, carry):
            layer = i // 6
            row = lax.rem(i, 6)
            key_t = 2 * x - 1 + layer
            key_h = 4 * part - 1 + row
            real = (key_t >= 0) & (key_t < TLAYERS) & (key_h >= 0) & (key_h < NH)
            first = jnp.where(real, (key_t * NH + key_h) * TW, 0)
            for pair in range(2):
                counts = [jnp.where(real, count_ref[first + 2 * pair + j], 0) for j in range(2)]
                until = jnp.where(lane < TILE, counts[0], counts[1] + TILE)
                valid[layer, row, pair : pair + 1, :] = jnp.where(lane < until, 1.0, 0.0)
            return carry

        lax.fori_loop(0, 24, mark, 0)

        key = lax.broadcasted_iota(jnp.int32, (128, KEYS), 1)
        flag = lax.broadcasted_iota(jnp.int32, (128, KEYS), 0)
        for pair in range(2):
            wanted = key // 128 * 4 + pair * 2 + lax.rem(key, 128) // TILE
            places[pair] = jnp.where(wanted == flag, 1.0, 0.0).astype(BF16)

        def make_bias(layer, carry):
            for a in range(2):
                wait_for(flag_all.at[layer, a], flag_sem.at[layer, a])
            for pair in range(2):
                for r in range(4):
                    if r % 2 == 0:
                        live = dot(flag_all[layer, r // 2].astype(BF16), places[pair], ((1,), (0,)))
                    ok = jnp.concatenate(
                        [valid[layer + a, r + b, pair : pair + 1, :] for a in range(3) for b in range(3)], axis=1
                    )
                    tiles = live[(r % 2) * 4 : (r % 2) * 4 + 4]
                    bias[layer, r, pair, 0:4, :] = (tiles * ok - 1.0) * BIG
            return carry

        lax.fori_loop(0, 2, make_bias, 0)

        def arrive(i, carry):
            row = row_of(i)

            @pl.when(has_low)
            def _():
                wait_for(pool.at[0, row], xsem.at[0, row])

            @pl.when(has_high)
            def _():
                wait_for(pool.at[3, row], xsem.at[1, row])

            return carry

        lax.fori_loop(0, 5, arrive, 0)

        position = lax.broadcasted_iota(jnp.int32, (TILE, HEAD_DIM), 0)

        def strip(layer, r):
            wait_for(qg.at[layer, r], qg_sem.at[layer, r])
            tile0 = ((2 * x + layer) * NH + 4 * part + r) * TW
            token_ok = jnp.concatenate([position < count_ref[tile0 + j] for j in range(TW)], axis=0)
            q = qg[layer, r, 0]
            g = qg[layer, r, 1]
            g = jnp.where(token_ok, g.astype(F32), 0.0).astype(BF16)
            scores, keys, values = [], [], []
            for pair in range(2):
                rows = slice(pair * TILE, pair * TILE + 3 * TILE)
                key = [pool[layer + a, pl.ds(r, 3), 0, pair].reshape(384, HEAD_DIM) for a in range(3)]
                value = [pool[layer + a, pl.ds(r, 3), 1, pair].reshape(384, HEAD_DIM) for a in range(3)]
                keys.append(jnp.concatenate(key, axis=0))
                values.append(jnp.concatenate(value, axis=0))
                out_of = jnp.concatenate(
                    [
                        jnp.broadcast_to(bias[layer, r, pair, pair + j : pair + j + 1, :], (TILE, KEYS))
                        for j in range(3)
                    ],
                    axis=0,
                )
                scores.append(dot(q[rows], keys[pair], ((1,), (1,))) + out_of)
            tops = [jnp.max(sc, axis=1, keepdims=True) for sc in scores]
            middle = jnp.maximum(tops[0][TILE:], tops[1][: 2 * TILE])
            top0 = jnp.concatenate([tops[0][:TILE], middle], axis=0)
            top1 = jnp.concatenate([middle, tops[1][2 * TILE :]], axis=0)
            expo = [jnp.exp2((sc - top) * EXP2_SCALE) for sc, top in zip(scores, (top0, top1))]
            sums = [jnp.sum(e, axis=1, keepdims=True) for e in expo]
            middle = sums[0][TILE:] + sums[1][: 2 * TILE]
            inv0 = 1.0 / jnp.concatenate([sums[0][:TILE], middle], axis=0)
            inv1 = 1.0 / jnp.concatenate([middle, sums[1][2 * TILE :]], axis=0)
            probs = [expo[0] * inv0, expo[1] * inv1]
            low = [p.astype(BF16) for p in probs]

            def join(a, b):
                return jnp.concatenate([a[:TILE], a[TILE:] + b[: 2 * TILE], b[2 * TILE :]], axis=0)

            attended = join(*[dot(low[i], values[i], ((1,), (0,))) for i in range(2)])
            attended = jnp.where(token_ok, attended, 0.0).astype(BF16)
            out[layer, r, 0] = attended
            delta = jnp.sum(g.astype(F32) * attended.astype(F32), axis=1, keepdims=True)
            grads = []
            for pair in range(2):
                rows = slice(pair * TILE, pair * TILE + 3 * TILE)
                dprobs = dot(g[rows], values[pair], ((1,), (1,)))
                dscores = (probs[pair] * (dprobs - delta[rows])).astype(BF16)
                grads.append(dot(dscores, keys[pair], ((1,), (0,))))
                grad_k = dot(dscores, q[rows], ((0,), (0,))).reshape(3, 3, 2 * TILE, HEAD_DIM)
                grad_v = dot(low[pair], g[rows], ((0,), (0,))).reshape(3, 3, 2 * TILE, HEAD_DIM)
                for a in range(3):
                    acc[layer + a, pl.ds(r, 3), 0, pair] += grad_k[a]
                    acc[layer + a, pl.ds(r, 3), 1, pair] += grad_v[a]
            out[layer, r, 1] = (join(*grads) * SCALE).astype(BF16)

        columns = head_columns(head)

        def seat_of(layer, row):
            return x * NZ + layer * 4 + (4 * part + row) // 2, lax.rem(row, 2) * 4

        def send_strip(layer, r):
            seat, m0 = seat_of(layer, r)

            def send_tile(j, carry):
                send(
                    out.at[layer, r, :, tile_rows(j), :], tokens.at[pl.ds(0, 2), :, columns],
                    out_send, token_sem.at[0], seat, m0 + j,
                )
                return carry

            lax.fori_loop(0, TW, send_tile, 0)

        def scaled(layer, row, i):
            return acc[layer, row, i] * (SCALE if i == 0 else 1.0)

        def has(side):
            return jnp.where(side == 0, x, NX - 1 - x) > 0

        def send_edge(i, side):
            @pl.when(has(side))
            def _():
                for j in range(2):
                    edge[side, i, j] = scaled(3 * side, row_of(i), j).astype(BF16)
                send(
                    edge.at[side, i], came.at[1 - side, i], edge_send.at[side], edge_sem.at[1 - side, i],
                    jnp.where(side == 0, low_seat, high_seat), m,
                )

        def finish(i, side):
            row = row_of(i)

            @pl.when(has(side))
            def _():
                wait_for(came.at[side, i], edge_sem.at[side, i])
                for j in range(2):
                    total[side, i, j] = (scaled(1 + side, row, j) + came[side, i, j].astype(F32)).astype(BF16)

            @pl.when(jnp.logical_not(has(side)))
            def _():
                for j in range(2):
                    total[side, i, j] = scaled(1 + side, row, j).astype(BF16)

            @pl.when(i == 0)
            def _():
                send(
                    total.at[side, i], passed.at[side],
                    part_send.at[side], part_sem.at[side], other_seat, m,
                )

            @pl.when(i == 1)
            def _():
                wait_for(passed.at[side], part_sem.at[side])
                total[side, i] = (total[side, i].astype(F32) + passed[side].astype(F32)).astype(BF16)

            @pl.when(i > 0)
            def _():
                seat, m0 = seat_of(side, row - 1)

                def send_tile(j, carry):
                    send(
                        total.at[side, i, :, j // 2, tile_rows(lax.rem(j, 2)), :],
                        tokens.at[pl.ds(2, 2), :, columns],
                        total_send, token_sem.at[1], seat, m0 + j,
                    )
                    return carry

                lax.fori_loop(0, TW, send_tile, 0)

        def step(i, carry):
            r = jnp.where(part == 0, 3 - i, i)

            def one(layer, carry):
                strip(layer, r)
                send_strip(layer, r)
                send_edge(i, layer)

                @pl.when(i == 3)
                def _():
                    send_edge(4, layer)

                @pl.when(jnp.logical_and(i > 0, layer == 0))
                def _():
                    finish(i - 1, 1)
                    finish(i - 1, 0)

                return carry

            return lax.fori_loop(0, 2, one, carry)

        lax.fori_loop(0, 4, step, 0)

        def last(n, carry):
            finish(3 + lax.rem(n, 2), 1 - n // 2)
            return carry

        lax.fori_loop(0, 4, last, 0)

        wait_for(out, out_send)
        wait_for(total.at[:, pl.ds(1, 4)], total_send)
        for side in range(2):
            wait_for(pool.at[0, 0], zsend.at[side])
            wait_for(total.at[side, 0], part_send.at[side])

            @pl.when(has_high if side else has_low)
            def _():
                wait_for(pool.at[0, pl.ds(0, 5)], xsend.at[side])
                wait_for(edge.at[side], edge_send.at[side])

    pl.when(active)(work)

    for i, ref in enumerate((k_ref, v_ref, q_ref, g_ref)):
        wait_for(ref, send_sem.at[i])
    for i in range(WAVES):
        wait_for(flag_mine, flag_send.at[i])
    for i in range(2):
        wait_for(tokens.at[pl.ds(2 * i, 2)], token_sem.at[i])


def relay_kernel(tokens, *outs):
    for i, ref in enumerate(outs):
        ref[...] = tokens[i]


def on_device(queries, keys, values, out_grad, window_lists, valid_counts):
    any_space = pl.BlockSpec(memory_space=pl.ANY)
    dma = pltpu.SemaphoreType.DMA
    row = (2, 2, 2 * TILE, HEAD_DIM)
    tokens = pl.pallas_call(
        kernel,
        out_shape=jax.ShapeDtypeStruct((4, TILE, D), BF16),
        in_specs=[any_space] * 4
        + [pl.BlockSpec(memory_space=pltpu.VMEM), pl.BlockSpec(memory_space=pltpu.SMEM)],
        out_specs=any_space,
        scratch_shapes=[
            pltpu.VMEM((4, 6) + row, BF16),
            pltpu.VMEM((2, 4, 2, TW * TILE, HEAD_DIM), BF16),
            pltpu.VMEM((2, 4, 2, TW * TILE, HEAD_DIM), BF16),
            pltpu.VMEM((4, 6) + row, F32),
            pltpu.VMEM((2, 5) + row, BF16),
            pltpu.VMEM((2, 5) + row, BF16),
            pltpu.VMEM((2,) + row, BF16),
            pltpu.VMEM((2, 5) + row, BF16),
            pltpu.VMEM((8, 128), F32),
            pltpu.VMEM((2, 2, 8, 128), F32),
            pltpu.VMEM((2, 128, KEYS), BF16),
            pltpu.VMEM((4, 6, 2, 128), F32),
            pltpu.VMEM((2, 4, 2, 4, KEYS), F32),
            dma((4,)), dma((2, 4)), dma((2, 4)), dma((WAVES,)), dma((2, 2)),
            dma((2,)), dma((2, 6)), dma((2,)), dma((2,)),
            dma, dma((2,)), dma((2,)), dma((2, 5)), dma((2,)), dma((2,)), dma,
        ],
        compiler_params=pltpu.CompilerParams(
            collective_id=0, has_side_effects=True, vmem_limit_bytes=56 * 1024 * 1024
        ),
        cost_estimate=pl.CostEstimate(flops=5_400_000_000, bytes_accessed=6_000_000, transcendentals=3_600_000),
        name="window_attention",
    )(queries, keys, values, out_grad, window_lists, valid_counts)

    block = pl.BlockSpec((16, D), lambda i: (i, 0))
    return pl.pallas_call(
        relay_kernel,
        grid=(TILE // 16,),
        out_shape=(jax.ShapeDtypeStruct((TILE, D), BF16),) * 4,
        in_specs=[pl.BlockSpec((4, 16, D), lambda i: (0, i, 0))],
        out_specs=(block,) * 4,
        name="relay",
    )(tokens)


def solution(mesh):
    rows = P(("seq", "mp"), None)
    return jax.shard_map(
        on_device,
        mesh=mesh,
        in_specs=(rows, rows, rows, rows, P("seq", None), P()),
        out_specs=(rows, rows, rows, rows),
        check_vma=False,
    )
```

```python
import math

import jax
import jax.numpy as jnp
from jax import lax
from jax.experimental import pallas as pl
from jax.experimental.pallas import tpu as pltpu
from jax.sharding import PartitionSpec as P

HEADS = 24
HEAD_DIM = 128
D = HEADS * HEAD_DIM
TILE = 64
WINDOW = 27
TLAYERS = 8
NH = 8
TW = 4
TILES = TLAYERS * NH * TW
NX = 4
NZ = 8
NM = 8
WAVES = 3
KEYS = 9 * 2 * TILE
BIG = 1e30
SCALE = 1.0 / math.sqrt(HEAD_DIM)
EXP2_SCALE = SCALE / math.log(2.0)
MESH = pl.DeviceIdType.MESH
BF16 = jnp.bfloat16
F32 = jnp.float32


def place():
    seat = lax.axis_index("seq")
    m = lax.axis_index("mp")
    return seat // NZ, lax.rem(seat, NZ), m


def worker_z(part, m, wave):
    u = lax.rem(wave + m // 2, 2)
    v = lax.rem(m + wave // 2, 2)
    return jnp.where(part == 0, 3 - u + 4 * v, lax.rem(4 - 3 * u + 4 * v, NZ))


def work_of(z, m):
    zq = lax.rem(z, 4)
    zh = z // 4
    part = jnp.where(zq >= 2, 0, 1)
    u = jnp.where(part == 0, 3 - zq, zq)
    v = jnp.where(jnp.logical_and(part == 1, u == 0), 1 - zh, zh)
    same_v = v == lax.rem(m, 2)
    same_u = u == lax.rem(m // 2, 2)
    wave = jnp.where(same_u, jnp.where(same_v, 0, 2), 1)
    return part, wave, jnp.logical_or(same_u, same_v)


def greet(x, z, m, part, wave, active):
    barrier = pltpu.get_barrier_semaphore()

    def signal(seat, mm):
        pl.semaphore_signal(barrier, inc=1, device_id=(seat, mm), device_id_type=MESH)

    @pl.when(active)
    def _():
        def owner(d, carry):
            zz = 2 * part + lax.rem(d // NM, 2) + 4 * (d // (2 * NM))
            signal(x * NZ + zz, lax.rem(m + d, NM))
            return carry

        lax.fori_loop(0, 4 * NM, owner, 0)
        signal(x * NZ + worker_z(1 - part, m, wave), m)

        @pl.when(x > 0)
        def _():
            signal((x - 1) * NZ + z, m)

        @pl.when(x < NX - 1)
        def _():
            signal((x + 1) * NZ + z, m)

    near = 1 + jnp.where(x > 0, 1, 0) + jnp.where(x < NX - 1, 1, 0)
    pl.semaphore_wait(barrier, HEADS + jnp.where(active, near, 0))


def wait_for(ref, sem):
    pltpu.make_async_copy(ref, ref, sem).wait()


def send(src, dst, send_sem, recv_sem, seat, m):
    pltpu.make_async_remote_copy(
        src_ref=src, dst_ref=dst, send_sem=send_sem, recv_sem=recv_sem,
        device_id=(seat, m), device_id_type=MESH,
    ).start()


def dot(a, b, dims):
    return lax.dot_general(a, b, (dims, ((), ())), preferred_element_type=F32)


def tile_rows(w):
    return pl.ds(pl.multiple_of(w * TILE, TILE), TILE)


def head_columns(head):
    return pl.ds(pl.multiple_of(head * HEAD_DIM, HEAD_DIM), HEAD_DIM)


def kernel(
    q_ref, k_ref, v_ref, g_ref, list_ref, count_ref,
    tokens,
    pool, qg, out, acc, edge, came, passed, total, flag_mine, flag_all, places, valid, bias,
    send_sem, kv_sem, qg_sem, flag_send, flag_sem, xsend, xsem, zsend, zsem,
    out_send, token_sem, edge_send, edge_sem, part_send, part_sem, total_send,
):
    x, z, m = place()
    zh = z // 4
    zl = lax.rem(z, 4)
    h = 2 * zl + m // 4
    w = lax.rem(m, 4)
    t = 2 * x + zh
    own = zl // 2
    part, wave, active = work_of(z, m)
    head = 3 * m + wave
    has_low = x > 0
    has_high = x < NX - 1
    low_seat = (x - 1) * NZ + z
    high_seat = (x + 1) * NZ + z
    other_seat = x * NZ + worker_z(1 - part, m, wave)

    spot = lax.broadcasted_iota(jnp.int32, (8, 128), 1)
    mine = lax.broadcasted_iota(jnp.int32, (8, 128), 0)
    near_t = t + spot // 12 - 1
    near_h = 2 * zl + mine // 4 + lax.rem(spot // 4, 3) - 1
    near = (near_t * NH + near_h) * TW + lax.rem(spot, 4)
    inside = (spot < 36) & (near_t >= 0) & (near_t < TLAYERS) & (near_h >= 0) & (near_h < NH)
    near = jnp.where(inside, near, -2)
    listed = jnp.zeros((8, 128), F32)
    for j in range(WINDOW):
        listed = jnp.where(list_ref[:, j : j + 1] == near, 1.0, listed)
    flag_mine[...] = listed
    pool[...] = jnp.zeros_like(pool)
    greet(x, z, m, part, wave, active)

    my_rows = tile_rows(lax.rem(w, 2))

    def send_kv(number, start, stop):
        def one(j, carry):
            wm = lax.rem(j + m + z, NM)
            seat = x * NZ + worker_z(own, wm, number)
            columns = head_columns(3 * wm + number)
            row = lax.rem(h, 4)
            for i, ref in ((0, k_ref), (1, v_ref)):
                send(
                    ref.at[:, columns], pool.at[1 + zh, 1 + row, i, w // 2, my_rows, :],
                    send_sem.at[i], kv_sem.at[zh, row], seat, wm,
                )
            return carry

        lax.fori_loop(start, stop, one, 0)

    def send_flags(number):
        send(
            flag_mine, flag_all.at[zh, lax.rem(zl, 2)],
            flag_send.at[number], flag_sem.at[zh, lax.rem(zl, 2)],
            x * NZ + worker_z(own, m, number), m,
        )

    def send_qg(number, start, stop):
        def one(j, carry):
            wm = lax.rem(j + m + z, NM)
            seat = x * NZ + worker_z(own, wm, number)
            columns = head_columns(3 * wm + number)
            row = lax.rem(h, 4)
            for i, ref in ((0, q_ref), (1, g_ref)):
                send(
                    ref.at[:, columns], qg.at[zh, row, i, tile_rows(w), :],
                    send_sem.at[2 + i], qg_sem.at[zh, row], seat, wm,
                )
            return carry

        lax.fori_loop(start, stop, one, 0)

    def row_of(i):
        return jnp.where(part == 0, 5 - i, i)

    def forward(i, carry):
        row = row_of(i)
        for side in range(2):
            @pl.when(i > 0)
            def _():
                wait_for(pool.at[1 + side, row], kv_sem.at[side, jnp.maximum(row, 1) - 1])

            @pl.when(i == 0)
            def _():
                wait_for(pool.at[1 + side, row], zsem.at[side])

            @pl.when(i == 1)
            def _():
                send(
                    pool.at[1 + side, row], pool.at[1 + side, jnp.where(part == 0, 0, 5)],
                    zsend.at[side], zsem.at[side], other_seat, m,
                )

        @pl.when(has_low)
        def _():
            send(pool.at[1, row], pool.at[3, row], xsend.at[0], xsem.at[1, row], low_seat, m)

        @pl.when(has_high)
        def _():
            send(pool.at[2, row], pool.at[0, row], xsend.at[1], xsem.at[0, row], high_seat, m)

        return carry

    def forward_own(number):
        @pl.when(jnp.logical_and(active, wave == number))
        def _():
            lax.fori_loop(1, 5, forward, 0)

    def forward_other(number):
        @pl.when(jnp.logical_and(active, wave == number))
        def _():
            forward(0, 0)

    send_flags(0)
    send_kv(0, 0, 8)
    send_flags(1)
    send_kv(1, 0, 8)
    send_flags(2)
    send_kv(2, 0, 4)
    forward_own(0)
    send_kv(2, 4, 8)
    send_qg(0, 0, 4)
    forward_own(1)
    send_qg(0, 4, 8)
    forward_other(0)
    forward_own(2)
    send_qg(1, 0, 4)
    forward_other(1)
    send_qg(1, 4, 8)
    forward_other(2)
    send_qg(2, 0, 8)

    def work():
        acc[...] = jnp.zeros_like(acc)
        lane = lax.broadcasted_iota(jnp.int32, (1, 128), 1)

        def mark(i, carry):
            layer = i // 6
            row = lax.rem(i, 6)
            key_t = 2 * x - 1 + layer
            key_h = 4 * part - 1 + row
            real = (key_t >= 0) & (key_t < TLAYERS) & (key_h >= 0) & (key_h < NH)
            first = jnp.where(real, (key_t * NH + key_h) * TW, 0)
            for pair in range(2):
                counts = [jnp.where(real, count_ref[first + 2 * pair + j], 0) for j in range(2)]
                until = jnp.where(lane < TILE, counts[0], counts[1] + TILE)
                valid[layer, row, pair : pair + 1, :] = jnp.where(lane < until, 1.0, 0.0)
            return carry

        lax.fori_loop(0, 24, mark, 0)

        key = lax.broadcasted_iota(jnp.int32, (128, KEYS), 1)
        flag = lax.broadcasted_iota(jnp.int32, (128, KEYS), 0)
        for pair in range(2):
            wanted = key // 128 * 4 + pair * 2 + lax.rem(key, 128) // TILE
            places[pair] = jnp.where(wanted == flag, 1.0, 0.0).astype(BF16)

        def make_bias(layer, carry):
            for a in range(2):
                wait_for(flag_all.at[layer, a], flag_sem.at[layer, a])
            for pair in range(2):
                for r in range(4):
                    if r % 2 == 0:
                        live = dot(flag_all[layer, r // 2].astype(BF16), places[pair], ((1,), (0,)))
                    ok = jnp.concatenate(
                        [valid[layer + a, r + b, pair : pair + 1, :] for a in range(3) for b in range(3)], axis=1
                    )
                    tiles = live[(r % 2) * 4 : (r % 2) * 4 + 4]
                    bias[layer, r, pair, 0:4, :] = (tiles * ok - 1.0) * BIG
            return carry

        lax.fori_loop(0, 2, make_bias, 0)

        def arrive(i, carry):
            row = row_of(i)

            @pl.when(has_low)
            def _():
                wait_for(pool.at[0, row], xsem.at[0, row])

            @pl.when(has_high)
            def _():
                wait_for(pool.at[3, row], xsem.at[1, row])

            return carry

        lax.fori_loop(0, 5, arrive, 0)

        position = lax.broadcasted_iota(jnp.int32, (TILE, HEAD_DIM), 0)

        def strip(layer, r):
            wait_for(qg.at[layer, r], qg_sem.at[layer, r])
            tile0 = ((2 * x + layer) * NH + 4 * part + r) * TW
            token_ok = jnp.concatenate([position < count_ref[tile0 + j] for j in range(TW)], axis=0)
            q = qg[layer, r, 0]
            g = qg[layer, r, 1]
            g = jnp.where(token_ok, g.astype(F32), 0.0).astype(BF16)
            scores, keys, values = [], [], []
            for pair in range(2):
                rows = slice(pair * TILE, pair * TILE + 3 * TILE)
                key = [pool[layer + a, pl.ds(r, 3), 0, pair].reshape(384, HEAD_DIM) for a in range(3)]
                value = [pool[layer + a, pl.ds(r, 3), 1, pair].reshape(384, HEAD_DIM) for a in range(3)]
                keys.append(jnp.concatenate(key, axis=0))
                values.append(jnp.concatenate(value, axis=0))
                out_of = jnp.concatenate(
                    [
                        jnp.broadcast_to(bias[layer, r, pair, pair + j : pair + j + 1, :], (TILE, KEYS))
                        for j in range(3)
                    ],
                    axis=0,
                )
                scores.append(dot(q[rows], keys[pair], ((1,), (1,))) + out_of)
            tops = [jnp.max(sc, axis=1, keepdims=True) for sc in scores]
            middle = jnp.maximum(tops[0][TILE:], tops[1][: 2 * TILE])
            top0 = jnp.concatenate([tops[0][:TILE], middle], axis=0)
            top1 = jnp.concatenate([middle, tops[1][2 * TILE :]], axis=0)
            expo = [jnp.exp2((sc - top) * EXP2_SCALE) for sc, top in zip(scores, (top0, top1))]
            sums = [jnp.sum(e, axis=1, keepdims=True) for e in expo]
            middle = sums[0][TILE:] + sums[1][: 2 * TILE]
            inv0 = 1.0 / jnp.concatenate([sums[0][:TILE], middle], axis=0)
            inv1 = 1.0 / jnp.concatenate([middle, sums[1][2 * TILE :]], axis=0)
            probs = [expo[0] * inv0, expo[1] * inv1]
            low = [p.astype(BF16) for p in probs]

            def join(a, b):
                return jnp.concatenate([a[:TILE], a[TILE:] + b[: 2 * TILE], b[2 * TILE :]], axis=0)

            attended = join(*[dot(low[i], values[i], ((1,), (0,))) for i in range(2)])
            attended = jnp.where(token_ok, attended, 0.0).astype(BF16)
            out[layer, r, 0] = attended
            delta = jnp.sum(g.astype(F32) * attended.astype(F32), axis=1, keepdims=True)
            grads = []
            for pair in range(2):
                rows = slice(pair * TILE, pair * TILE + 3 * TILE)
                dprobs = dot(g[rows], values[pair], ((1,), (1,)))
                dscores = (probs[pair] * (dprobs - delta[rows])).astype(BF16)
                grads.append(dot(dscores, keys[pair], ((1,), (0,))))
                grad_k = dot(dscores, q[rows], ((0,), (0,))).reshape(3, 3, 2 * TILE, HEAD_DIM)
                grad_v = dot(low[pair], g[rows], ((0,), (0,))).reshape(3, 3, 2 * TILE, HEAD_DIM)
                for a in range(3):
                    acc[layer + a, pl.ds(r, 3), 0, pair] += grad_k[a]
                    acc[layer + a, pl.ds(r, 3), 1, pair] += grad_v[a]
            out[layer, r, 1] = (join(*grads) * SCALE).astype(BF16)

        columns = head_columns(head)

        def seat_of(layer, row):
            return x * NZ + layer * 4 + (4 * part + row) // 2, lax.rem(row, 2) * 4

        def send_strip(layer, r):
            seat, m0 = seat_of(layer, r)

            def send_tile(j, carry):
                send(
                    out.at[layer, r, :, tile_rows(j), :], tokens.at[pl.ds(0, 2), :, columns],
                    out_send, token_sem.at[0], seat, m0 + j,
                )
                return carry

            lax.fori_loop(0, TW, send_tile, 0)

        def scaled(layer, row, i):
            return acc[layer, row, i] * (SCALE if i == 0 else 1.0)

        def has(side):
            return jnp.where(side == 0, x, NX - 1 - x) > 0

        def send_edge(i, side):
            @pl.when(has(side))
            def _():
                for j in range(2):
                    edge[side, i, j] = scaled(3 * side, row_of(i), j).astype(BF16)
                send(
                    edge.at[side, i], came.at[1 - side, i], edge_send.at[side], edge_sem.at[1 - side, i],
                    jnp.where(side == 0, low_seat, high_seat), m,
                )

        def finish(i, side):
            row = row_of(i)

            @pl.when(has(side))
            def _():
                wait_for(came.at[side, i], edge_sem.at[side, i])
                for j in range(2):
                    total[side, i, j] = (scaled(1 + side, row, j) + came[side, i, j].astype(F32)).astype(BF16)

            @pl.when(jnp.logical_not(has(side)))
            def _():
                for j in range(2):
                    total[side, i, j] = scaled(1 + side, row, j).astype(BF16)

            @pl.when(i == 0)
            def _():
                send(
                    total.at[side, i], passed.at[side],
                    part_send.at[side], part_sem.at[side], other_seat, m,
                )

            @pl.when(i == 1)
            def _():
                wait_for(passed.at[side], part_sem.at[side])
                total[side, i] = (total[side, i].astype(F32) + passed[side].astype(F32)).astype(BF16)

            @pl.when(i > 0)
            def _():
                seat, m0 = seat_of(side, row - 1)

                def send_tile(j, carry):
                    send(
                        total.at[side, i, :, j // 2, tile_rows(lax.rem(j, 2)), :],
                        tokens.at[pl.ds(2, 2), :, columns],
                        total_send, token_sem.at[1], seat, m0 + j,
                    )
                    return carry

                lax.fori_loop(0, TW, send_tile, 0)

        def step(i, carry):
            r = jnp.where(part == 0, 3 - i, i)

            def one(layer, carry):
                strip(layer, r)
                send_strip(layer, r)
                send_edge(i, layer)

                @pl.when(i == 3)
                def _():
                    send_edge(4, layer)

                @pl.when(jnp.logical_and(i > 0, layer == 0))
                def _():
                    finish(i - 1, 1)
                    finish(i - 1, 0)

                return carry

            return lax.fori_loop(0, 2, one, carry)

        lax.fori_loop(0, 4, step, 0)

        def last(n, carry):
            finish(3 + lax.rem(n, 2), 1 - n // 2)
            return carry

        lax.fori_loop(0, 4, last, 0)

        wait_for(out, out_send)
        wait_for(total.at[:, pl.ds(1, 4)], total_send)
        for side in range(2):
            wait_for(pool.at[0, 0], zsend.at[side])
            wait_for(total.at[side, 0], part_send.at[side])

            @pl.when(has_high if side else has_low)
            def _():
                wait_for(pool.at[0, pl.ds(0, 5)], xsend.at[side])
                wait_for(edge.at[side], edge_send.at[side])

    pl.when(active)(work)

    for i, ref in enumerate((k_ref, v_ref, q_ref, g_ref)):
        wait_for(ref, send_sem.at[i])
    for i in range(WAVES):
        wait_for(flag_mine, flag_send.at[i])
    for i in range(2):
        wait_for(tokens.at[pl.ds(2 * i, 2)], token_sem.at[i])


def relay_kernel(tokens, a, b, c, d, held, load_sem, store_sem):
    loads = [pltpu.make_async_copy(tokens.at[i], held.at[i], load_sem.at[i]) for i in range(4)]
    stores = [pltpu.make_async_copy(held.at[i], ref, store_sem.at[i]) for i, ref in enumerate((a, b, c, d))]
    for copy in loads:
        copy.start()
    for load, store in zip(loads, stores):
        load.wait()
        store.start()
    for copy in stores:
        copy.wait()


def on_device(queries, keys, values, out_grad, window_lists, valid_counts):
    any_space = pl.BlockSpec(memory_space=pl.ANY)
    dma = pltpu.SemaphoreType.DMA
    row = (2, 2, 2 * TILE, HEAD_DIM)
    tokens = pl.pallas_call(
        kernel,
        out_shape=jax.ShapeDtypeStruct((4, TILE, D), BF16),
        in_specs=[any_space] * 4
        + [pl.BlockSpec(memory_space=pltpu.VMEM), pl.BlockSpec(memory_space=pltpu.SMEM)],
        out_specs=any_space,
        scratch_shapes=[
            pltpu.VMEM((4, 6) + row, BF16),
            pltpu.VMEM((2, 4, 2, TW * TILE, HEAD_DIM), BF16),
            pltpu.VMEM((2, 4, 2, TW * TILE, HEAD_DIM), BF16),
            pltpu.VMEM((4, 6) + row, F32),
            pltpu.VMEM((2, 5) + row, BF16),
            pltpu.VMEM((2, 5) + row, BF16),
            pltpu.VMEM((2,) + row, BF16),
            pltpu.VMEM((2, 5) + row, BF16),
            pltpu.VMEM((8, 128), F32),
            pltpu.VMEM((2, 2, 8, 128), F32),
            pltpu.VMEM((2, 128, KEYS), BF16),
            pltpu.VMEM((4, 6, 2, 128), F32),
            pltpu.VMEM((2, 4, 2, 4, KEYS), F32),
            dma((4,)), dma((2, 4)), dma((2, 4)), dma((WAVES,)), dma((2, 2)),
            dma((2,)), dma((2, 6)), dma((2,)), dma((2,)),
            dma, dma((2,)), dma((2,)), dma((2, 5)), dma((2,)), dma((2,)), dma,
        ],
        compiler_params=pltpu.CompilerParams(
            collective_id=0, has_side_effects=True, vmem_limit_bytes=56 * 1024 * 1024
        ),
        cost_estimate=pl.CostEstimate(flops=5_400_000_000, bytes_accessed=6_000_000, transcendentals=3_600_000),
        name="window_attention",
    )(queries, keys, values, out_grad, window_lists, valid_counts)

    return pl.pallas_call(
        relay_kernel,
        out_shape=(jax.ShapeDtypeStruct((TILE, D), BF16),) * 4,
        in_specs=[any_space],
        out_specs=(any_space,) * 4,
        scratch_shapes=[pltpu.VMEM((4, TILE, D), BF16), dma((4,)), dma((4,))],
        name="relay",
    )(tokens)


def solution(mesh):
    rows = P(("seq", "mp"), None)
    return jax.shard_map(
        on_device,
        mesh=mesh,
        in_specs=(rows, rows, rows, rows, P("seq", None), P()),
        out_specs=(rows, rows, rows, rows),
        check_vma=False,
    )
```

```python
import math

import jax
import jax.numpy as jnp
from jax import lax
from jax.experimental import pallas as pl
from jax.experimental.pallas import tpu as pltpu
from jax.sharding import PartitionSpec as P

HEADS = 24
HEAD_DIM = 128
D = HEADS * HEAD_DIM
TILE = 64
WINDOW = 27
TLAYERS = 8
NH = 8
TW = 4
TILES = TLAYERS * NH * TW
NX = 4
NZ = 8
NM = 8
WAVES = 3
KEYS = 9 * 2 * TILE
BIG = 1e30
SCALE = 1.0 / math.sqrt(HEAD_DIM)
EXP2_SCALE = SCALE / math.log(2.0)
MESH = pl.DeviceIdType.MESH
BF16 = jnp.bfloat16
F32 = jnp.float32


def place():
    seat = lax.axis_index("seq")
    m = lax.axis_index("mp")
    return seat // NZ, lax.rem(seat, NZ), m


def worker_z(part, m, wave):
    u = lax.rem(wave + m // 2, 2)
    v = lax.rem(m + wave // 2, 2)
    return jnp.where(part == 0, 3 - u + 4 * v, lax.rem(4 - 3 * u + 4 * v, NZ))


def work_of(z, m):
    zq = lax.rem(z, 4)
    zh = z // 4
    part = jnp.where(zq >= 2, 0, 1)
    u = jnp.where(part == 0, 3 - zq, zq)
    v = jnp.where(jnp.logical_and(part == 1, u == 0), 1 - zh, zh)
    same_v = v == lax.rem(m, 2)
    same_u = u == lax.rem(m // 2, 2)
    wave = jnp.where(same_u, jnp.where(same_v, 0, 2), 1)
    return part, wave, jnp.logical_or(same_u, same_v)


def greet(x, z, m, part, wave, active, two):
    barrier = pltpu.get_barrier_semaphore()

    def signal(seat, mm):
        pl.semaphore_signal(barrier, inc=1, device_id=(seat, mm), device_id_type=MESH)

    @pl.when(active)
    def _():
        def owner(d, carry):
            zz = 2 * part + lax.rem(d // NM, 2) + 4 * (d // (2 * NM))
            signal(x * NZ + zz, lax.rem(m + d, NM))
            return carry

        lax.fori_loop(0, 4 * NM, owner, 0)
        signal(x * NZ + worker_z(1 - part, m, wave), m)

        def border(d, carry):
            zz = 2 - part + 4 * (z // 4)
            mm = 4 * part + d

            @pl.when(jnp.logical_or(zz != z, mm != m))
            def _():
                signal(x * NZ + zz, mm)

            return carry

        lax.fori_loop(0, TW, border, 0)

        @pl.when(x > 0)
        def _():
            signal((x - 1) * NZ + z, m)

        @pl.when(x < NX - 1)
        def _():
            signal((x + 1) * NZ + z, m)

    near = 1 + jnp.where(x > 0, 1, 0) + jnp.where(x < NX - 1, 1, 0)
    others = jnp.where(two, jnp.where(active, HEADS // 2 - 1, HEADS // 2), 0)
    pl.semaphore_wait(barrier, HEADS + others + jnp.where(active, near, 0))


def wait_for(ref, sem):
    pltpu.make_async_copy(ref, ref, sem).wait()


def send(src, dst, send_sem, recv_sem, seat, m):
    pltpu.make_async_remote_copy(
        src_ref=src, dst_ref=dst, send_sem=send_sem, recv_sem=recv_sem,
        device_id=(seat, m), device_id_type=MESH,
    ).start()


def dot(a, b, dims):
    return lax.dot_general(a, b, (dims, ((), ())), preferred_element_type=F32)


def tile_rows(w):
    return pl.ds(pl.multiple_of(w * TILE, TILE), TILE)


def head_columns(head):
    return pl.ds(pl.multiple_of(head * HEAD_DIM, HEAD_DIM), HEAD_DIM)


def kernel(
    q_ref, k_ref, v_ref, g_ref, list_ref, count_ref,
    tokens,
    pool, qg, out, acc, edge, came, passed, total, flag_mine, flag_all, places, valid, bias,
    send_sem, kv_sem, qg_sem, flag_send, flag_sem, xsend, xsem, zsend, zsem,
    out_send, token_sem, edge_send, edge_sem, part_send, part_sem, total_send, border_send,
):
    x, z, m = place()
    zh = z // 4
    zl = lax.rem(z, 4)
    h = 2 * zl + m // 4
    w = lax.rem(m, 4)
    t = 2 * x + zh
    own = zl // 2
    part, wave, active = work_of(z, m)
    head = 3 * m + wave
    has_low = x > 0
    has_high = x < NX - 1
    low_seat = (x - 1) * NZ + z
    high_seat = (x + 1) * NZ + z
    other_z = worker_z(1 - part, m, wave)
    other_seat = x * NZ + other_z
    two = jnp.logical_or(h == 3, h == 4)

    spot = lax.broadcasted_iota(jnp.int32, (8, 128), 1)
    mine = lax.broadcasted_iota(jnp.int32, (8, 128), 0)
    near_t = t + spot // 12 - 1
    near_h = 2 * zl + mine // 4 + lax.rem(spot // 4, 3) - 1
    near = (near_t * NH + near_h) * TW + lax.rem(spot, 4)
    inside = (spot < 36) & (near_t >= 0) & (near_t < TLAYERS) & (near_h >= 0) & (near_h < NH)
    near = jnp.where(inside, near, -2)
    listed = jnp.zeros((8, 128), F32)
    for j in range(WINDOW):
        listed = jnp.where(list_ref[:, j : j + 1] == near, 1.0, listed)
    flag_mine[...] = listed
    pool[...] = jnp.zeros_like(pool)
    greet(x, z, m, part, wave, active, two)

    my_rows = tile_rows(lax.rem(w, 2))

    def send_kv(number, start, stop):
        def one(j, carry):
            wm = lax.rem(j + m + z, NM)
            seat = x * NZ + worker_z(own, wm, number)
            columns = head_columns(3 * wm + number)
            row = lax.rem(h, 4)
            for i, ref in ((0, k_ref), (1, v_ref)):
                send(
                    ref.at[:, columns], pool.at[1 + zh, 1 + row, i, w // 2, my_rows, :],
                    send_sem.at[i], kv_sem.at[zh, row], seat, wm,
                )

            oz = worker_z(1 - own, wm, number)
            near = jnp.logical_and(two, oz // 4 == zh)
            here = jnp.logical_and(oz == z, wm == m)
            border = [pool.at[1 + zh, jnp.where(own == 0, 0, 5), i, w // 2, my_rows, :] for i in range(2)]

            @pl.when(jnp.logical_and(near, jnp.logical_not(here)))
            def _():
                for i, ref in ((0, k_ref), (1, v_ref)):
                    send(ref.at[:, columns], border[i], border_send.at[i], zsem.at[zh], x * NZ + oz, wm)

            @pl.when(jnp.logical_and(near, here))
            def _():
                for i, ref in ((0, k_ref), (1, v_ref)):
                    pltpu.make_async_copy(ref.at[:, columns], border[i], zsem.at[zh]).start()

            return carry

        lax.fori_loop(start, stop, one, 0)

    def send_flags(number):
        send(
            flag_mine, flag_all.at[zh, lax.rem(zl, 2)],
            flag_send.at[number], flag_sem.at[zh, lax.rem(zl, 2)],
            x * NZ + worker_z(own, m, number), m,
        )

    def send_qg(number, start, stop):
        def one(j, carry):
            wm = lax.rem(j + m + z, NM)
            seat = x * NZ + worker_z(own, wm, number)
            columns = head_columns(3 * wm + number)
            row = lax.rem(h, 4)
            for i, ref in ((0, q_ref), (1, g_ref)):
                send(
                    ref.at[:, columns], qg.at[zh, row, i, tile_rows(w), :],
                    send_sem.at[2 + i], qg_sem.at[zh, row], seat, wm,
                )
            return carry

        lax.fori_loop(start, stop, one, 0)

    def row_of(i):
        return jnp.where(part == 0, 5 - i, i)

    def forward(i, carry):
        row = row_of(i)
        for side in range(2):
            @pl.when(i > 0)
            def _():
                wait_for(pool.at[1 + side, row], kv_sem.at[side, jnp.maximum(row, 1) - 1])

            @pl.when(i == 0)
            def _():
                wait_for(pool.at[1 + side, row], zsem.at[side])

            @pl.when(jnp.logical_and(i == 1, other_z // 4 != side))
            def _():
                send(
                    pool.at[1 + side, row], pool.at[1 + side, jnp.where(part == 0, 0, 5)],
                    zsend.at[side], zsem.at[side], other_seat, m,
                )

        @pl.when(has_low)
        def _():
            send(pool.at[1, row], pool.at[3, row], xsend.at[0], xsem.at[1, row], low_seat, m)

        @pl.when(has_high)
        def _():
            send(pool.at[2, row], pool.at[0, row], xsend.at[1], xsem.at[0, row], high_seat, m)

        return carry

    def forward_own(number):
        @pl.when(jnp.logical_and(active, wave == number))
        def _():
            lax.fori_loop(1, 5, forward, 0)

    def forward_other(number):
        @pl.when(jnp.logical_and(active, wave == number))
        def _():
            forward(0, 0)

    send_flags(0)
    send_kv(0, 0, 8)
    send_flags(1)
    send_kv(1, 0, 8)
    send_flags(2)
    send_kv(2, 0, 4)
    forward_own(0)
    send_kv(2, 4, 8)
    send_qg(0, 0, 4)
    forward_own(1)
    send_qg(0, 4, 8)
    forward_other(0)
    forward_own(2)
    send_qg(1, 0, 4)
    forward_other(1)
    send_qg(1, 4, 8)
    forward_other(2)
    send_qg(2, 0, 8)

    def work():
        acc[...] = jnp.zeros_like(acc)
        lane = lax.broadcasted_iota(jnp.int32, (1, 128), 1)

        def mark(i, carry):
            layer = i // 6
            row = lax.rem(i, 6)
            key_t = 2 * x - 1 + layer
            key_h = 4 * part - 1 + row
            real = (key_t >= 0) & (key_t < TLAYERS) & (key_h >= 0) & (key_h < NH)
            first = jnp.where(real, (key_t * NH + key_h) * TW, 0)
            for pair in range(2):
                counts = [jnp.where(real, count_ref[first + 2 * pair + j], 0) for j in range(2)]
                until = jnp.where(lane < TILE, counts[0], counts[1] + TILE)
                valid[layer, row, pair : pair + 1, :] = jnp.where(lane < until, 1.0, 0.0)
            return carry

        lax.fori_loop(0, 24, mark, 0)

        key = lax.broadcasted_iota(jnp.int32, (128, KEYS), 1)
        flag = lax.broadcasted_iota(jnp.int32, (128, KEYS), 0)
        for pair in range(2):
            wanted = key // 128 * 4 + pair * 2 + lax.rem(key, 128) // TILE
            places[pair] = jnp.where(wanted == flag, 1.0, 0.0).astype(BF16)

        def make_bias(layer, carry):
            for a in range(2):
                wait_for(flag_all.at[layer, a], flag_sem.at[layer, a])
            for pair in range(2):
                for r in range(4):
                    if r % 2 == 0:
                        live = dot(flag_all[layer, r // 2].astype(BF16), places[pair], ((1,), (0,)))
                    ok = jnp.concatenate(
                        [valid[layer + a, r + b, pair : pair + 1, :] for a in range(3) for b in range(3)], axis=1
                    )
                    tiles = live[(r % 2) * 4 : (r % 2) * 4 + 4]
                    bias[layer, r, pair, 0:4, :] = (tiles * ok - 1.0) * BIG
            return carry

        lax.fori_loop(0, 2, make_bias, 0)

        def arrive(i, carry):
            row = row_of(i)

            @pl.when(has_low)
            def _():
                wait_for(pool.at[0, row], xsem.at[0, row])

            @pl.when(has_high)
            def _():
                wait_for(pool.at[3, row], xsem.at[1, row])

            return carry

        lax.fori_loop(0, 5, arrive, 0)

        position = lax.broadcasted_iota(jnp.int32, (TILE, HEAD_DIM), 0)

        def strip(layer, r):
            wait_for(qg.at[layer, r], qg_sem.at[layer, r])
            tile0 = ((2 * x + layer) * NH + 4 * part + r) * TW
            token_ok = jnp.concatenate([position < count_ref[tile0 + j] for j in range(TW)], axis=0)
            q = qg[layer, r, 0]
            g = qg[layer, r, 1]
            g = jnp.where(token_ok, g.astype(F32), 0.0).astype(BF16)
            scores, keys, values = [], [], []
            for pair in range(2):
                rows = slice(pair * TILE, pair * TILE + 3 * TILE)
                key = [pool[layer + a, pl.ds(r, 3), 0, pair].reshape(384, HEAD_DIM) for a in range(3)]
                value = [pool[layer + a, pl.ds(r, 3), 1, pair].reshape(384, HEAD_DIM) for a in range(3)]
                keys.append(jnp.concatenate(key, axis=0))
                values.append(jnp.concatenate(value, axis=0))
                out_of = jnp.concatenate(
                    [
                        jnp.broadcast_to(bias[layer, r, pair, pair + j : pair + j + 1, :], (TILE, KEYS))
                        for j in range(3)
                    ],
                    axis=0,
                )
                scores.append(dot(q[rows], keys[pair], ((1,), (1,))) + out_of)
            tops = [jnp.max(sc, axis=1, keepdims=True) for sc in scores]
            middle = jnp.maximum(tops[0][TILE:], tops[1][: 2 * TILE])
            top0 = jnp.concatenate([tops[0][:TILE], middle], axis=0)
            top1 = jnp.concatenate([middle, tops[1][2 * TILE :]], axis=0)
            expo = [jnp.exp2((sc - top) * EXP2_SCALE) for sc, top in zip(scores, (top0, top1))]
            sums = [jnp.sum(e, axis=1, keepdims=True) for e in expo]
            middle = sums[0][TILE:] + sums[1][: 2 * TILE]
            inv0 = 1.0 / jnp.concatenate([sums[0][:TILE], middle], axis=0)
            inv1 = 1.0 / jnp.concatenate([middle, sums[1][2 * TILE :]], axis=0)
            probs = [expo[0] * inv0, expo[1] * inv1]
            low = [p.astype(BF16) for p in probs]

            def join(a, b):
                return jnp.concatenate([a[:TILE], a[TILE:] + b[: 2 * TILE], b[2 * TILE :]], axis=0)

            attended = join(*[dot(low[i], values[i], ((1,), (0,))) for i in range(2)])
            attended = jnp.where(token_ok, attended, 0.0).astype(BF16)
            out[layer, r, 0] = attended
            delta = jnp.sum(g.astype(F32) * attended.astype(F32), axis=1, keepdims=True)
            grads = []
            for pair in range(2):
                rows = slice(pair * TILE, pair * TILE + 3 * TILE)
                dprobs = dot(g[rows], values[pair], ((1,), (1,)))
                dscores = (probs[pair] * (dprobs - delta[rows])).astype(BF16)
                grads.append(dot(dscores, keys[pair], ((1,), (0,))))
                grad_k = dot(dscores, q[rows], ((0,), (0,))).reshape(3, 3, 2 * TILE, HEAD_DIM)
                grad_v = dot(low[pair], g[rows], ((0,), (0,))).reshape(3, 3, 2 * TILE, HEAD_DIM)
                for a in range(3):
                    acc[layer + a, pl.ds(r, 3), 0, pair] += grad_k[a]
                    acc[layer + a, pl.ds(r, 3), 1, pair] += grad_v[a]
            out[layer, r, 1] = (join(*grads) * SCALE).astype(BF16)

        columns = head_columns(head)

        def seat_of(layer, row):
            return x * NZ + layer * 4 + (4 * part + row) // 2, lax.rem(row, 2) * 4

        def send_strip(layer, r):
            seat, m0 = seat_of(layer, r)

            def send_tile(j, carry):
                send(
                    out.at[layer, r, :, tile_rows(j), :], tokens.at[pl.ds(0, 2), :, columns],
                    out_send, token_sem.at[0], seat, m0 + j,
                )
                return carry

            lax.fori_loop(0, TW, send_tile, 0)

        def scaled(layer, row, i):
            return acc[layer, row, i] * (SCALE if i == 0 else 1.0)

        def has(side):
            return jnp.where(side == 0, x, NX - 1 - x) > 0

        def send_edge(i, side):
            @pl.when(has(side))
            def _():
                for j in range(2):
                    edge[side, i, j] = scaled(3 * side, row_of(i), j).astype(BF16)
                send(
                    edge.at[side, i], came.at[1 - side, i], edge_send.at[side], edge_sem.at[1 - side, i],
                    jnp.where(side == 0, low_seat, high_seat), m,
                )

        def finish(i, side):
            row = row_of(i)

            @pl.when(has(side))
            def _():
                wait_for(came.at[side, i], edge_sem.at[side, i])
                for j in range(2):
                    total[side, i, j] = (scaled(1 + side, row, j) + came[side, i, j].astype(F32)).astype(BF16)

            @pl.when(jnp.logical_not(has(side)))
            def _():
                for j in range(2):
                    total[side, i, j] = scaled(1 + side, row, j).astype(BF16)

            @pl.when(i == 0)
            def _():
                send(
                    total.at[side, i], passed.at[side],
                    part_send.at[side], part_sem.at[side], other_seat, m,
                )

            @pl.when(i == 1)
            def _():
                wait_for(passed.at[side], part_sem.at[side])
                total[side, i] = (total[side, i].astype(F32) + passed[side].astype(F32)).astype(BF16)

            @pl.when(i > 0)
            def _():
                seat, m0 = seat_of(side, row - 1)

                def send_tile(j, carry):
                    send(
                        total.at[side, i, :, j // 2, tile_rows(lax.rem(j, 2)), :],
                        tokens.at[pl.ds(2, 2), :, columns],
                        total_send, token_sem.at[1], seat, m0 + j,
                    )
                    return carry

                lax.fori_loop(0, TW, send_tile, 0)

        def step(i, carry):
            r = jnp.where(part == 0, 3 - i, i)

            def one(layer, carry):
                strip(layer, r)
                send_strip(layer, r)
                send_edge(i, layer)

                @pl.when(i == 3)
                def _():
                    send_edge(4, layer)

                @pl.when(jnp.logical_and(i > 0, layer == 0))
                def _():
                    finish(i - 1, 1)
                    finish(i - 1, 0)

                return carry

            return lax.fori_loop(0, 2, one, carry)

        lax.fori_loop(0, 4, step, 0)

        def last(n, carry):
            finish(3 + lax.rem(n, 2), 1 - n // 2)
            return carry

        lax.fori_loop(0, 4, last, 0)

        wait_for(out, out_send)
        wait_for(total.at[:, pl.ds(1, 4)], total_send)
        for side in range(2):

            @pl.when(other_z // 4 != side)
            def _():
                wait_for(pool.at[0, 0], zsend.at[side])

            wait_for(total.at[side, 0], part_send.at[side])

            @pl.when(has_high if side else has_low)
            def _():
                wait_for(pool.at[0, pl.ds(0, 5)], xsend.at[side])
                wait_for(edge.at[side], edge_send.at[side])

    pl.when(active)(work)

    for i, ref in enumerate((k_ref, v_ref, q_ref, g_ref)):
        wait_for(ref, send_sem.at[i])
    for i, ref in enumerate((k_ref, v_ref)):
        @pl.when(jnp.logical_and(two, active))
        def _():
            wait_for(ref.at[:, : (HEADS // 2 - 1) * HEAD_DIM], border_send.at[i])

        @pl.when(jnp.logical_and(two, jnp.logical_not(active)))
        def _():
            wait_for(ref.at[:, : HEADS // 2 * HEAD_DIM], border_send.at[i])

    for i in range(WAVES):
        wait_for(flag_mine, flag_send.at[i])
    for i in range(2):
        wait_for(tokens.at[pl.ds(2 * i, 2)], token_sem.at[i])


def relay_kernel(tokens, a, b, c, d, held, load_sem, store_sem):
    loads = [pltpu.make_async_copy(tokens.at[i], held.at[i], load_sem.at[i]) for i in range(4)]
    stores = [pltpu.make_async_copy(held.at[i], ref, store_sem.at[i]) for i, ref in enumerate((a, b, c, d))]
    for copy in loads:
        copy.start()
    for load, store in zip(loads, stores):
        load.wait()
        store.start()
    for copy in stores:
        copy.wait()


def on_device(queries, keys, values, out_grad, window_lists, valid_counts):
    any_space = pl.BlockSpec(memory_space=pl.ANY)
    dma = pltpu.SemaphoreType.DMA
    row = (2, 2, 2 * TILE, HEAD_DIM)
    tokens = pl.pallas_call(
        kernel,
        out_shape=jax.ShapeDtypeStruct((4, TILE, D), BF16),
        in_specs=[any_space] * 4
        + [pl.BlockSpec(memory_space=pltpu.VMEM), pl.BlockSpec(memory_space=pltpu.SMEM)],
        out_specs=any_space,
        scratch_shapes=[
            pltpu.VMEM((4, 6) + row, BF16),
            pltpu.VMEM((2, 4, 2, TW * TILE, HEAD_DIM), BF16),
            pltpu.VMEM((2, 4, 2, TW * TILE, HEAD_DIM), BF16),
            pltpu.VMEM((4, 6) + row, F32),
            pltpu.VMEM((2, 5) + row, BF16),
            pltpu.VMEM((2, 5) + row, BF16),
            pltpu.VMEM((2,) + row, BF16),
            pltpu.VMEM((2, 5) + row, BF16),
            pltpu.VMEM((8, 128), F32),
            pltpu.VMEM((2, 2, 8, 128), F32),
            pltpu.VMEM((2, 128, KEYS), BF16),
            pltpu.VMEM((4, 6, 2, 128), F32),
            pltpu.VMEM((2, 4, 2, 4, KEYS), F32),
            dma((4,)), dma((2, 4)), dma((2, 4)), dma((WAVES,)), dma((2, 2)),
            dma((2,)), dma((2, 6)), dma((2,)), dma((2,)),
            dma, dma((2,)), dma((2,)), dma((2, 5)), dma((2,)), dma((2,)), dma, dma((2,)),
        ],
        compiler_params=pltpu.CompilerParams(
            collective_id=0, has_side_effects=True, vmem_limit_bytes=56 * 1024 * 1024
        ),
        cost_estimate=pl.CostEstimate(flops=5_400_000_000, bytes_accessed=6_000_000, transcendentals=3_600_000),
        name="window_attention",
    )(queries, keys, values, out_grad, window_lists, valid_counts)

    return pl.pallas_call(
        relay_kernel,
        out_shape=(jax.ShapeDtypeStruct((TILE, D), BF16),) * 4,
        in_specs=[any_space],
        out_specs=(any_space,) * 4,
        scratch_shapes=[pltpu.VMEM((4, TILE, D), BF16), dma((4,)), dma((4,))],
        name="relay",
    )(tokens)


def solution(mesh):
    rows = P(("seq", "mp"), None)
    return jax.shard_map(
        on_device,
        mesh=mesh,
        in_specs=(rows, rows, rows, rows, P("seq", None), P()),
        out_specs=(rows, rows, rows, rows),
        check_vma=False,
    )
```

```python
import math

import jax
import jax.numpy as jnp
from jax import lax
from jax.experimental import pallas as pl
from jax.experimental.pallas import tpu as pltpu
from jax.sharding import PartitionSpec as P

HEADS = 24
HEAD_DIM = 128
D = HEADS * HEAD_DIM
TILE = 64
WINDOW = 27
TLAYERS = 8
NH = 8
TW = 4
TILES = TLAYERS * NH * TW
NX = 4
NZ = 8
NM = 8
WAVES = 3
KEYS = 9 * 2 * TILE
BIG = 1e30
SCALE = 1.0 / math.sqrt(HEAD_DIM)
EXP2_SCALE = SCALE / math.log(2.0)
MESH = pl.DeviceIdType.MESH
BF16 = jnp.bfloat16
F32 = jnp.float32


def place():
    seat = lax.axis_index("seq")
    m = lax.axis_index("mp")
    return seat // NZ, lax.rem(seat, NZ), m


def worker_z(part, m, wave):
    u = lax.rem(wave + 1, 2)
    v = lax.rem(m + wave // 2, 2)
    return jnp.where(part == 0, 3 - u + 4 * v, lax.rem(4 - 3 * u + 4 * v, NZ))


def work_of(z, m):
    zq = lax.rem(z, 4)
    zh = z // 4
    part = jnp.where(zq >= 2, 0, 1)
    u = jnp.where(part == 0, 3 - zq, zq)
    v = jnp.where(jnp.logical_and(part == 1, u == 0), 1 - zh, zh)
    same_v = v == lax.rem(m, 2)
    same_u = u == 1
    wave = jnp.where(same_u, jnp.where(same_v, 0, 2), 1)
    return part, wave, jnp.logical_or(same_u, same_v)


def greet(x, z, m, part, wave, active, two):
    barrier = pltpu.get_barrier_semaphore()

    def signal(seat, mm):
        pl.semaphore_signal(barrier, inc=1, device_id=(seat, mm), device_id_type=MESH)

    @pl.when(active)
    def _():
        def owner(d, carry):
            zz = 2 * part + lax.rem(d // NM, 2) + 4 * (d // (2 * NM))
            signal(x * NZ + zz, lax.rem(m + d, NM))
            return carry

        lax.fori_loop(0, 4 * NM, owner, 0)
        signal(x * NZ + worker_z(1 - part, m, wave), m)

        def border(d, carry):
            zz = 2 - part + 4 * (z // 4)
            mm = 4 * part + d

            @pl.when(jnp.logical_or(zz != z, mm != m))
            def _():
                signal(x * NZ + zz, mm)

            return carry

        lax.fori_loop(0, TW, border, 0)

        @pl.when(x > 0)
        def _():
            signal((x - 1) * NZ + z, m)

        @pl.when(x < NX - 1)
        def _():
            signal((x + 1) * NZ + z, m)

    near = 1 + jnp.where(x > 0, 1, 0) + jnp.where(x < NX - 1, 1, 0)
    others = jnp.where(two, jnp.where(active, HEADS // 2 - 1, HEADS // 2), 0)
    pl.semaphore_wait(barrier, HEADS + others + jnp.where(active, near, 0))


def wait_for(ref, sem):
    pltpu.make_async_copy(ref, ref, sem).wait()


def send(src, dst, send_sem, recv_sem, seat, m):
    pltpu.make_async_remote_copy(
        src_ref=src, dst_ref=dst, send_sem=send_sem, recv_sem=recv_sem,
        device_id=(seat, m), device_id_type=MESH,
    ).start()


def dot(a, b, dims):
    return lax.dot_general(a, b, (dims, ((), ())), preferred_element_type=F32)


def tile_rows(w):
    return pl.ds(pl.multiple_of(w * TILE, TILE), TILE)


def head_columns(head):
    return pl.ds(pl.multiple_of(head * HEAD_DIM, HEAD_DIM), HEAD_DIM)


def kernel(
    q_ref, k_ref, v_ref, g_ref, list_ref, count_ref,
    tokens, extra,
    pool, qg, out, acc, edge, came, passed, total, flag_mine, flag_all, places, valid, bias,
    send_sem, kv_sem, qg_sem, flag_send, flag_sem, xsend, xsem, zsend, zsem,
    out_send, token_sem, edge_send, edge_sem, part_send, part_sem, total_send, border_send, near_send, extra_sem,
):
    x, z, m = place()
    zh = z // 4
    zl = lax.rem(z, 4)
    h = 2 * zl + m // 4
    w = lax.rem(m, 4)
    t = 2 * x + zh
    own = zl // 2
    part, wave, active = work_of(z, m)
    head = 3 * m + wave
    has_low = x > 0
    has_high = x < NX - 1
    low_seat = (x - 1) * NZ + z
    high_seat = (x + 1) * NZ + z
    other_z = worker_z(1 - part, m, wave)
    other_seat = x * NZ + other_z
    two = jnp.logical_or(h == 3, h == 4)

    spot = lax.broadcasted_iota(jnp.int32, (8, 128), 1)
    mine = lax.broadcasted_iota(jnp.int32, (8, 128), 0)
    near_t = t + spot // 12 - 1
    near_h = 2 * zl + mine // 4 + lax.rem(spot // 4, 3) - 1
    near = (near_t * NH + near_h) * TW + lax.rem(spot, 4)
    inside = (spot < 36) & (near_t >= 0) & (near_t < TLAYERS) & (near_h >= 0) & (near_h < NH)
    near = jnp.where(inside, near, -2)
    listed = jnp.zeros((8, 128), F32)
    for j in range(WINDOW):
        listed = jnp.where(list_ref[:, j : j + 1] == near, 1.0, listed)
    flag_mine[...] = listed
    pool[...] = jnp.zeros_like(pool)
    greet(x, z, m, part, wave, active, two)

    my_rows = tile_rows(lax.rem(w, 2))

    def send_kv(number, start, stop):
        def one(j, carry):
            wm = lax.rem(j + m + z, NM)
            seat = x * NZ + worker_z(own, wm, number)
            columns = head_columns(3 * wm + number)
            row = lax.rem(h, 4)
            for i, ref in ((0, k_ref), (1, v_ref)):
                send(
                    ref.at[:, columns], pool.at[1 + zh, 1 + row, i, w // 2, my_rows, :],
                    send_sem.at[i], kv_sem.at[zh, row], seat, wm,
                )

            oz = worker_z(1 - own, wm, number)
            near = jnp.logical_and(two, oz // 4 == zh)
            here = jnp.logical_and(oz == z, wm == m)
            border = [pool.at[1 + zh, jnp.where(own == 0, 0, 5), i, w // 2, my_rows, :] for i in range(2)]

            @pl.when(jnp.logical_and(near, jnp.logical_not(here)))
            def _():
                for i, ref in ((0, k_ref), (1, v_ref)):
                    send(ref.at[:, columns], border[i], border_send.at[i], zsem.at[zh], x * NZ + oz, wm)

            @pl.when(jnp.logical_and(near, here))
            def _():
                for i, ref in ((0, k_ref), (1, v_ref)):
                    pltpu.make_async_copy(ref.at[:, columns], border[i], zsem.at[zh]).start()

            return carry

        lax.fori_loop(start, stop, one, 0)

    def send_flags(number):
        send(
            flag_mine, flag_all.at[zh, lax.rem(zl, 2)],
            flag_send.at[number], flag_sem.at[zh, lax.rem(zl, 2)],
            x * NZ + worker_z(own, m, number), m,
        )

    def send_qg(number, start, stop):
        def one(j, carry):
            wm = lax.rem(j + m + z, NM)
            seat = x * NZ + worker_z(own, wm, number)
            columns = head_columns(3 * wm + number)
            row = lax.rem(h, 4)
            for i, ref in ((0, q_ref), (1, g_ref)):
                send(
                    ref.at[:, columns], qg.at[zh, row, i, tile_rows(w), :],
                    send_sem.at[2 + i], qg_sem.at[zh, row], seat, wm,
                )
            return carry

        lax.fori_loop(start, stop, one, 0)

    def row_of(i):
        return jnp.where(part == 0, 5 - i, i)

    def forward(i, carry):
        row = row_of(i)
        for side in range(2):
            @pl.when(i > 0)
            def _():
                wait_for(pool.at[1 + side, row], kv_sem.at[side, jnp.maximum(row, 1) - 1])

            @pl.when(i == 0)
            def _():
                wait_for(pool.at[1 + side, row], zsem.at[side])

            @pl.when(jnp.logical_and(i == 1, other_z // 4 != side))
            def _():
                send(
                    pool.at[1 + side, row], pool.at[1 + side, jnp.where(part == 0, 0, 5)],
                    zsend.at[side], zsem.at[side], other_seat, m,
                )

        @pl.when(has_low)
        def _():
            send(pool.at[1, row], pool.at[3, row], xsend.at[0], xsem.at[1, row], low_seat, m)

        @pl.when(has_high)
        def _():
            send(pool.at[2, row], pool.at[0, row], xsend.at[1], xsem.at[0, row], high_seat, m)

        return carry

    def forward_own(number):
        @pl.when(jnp.logical_and(active, wave == number))
        def _():
            lax.fori_loop(1, 5, forward, 0)

    def forward_other(number):
        @pl.when(jnp.logical_and(active, wave == number))
        def _():
            forward(0, 0)

    send_flags(0)
    send_kv(0, 0, 8)
    send_flags(1)
    send_kv(1, 0, 8)
    send_flags(2)
    send_kv(2, 0, 4)
    forward_own(0)
    send_kv(2, 4, 8)
    send_qg(0, 0, 4)
    forward_own(1)
    send_qg(0, 4, 8)
    forward_other(0)
    forward_own(2)
    send_qg(1, 0, 4)
    forward_other(1)
    send_qg(1, 4, 8)
    forward_other(2)
    send_qg(2, 0, 8)

    def work():
        acc[...] = jnp.zeros_like(acc)
        lane = lax.broadcasted_iota(jnp.int32, (1, 128), 1)

        def mark(i, carry):
            layer = i // 6
            row = lax.rem(i, 6)
            key_t = 2 * x - 1 + layer
            key_h = 4 * part - 1 + row
            real = (key_t >= 0) & (key_t < TLAYERS) & (key_h >= 0) & (key_h < NH)
            first = jnp.where(real, (key_t * NH + key_h) * TW, 0)
            for pair in range(2):
                counts = [jnp.where(real, count_ref[first + 2 * pair + j], 0) for j in range(2)]
                until = jnp.where(lane < TILE, counts[0], counts[1] + TILE)
                valid[layer, row, pair : pair + 1, :] = jnp.where(lane < until, 1.0, 0.0)
            return carry

        lax.fori_loop(0, 24, mark, 0)

        key = lax.broadcasted_iota(jnp.int32, (128, KEYS), 1)
        flag = lax.broadcasted_iota(jnp.int32, (128, KEYS), 0)
        for pair in range(2):
            wanted = key // 128 * 4 + pair * 2 + lax.rem(key, 128) // TILE
            places[pair] = jnp.where(wanted == flag, 1.0, 0.0).astype(BF16)

        def make_bias(layer, carry):
            for a in range(2):
                wait_for(flag_all.at[layer, a], flag_sem.at[layer, a])
            for pair in range(2):
                for r in range(4):
                    if r % 2 == 0:
                        live = dot(flag_all[layer, r // 2].astype(BF16), places[pair], ((1,), (0,)))
                    ok = jnp.concatenate(
                        [valid[layer + a, r + b, pair : pair + 1, :] for a in range(3) for b in range(3)], axis=1
                    )
                    tiles = live[(r % 2) * 4 : (r % 2) * 4 + 4]
                    bias[layer, r, pair, 0:4, :] = (tiles * ok - 1.0) * BIG
            return carry

        lax.fori_loop(0, 2, make_bias, 0)

        def arrive(i, carry):
            row = row_of(i)

            @pl.when(has_low)
            def _():
                wait_for(pool.at[0, row], xsem.at[0, row])

            @pl.when(has_high)
            def _():
                wait_for(pool.at[3, row], xsem.at[1, row])

            return carry

        lax.fori_loop(0, 5, arrive, 0)

        position = lax.broadcasted_iota(jnp.int32, (TILE, HEAD_DIM), 0)

        def strip(layer, r):
            wait_for(qg.at[layer, r], qg_sem.at[layer, r])
            tile0 = ((2 * x + layer) * NH + 4 * part + r) * TW
            token_ok = jnp.concatenate([position < count_ref[tile0 + j] for j in range(TW)], axis=0)
            q = qg[layer, r, 0]
            g = qg[layer, r, 1]
            g = jnp.where(token_ok, g.astype(F32), 0.0).astype(BF16)
            scores, keys, values = [], [], []
            for pair in range(2):
                rows = slice(pair * TILE, pair * TILE + 3 * TILE)
                key = [pool[layer + a, pl.ds(r, 3), 0, pair].reshape(384, HEAD_DIM) for a in range(3)]
                value = [pool[layer + a, pl.ds(r, 3), 1, pair].reshape(384, HEAD_DIM) for a in range(3)]
                keys.append(jnp.concatenate(key, axis=0))
                values.append(jnp.concatenate(value, axis=0))
                out_of = jnp.concatenate(
                    [
                        jnp.broadcast_to(bias[layer, r, pair, pair + j : pair + j + 1, :], (TILE, KEYS))
                        for j in range(3)
                    ],
                    axis=0,
                )
                scores.append(dot(q[rows], keys[pair], ((1,), (1,))) + out_of)
            tops = [jnp.max(sc, axis=1, keepdims=True) for sc in scores]
            middle = jnp.maximum(tops[0][TILE:], tops[1][: 2 * TILE])
            top0 = jnp.concatenate([tops[0][:TILE], middle], axis=0)
            top1 = jnp.concatenate([middle, tops[1][2 * TILE :]], axis=0)
            expo = [jnp.exp2((sc - top) * EXP2_SCALE) for sc, top in zip(scores, (top0, top1))]
            sums = [jnp.sum(e, axis=1, keepdims=True) for e in expo]
            middle = sums[0][TILE:] + sums[1][: 2 * TILE]
            inv0 = 1.0 / jnp.concatenate([sums[0][:TILE], middle], axis=0)
            inv1 = 1.0 / jnp.concatenate([middle, sums[1][2 * TILE :]], axis=0)
            probs = [expo[0] * inv0, expo[1] * inv1]
            low = [p.astype(BF16) for p in probs]

            def join(a, b):
                return jnp.concatenate([a[:TILE], a[TILE:] + b[: 2 * TILE], b[2 * TILE :]], axis=0)

            attended = join(*[dot(low[i], values[i], ((1,), (0,))) for i in range(2)])
            attended = jnp.where(token_ok, attended, 0.0).astype(BF16)
            out[layer, r, 0] = attended
            delta = jnp.sum(g.astype(F32) * attended.astype(F32), axis=1, keepdims=True)
            grads = []
            for pair in range(2):
                rows = slice(pair * TILE, pair * TILE + 3 * TILE)
                dprobs = dot(g[rows], values[pair], ((1,), (1,)))
                dscores = (probs[pair] * (dprobs - delta[rows])).astype(BF16)
                grads.append(dot(dscores, keys[pair], ((1,), (0,))))
                grad_k = dot(dscores, q[rows], ((0,), (0,))).reshape(3, 3, 2 * TILE, HEAD_DIM)
                grad_v = dot(low[pair], g[rows], ((0,), (0,))).reshape(3, 3, 2 * TILE, HEAD_DIM)
                for a in range(3):
                    acc[layer + a, pl.ds(r, 3), 0, pair] += grad_k[a]
                    acc[layer + a, pl.ds(r, 3), 1, pair] += grad_v[a]
            out[layer, r, 1] = (join(*grads) * SCALE).astype(BF16)

        columns = head_columns(head)

        def seat_of(layer, row):
            there = 4 * part + row
            return x * NZ + layer * 4 + there // 2, lax.rem(there, 2) * 4

        def send_strip(layer, r):
            seat, m0 = seat_of(layer, r)

            def send_tile(j, carry):
                send(
                    out.at[layer, r, :, tile_rows(j), :], tokens.at[pl.ds(0, 2), :, columns],
                    out_send, token_sem.at[0], seat, m0 + j,
                )
                return carry

            lax.fori_loop(0, TW, send_tile, 0)

        def scaled(layer, row, i):
            return acc[layer, row, i] * (SCALE if i == 0 else 1.0)

        def has(side):
            return jnp.where(side == 0, x, NX - 1 - x) > 0

        def send_edge(i, side):
            @pl.when(has(side))
            def _():
                for j in range(2):
                    edge[side, i, j] = scaled(3 * side, row_of(i), j).astype(BF16)
                send(
                    edge.at[side, i], came.at[1 - side, i], edge_send.at[side], edge_sem.at[1 - side, i],
                    jnp.where(side == 0, low_seat, high_seat), m,
                )

        def finish(i, side):
            row = row_of(i)

            @pl.when(has(side))
            def _():
                wait_for(came.at[side, i], edge_sem.at[side, i])
                for j in range(2):
                    total[side, i, j] = (scaled(1 + side, row, j) + came[side, i, j].astype(F32)).astype(BF16)

            @pl.when(jnp.logical_not(has(side)))
            def _():
                for j in range(2):
                    total[side, i, j] = scaled(1 + side, row, j).astype(BF16)

            @pl.when(jnp.logical_and(i == 0, side == z // 4))
            def _():
                seat, m0 = seat_of(side, row - 1)

                def send_tile(j, carry):
                    src = total.at[side, i, :, j // 2, tile_rows(lax.rem(j, 2)), :]
                    dst = extra.at[:, :, columns]
                    here = jnp.logical_and(two, m0 + j == m)

                    @pl.when(here)
                    def _():
                        pltpu.make_async_copy(src, dst, extra_sem).start()

                    @pl.when(jnp.logical_not(here))
                    def _():
                        send(src, dst, near_send, extra_sem, seat, m0 + j)

                    return carry

                lax.fori_loop(0, TW, send_tile, 0)

            @pl.when(jnp.logical_and(i == 0, side != z // 4))
            def _():
                send(
                    total.at[side, i], passed.at[side],
                    part_send.at[side], part_sem.at[side], other_seat, m,
                )

            @pl.when(jnp.logical_and(i == 1, side != other_z // 4))
            def _():
                wait_for(passed.at[side], part_sem.at[side])
                total[side, i] = (total[side, i].astype(F32) + passed[side].astype(F32)).astype(BF16)

            @pl.when(i > 0)
            def _():
                seat, m0 = seat_of(side, row - 1)

                def send_tile(j, carry):
                    send(
                        total.at[side, i, :, j // 2, tile_rows(lax.rem(j, 2)), :],
                        tokens.at[pl.ds(2, 2), :, columns],
                        total_send, token_sem.at[1], seat, m0 + j,
                    )
                    return carry

                lax.fori_loop(0, TW, send_tile, 0)

        def step(i, carry):
            r = jnp.where(part == 0, 3 - i, i)

            def one(layer, carry):
                strip(layer, r)
                send_strip(layer, r)
                send_edge(i, layer)

                @pl.when(i == 3)
                def _():
                    send_edge(4, layer)

                @pl.when(jnp.logical_and(i > 0, layer == 0))
                def _():
                    finish(i - 1, 1)
                    finish(i - 1, 0)

                return carry

            return lax.fori_loop(0, 2, one, carry)

        lax.fori_loop(0, 4, step, 0)

        def last(n, carry):
            finish(3 + lax.rem(n, 2), 1 - n // 2)
            return carry

        lax.fori_loop(0, 4, last, 0)

        @pl.when(two)
        def _():
            wait_for(out.at[0, 0, :, pl.ds(0, 3 * TILE), :], near_send)

        @pl.when(jnp.logical_not(two))
        def _():
            wait_for(out.at[0, 0], near_send)

        wait_for(out, out_send)
        wait_for(total.at[:, pl.ds(1, 4)], total_send)
        for side in range(2):

            @pl.when(other_z // 4 != side)
            def _():
                wait_for(pool.at[0, 0], zsend.at[side])


            @pl.when(z // 4 != side)
            def _():
                wait_for(total.at[side, 0], part_send.at[side])


            @pl.when(has_high if side else has_low)
            def _():
                wait_for(pool.at[0, pl.ds(0, 5)], xsend.at[side])
                wait_for(edge.at[side], edge_send.at[side])

    pl.when(active)(work)

    for i, ref in enumerate((k_ref, v_ref, q_ref, g_ref)):
        wait_for(ref, send_sem.at[i])
    for i, ref in enumerate((k_ref, v_ref)):
        @pl.when(jnp.logical_and(two, active))
        def _():
            wait_for(ref.at[:, : (HEADS // 2 - 1) * HEAD_DIM], border_send.at[i])

        @pl.when(jnp.logical_and(two, jnp.logical_not(active)))
        def _():
            wait_for(ref.at[:, : HEADS // 2 * HEAD_DIM], border_send.at[i])

    for i in range(WAVES):
        wait_for(flag_mine, flag_send.at[i])
    for i in range(2):
        wait_for(tokens.at[pl.ds(2 * i, 2)], token_sem.at[i])

    @pl.when(two)
    def _():
        wait_for(extra.at[:, :, : HEADS // 2 * HEAD_DIM], extra_sem)


def relay_kernel(tokens, extra, a, b, c, d, held, more, load_sem, more_sem, store_sem):
    x, z, m = place()
    h = 2 * lax.rem(z, 4) + m // 4
    two = jnp.logical_or(h == 3, h == 4)
    loads = [pltpu.make_async_copy(tokens.at[i], held.at[i], load_sem.at[i]) for i in range(4)]
    stores = [pltpu.make_async_copy(held.at[i], ref, store_sem.at[i]) for i, ref in enumerate((a, b, c, d))]
    extras = pltpu.make_async_copy(extra, more, more_sem)

    @pl.when(two)
    def _():
        extras.start()

    for copy in loads[2:] + loads[:2]:
        copy.start()
    for i in (2, 3):
        loads[i].wait()

    @pl.when(two)
    def _():
        extras.wait()
        for head in range(HEADS):
            columns = slice(head * HEAD_DIM, (head + 1) * HEAD_DIM)

            @pl.when(worker_z(jnp.where(h == 4, 0, 1), head // 3, head % 3) // 4 == z // 4)
            def _():
                both = held[2:, :, columns].astype(F32) + more[:, :, columns].astype(F32)
                held[2:, :, columns] = both.astype(BF16)

    for i in (2, 3):
        stores[i].start()
    for i in (0, 1):
        loads[i].wait()
        stores[i].start()
    for copy in stores:
        copy.wait()


def on_device(queries, keys, values, out_grad, window_lists, valid_counts):
    any_space = pl.BlockSpec(memory_space=pl.ANY)
    dma = pltpu.SemaphoreType.DMA
    row = (2, 2, 2 * TILE, HEAD_DIM)
    tokens, extra = pl.pallas_call(
        kernel,
        out_shape=(jax.ShapeDtypeStruct((4, TILE, D), BF16), jax.ShapeDtypeStruct((2, TILE, D), BF16)),
        in_specs=[any_space] * 4
        + [pl.BlockSpec(memory_space=pltpu.VMEM), pl.BlockSpec(memory_space=pltpu.SMEM)],
        out_specs=(any_space,) * 2,
        scratch_shapes=[
            pltpu.VMEM((4, 6) + row, BF16),
            pltpu.VMEM((2, 4, 2, TW * TILE, HEAD_DIM), BF16),
            pltpu.VMEM((2, 4, 2, TW * TILE, HEAD_DIM), BF16),
            pltpu.VMEM((4, 6) + row, F32),
            pltpu.VMEM((2, 5) + row, BF16),
            pltpu.VMEM((2, 5) + row, BF16),
            pltpu.VMEM((2,) + row, BF16),
            pltpu.VMEM((2, 5) + row, BF16),
            pltpu.VMEM((8, 128), F32),
            pltpu.VMEM((2, 2, 8, 128), F32),
            pltpu.VMEM((2, 128, KEYS), BF16),
            pltpu.VMEM((4, 6, 2, 128), F32),
            pltpu.VMEM((2, 4, 2, 4, KEYS), F32),
            dma((4,)), dma((2, 4)), dma((2, 4)), dma((WAVES,)), dma((2, 2)),
            dma((2,)), dma((2, 6)), dma((2,)), dma((2,)),
            dma, dma((2,)), dma((2,)), dma((2, 5)), dma((2,)), dma((2,)), dma, dma((2,)),
            dma, dma,
        ],
        compiler_params=pltpu.CompilerParams(
            collective_id=0, has_side_effects=True, vmem_limit_bytes=56 * 1024 * 1024
        ),
        cost_estimate=pl.CostEstimate(flops=5_400_000_000, bytes_accessed=6_000_000, transcendentals=3_600_000),
        name="window_attention",
    )(queries, keys, values, out_grad, window_lists, valid_counts)

    return pl.pallas_call(
        relay_kernel,
        out_shape=(jax.ShapeDtypeStruct((TILE, D), BF16),) * 4,
        in_specs=[any_space] * 2,
        out_specs=(any_space,) * 4,
        scratch_shapes=[
            pltpu.VMEM((4, TILE, D), BF16), pltpu.VMEM((2, TILE, D), BF16), dma((4,)), dma, dma((4,)),
        ],
        name="relay",
    )(tokens, extra)


def solution(mesh):
    rows = P(("seq", "mp"), None)
    return jax.shard_map(
        on_device,
        mesh=mesh,
        in_specs=(rows, rows, rows, rows, P("seq", None), P()),
        out_specs=(rows, rows, rows, rows),
        check_vma=False,
    )
```

```python
import math

import jax
import jax.numpy as jnp
from jax import lax
from jax.experimental import pallas as pl
from jax.experimental.pallas import tpu as pltpu
from jax.sharding import PartitionSpec as P

HEADS = 24
HEAD_DIM = 128
D = HEADS * HEAD_DIM
TILE = 64
WINDOW = 27
TLAYERS = 8
NH = 8
TW = 4
TILES = TLAYERS * NH * TW
NX = 4
NZ = 8
NM = 8
WAVES = 3
KEYS = 9 * 2 * TILE
BIG = 1e30
SCALE = 1.0 / math.sqrt(HEAD_DIM)
EXP2_SCALE = SCALE / math.log(2.0)
MESH = pl.DeviceIdType.MESH
BF16 = jnp.bfloat16
F32 = jnp.float32


def place():
    seat = lax.axis_index("seq")
    m = lax.axis_index("mp")
    return seat // NZ, lax.rem(seat, NZ), m


def worker_z(part, m, wave):
    u = lax.rem(wave + 1, 2)
    v = lax.rem(m + wave // 2, 2)
    return jnp.where(part == 0, 3 - u + 4 * v, lax.rem(4 - 3 * u + 4 * v, NZ))


def work_of(z, m):
    zq = lax.rem(z, 4)
    zh = z // 4
    part = jnp.where(zq >= 2, 0, 1)
    u = jnp.where(part == 0, 3 - zq, zq)
    v = jnp.where(jnp.logical_and(part == 1, u == 0), 1 - zh, zh)
    same_v = v == lax.rem(m, 2)
    same_u = u == 1
    wave = jnp.where(same_u, jnp.where(same_v, 0, 2), 1)
    return part, wave, jnp.logical_or(same_u, same_v)


def greet(x, z, m, part, wave, active, two):
    barrier = pltpu.get_barrier_semaphore()

    def signal(seat, mm):
        pl.semaphore_signal(barrier, inc=1, device_id=(seat, mm), device_id_type=MESH)

    @pl.when(active)
    def _():
        def owner(d, carry):
            zz = 2 * part + lax.rem(d // NM, 2) + 4 * (d // (2 * NM))
            signal(x * NZ + zz, lax.rem(m + d, NM))
            return carry

        lax.fori_loop(0, 4 * NM, owner, 0)
        signal(x * NZ + worker_z(1 - part, m, wave), m)

        def border(d, carry):
            zz = 2 - part + 4 * (z // 4)
            mm = 4 * part + d

            @pl.when(jnp.logical_or(zz != z, mm != m))
            def _():
                signal(x * NZ + zz, mm)

            return carry

        lax.fori_loop(0, TW, border, 0)

        @pl.when(x > 0)
        def _():
            signal((x - 1) * NZ + z, m)

        @pl.when(x < NX - 1)
        def _():
            signal((x + 1) * NZ + z, m)

    near = 1 + jnp.where(x > 0, 1, 0) + jnp.where(x < NX - 1, 1, 0)
    others = jnp.where(two, jnp.where(active, HEADS // 2 - 1, HEADS // 2), 0)
    pl.semaphore_wait(barrier, HEADS + others + jnp.where(active, near, 0))


def wait_for(ref, sem):
    pltpu.make_async_copy(ref, ref, sem).wait()


def send(src, dst, send_sem, recv_sem, seat, m):
    pltpu.make_async_remote_copy(
        src_ref=src, dst_ref=dst, send_sem=send_sem, recv_sem=recv_sem,
        device_id=(seat, m), device_id_type=MESH,
    ).start()


def dot(a, b, dims):
    return lax.dot_general(a, b, (dims, ((), ())), preferred_element_type=F32)


def tile_rows(w):
    return pl.ds(pl.multiple_of(w * TILE, TILE), TILE)


def head_columns(head):
    return pl.ds(pl.multiple_of(head * HEAD_DIM, HEAD_DIM), HEAD_DIM)


def kernel(
    q_ref, k_ref, v_ref, g_ref, list_ref, count_ref,
    tokens, extra,
    pool, qg, out, acc, edge, came, passed, total, flag_mine, flag_all, places, valid, bias,
    send_sem, kv_sem, qg_sem, flag_send, flag_sem, xsend, xsem, zsend, zsem,
    out_send, token_sem, edge_send, edge_sem, part_send, part_sem, total_send, border_send, near_send, extra_sem,
):
    x, z, m = place()
    zh = z // 4
    zl = lax.rem(z, 4)
    h = 2 * zl + m // 4
    w = lax.rem(m, 4)
    t = 2 * x + zh
    own = zl // 2
    part, wave, active = work_of(z, m)
    head = 3 * m + wave
    has_low = x > 0
    has_high = x < NX - 1
    low_seat = (x - 1) * NZ + z
    high_seat = (x + 1) * NZ + z
    other_z = worker_z(1 - part, m, wave)
    other_seat = x * NZ + other_z
    two = jnp.logical_or(h == 3, h == 4)

    spot = lax.broadcasted_iota(jnp.int32, (8, 128), 1)
    mine = lax.broadcasted_iota(jnp.int32, (8, 128), 0)
    near_t = t + spot // 12 - 1
    near_h = 2 * zl + mine // 4 + lax.rem(spot // 4, 3) - 1
    near = (near_t * NH + near_h) * TW + lax.rem(spot, 4)
    inside = (spot < 36) & (near_t >= 0) & (near_t < TLAYERS) & (near_h >= 0) & (near_h < NH)
    near = jnp.where(inside, near, -2)
    listed = jnp.zeros((8, 128), F32)
    for j in range(WINDOW):
        listed = jnp.where(list_ref[:, j : j + 1] == near, 1.0, listed)
    flag_mine[...] = listed
    pool[...] = jnp.zeros_like(pool)
    greet(x, z, m, part, wave, active, two)

    my_rows = tile_rows(lax.rem(w, 2))

    def send_kv(number, start, stop):
        def one(j, carry):
            wm = lax.rem(j + m + z, NM)
            seat = x * NZ + worker_z(own, wm, number)
            columns = head_columns(3 * wm + number)
            row = lax.rem(h, 4)
            for i, ref in ((0, k_ref), (1, v_ref)):
                send(
                    ref.at[:, columns], pool.at[1 + zh, 1 + row, i, w // 2, my_rows, :],
                    send_sem.at[i], kv_sem.at[zh, row], seat, wm,
                )

            oz = worker_z(1 - own, wm, number)
            near = jnp.logical_and(two, oz // 4 == zh)
            here = jnp.logical_and(oz == z, wm == m)
            border = [pool.at[1 + zh, jnp.where(own == 0, 0, 5), i, w // 2, my_rows, :] for i in range(2)]

            @pl.when(jnp.logical_and(near, jnp.logical_not(here)))
            def _():
                for i, ref in ((0, k_ref), (1, v_ref)):
                    send(ref.at[:, columns], border[i], border_send.at[i], zsem.at[zh], x * NZ + oz, wm)

            @pl.when(jnp.logical_and(near, here))
            def _():
                for i, ref in ((0, k_ref), (1, v_ref)):
                    pltpu.make_async_copy(ref.at[:, columns], border[i], zsem.at[zh]).start()

            return carry

        lax.fori_loop(start, stop, one, 0)

    def send_flags(number):
        send(
            flag_mine, flag_all.at[zh, lax.rem(zl, 2)],
            flag_send.at[number], flag_sem.at[zh, lax.rem(zl, 2)],
            x * NZ + worker_z(own, m, number), m,
        )

    def send_qg(number, start, stop):
        def one(j, carry):
            wm = lax.rem(j + m + z, NM)
            seat = x * NZ + worker_z(own, wm, number)
            columns = head_columns(3 * wm + number)
            row = lax.rem(h, 4)
            for i, ref in ((0, q_ref), (1, g_ref)):
                send(
                    ref.at[:, columns], qg.at[zh, row, i, tile_rows(w), :],
                    send_sem.at[2 + i], qg_sem.at[zh, row], seat, wm,
                )
            return carry

        lax.fori_loop(start, stop, one, 0)

    def row_of(i):
        return jnp.where(part == 0, 5 - i, i)

    def forward(i, carry):
        row = row_of(i)
        for side in range(2):
            @pl.when(i > 0)
            def _():
                wait_for(pool.at[1 + side, row], kv_sem.at[side, jnp.maximum(row, 1) - 1])

            @pl.when(i == 0)
            def _():
                wait_for(pool.at[1 + side, row], zsem.at[side])

            @pl.when(jnp.logical_and(i == 1, other_z // 4 != side))
            def _():
                send(
                    pool.at[1 + side, row], pool.at[1 + side, jnp.where(part == 0, 0, 5)],
                    zsend.at[side], zsem.at[side], other_seat, m,
                )

        @pl.when(has_low)
        def _():
            send(pool.at[1, row], pool.at[3, row], xsend.at[0], xsem.at[1, row], low_seat, m)

        @pl.when(has_high)
        def _():
            send(pool.at[2, row], pool.at[0, row], xsend.at[1], xsem.at[0, row], high_seat, m)

        return carry

    def forward_own(number):
        @pl.when(jnp.logical_and(active, wave == number))
        def _():
            lax.fori_loop(1, 5, forward, 0)

    def forward_other(number):
        @pl.when(jnp.logical_and(active, wave == number))
        def _():
            forward(0, 0)

    send_flags(0)
    send_kv(0, 0, 8)
    send_flags(1)
    send_kv(1, 0, 8)
    send_flags(2)
    send_kv(2, 0, 4)
    forward_own(0)
    send_kv(2, 4, 8)
    send_qg(0, 0, 4)
    forward_own(1)
    send_qg(0, 4, 8)
    forward_other(0)
    forward_own(2)
    send_qg(1, 0, 4)
    forward_other(1)
    send_qg(1, 4, 8)
    forward_other(2)
    send_qg(2, 0, 8)

    def work():
        acc[...] = jnp.zeros_like(acc)
        lane = lax.broadcasted_iota(jnp.int32, (1, 128), 1)

        def mark(i, carry):
            layer = i // 6
            row = lax.rem(i, 6)
            key_t = 2 * x - 1 + layer
            key_h = 4 * part - 1 + row
            real = (key_t >= 0) & (key_t < TLAYERS) & (key_h >= 0) & (key_h < NH)
            first = jnp.where(real, (key_t * NH + key_h) * TW, 0)
            for pair in range(2):
                counts = [jnp.where(real, count_ref[first + 2 * pair + j], 0) for j in range(2)]
                until = jnp.where(lane < TILE, counts[0], counts[1] + TILE)
                valid[layer, row, pair : pair + 1, :] = jnp.where(lane < until, 1.0, 0.0)
            return carry

        lax.fori_loop(0, 24, mark, 0)

        key = lax.broadcasted_iota(jnp.int32, (128, KEYS), 1)
        flag = lax.broadcasted_iota(jnp.int32, (128, KEYS), 0)
        for pair in range(2):
            wanted = key // 128 * 4 + pair * 2 + lax.rem(key, 128) // TILE
            places[pair] = jnp.where(wanted == flag, 1.0, 0.0).astype(BF16)

        def make_bias(layer, carry):
            for a in range(2):
                wait_for(flag_all.at[layer, a], flag_sem.at[layer, a])
            for pair in range(2):
                for r in range(4):
                    if r % 2 == 0:
                        live = dot(flag_all[layer, r // 2].astype(BF16), places[pair], ((1,), (0,)))
                    ok = jnp.concatenate(
                        [valid[layer + a, r + b, pair : pair + 1, :] for a in range(3) for b in range(3)], axis=1
                    )
                    tiles = live[(r % 2) * 4 : (r % 2) * 4 + 4]
                    bias[layer, r, pair, 0:4, :] = (tiles * ok - 1.0) * BIG
            return carry

        lax.fori_loop(0, 2, make_bias, 0)

        def arrive(i, carry):
            row = row_of(i)

            @pl.when(has_low)
            def _():
                wait_for(pool.at[0, row], xsem.at[0, row])

            @pl.when(has_high)
            def _():
                wait_for(pool.at[3, row], xsem.at[1, row])

            return carry

        lax.fori_loop(0, 5, arrive, 0)

        position = lax.broadcasted_iota(jnp.int32, (TILE, HEAD_DIM), 0)

        def strip(layer, r):
            wait_for(qg.at[layer, r], qg_sem.at[layer, r])
            tile0 = ((2 * x + layer) * NH + 4 * part + r) * TW
            token_ok = jnp.concatenate([position < count_ref[tile0 + j] for j in range(TW)], axis=0)
            q = qg[layer, r, 0]
            g = qg[layer, r, 1]
            g = jnp.where(token_ok, g.astype(F32), 0.0).astype(BF16)
            scores, keys, values = [], [], []
            for pair in range(2):
                rows = slice(pair * TILE, pair * TILE + 3 * TILE)
                key = [pool[layer + a, pl.ds(r, 3), 0, pair].reshape(384, HEAD_DIM) for a in range(3)]
                value = [pool[layer + a, pl.ds(r, 3), 1, pair].reshape(384, HEAD_DIM) for a in range(3)]
                keys.append(jnp.concatenate(key, axis=0))
                values.append(jnp.concatenate(value, axis=0))
                out_of = jnp.concatenate(
                    [
                        jnp.broadcast_to(bias[layer, r, pair, pair + j : pair + j + 1, :], (TILE, KEYS))
                        for j in range(3)
                    ],
                    axis=0,
                )
                scores.append(dot(q[rows], keys[pair], ((1,), (1,))) + out_of)
            tops = [jnp.max(sc, axis=1, keepdims=True) for sc in scores]
            middle = jnp.maximum(tops[0][TILE:], tops[1][: 2 * TILE])
            top0 = jnp.concatenate([tops[0][:TILE], middle], axis=0)
            top1 = jnp.concatenate([middle, tops[1][2 * TILE :]], axis=0)
            expo = [jnp.exp2((sc - top) * EXP2_SCALE) for sc, top in zip(scores, (top0, top1))]
            sums = [jnp.sum(e, axis=1, keepdims=True) for e in expo]
            middle = sums[0][TILE:] + sums[1][: 2 * TILE]
            inv0 = 1.0 / jnp.concatenate([sums[0][:TILE], middle], axis=0)
            inv1 = 1.0 / jnp.concatenate([middle, sums[1][2 * TILE :]], axis=0)
            probs = [expo[0] * inv0, expo[1] * inv1]
            low = [p.astype(BF16) for p in probs]

            def join(a, b):
                return jnp.concatenate([a[:TILE], a[TILE:] + b[: 2 * TILE], b[2 * TILE :]], axis=0)

            attended = join(*[dot(low[i], values[i], ((1,), (0,))) for i in range(2)])
            attended = jnp.where(token_ok, attended, 0.0).astype(BF16)
            out[layer, r, 0] = attended
            delta = jnp.sum(g.astype(F32) * attended.astype(F32), axis=1, keepdims=True)
            grads = []
            for pair in range(2):
                rows = slice(pair * TILE, pair * TILE + 3 * TILE)
                dprobs = dot(g[rows], values[pair], ((1,), (1,)))
                dscores = (probs[pair] * (dprobs - delta[rows])).astype(BF16)
                grads.append(dot(dscores, keys[pair], ((1,), (0,))))
                grad_k = dot(dscores, q[rows], ((0,), (0,))).reshape(3, 3, 2 * TILE, HEAD_DIM)
                grad_v = dot(low[pair], g[rows], ((0,), (0,))).reshape(3, 3, 2 * TILE, HEAD_DIM)
                for a in range(3):
                    acc[layer + a, pl.ds(r, 3), 0, pair] += grad_k[a]
                    acc[layer + a, pl.ds(r, 3), 1, pair] += grad_v[a]
            out[layer, r, 1] = (join(*grads) * SCALE).astype(BF16)

        columns = head_columns(head)

        def seat_of(layer, row):
            there = 4 * part + row
            return x * NZ + layer * 4 + there // 2, lax.rem(there, 2) * 4

        def send_strip(layer, r):
            seat, m0 = seat_of(layer, r)

            def send_tile(j, carry):
                send(
                    out.at[layer, r, :, tile_rows(j), :], tokens.at[pl.ds(0, 2), :, columns],
                    out_send, token_sem.at[0], seat, m0 + j,
                )
                return carry

            lax.fori_loop(0, TW, send_tile, 0)

        def scaled(layer, row, i):
            return acc[layer, row, i] * (SCALE if i == 0 else 1.0)

        def has(side):
            return jnp.where(side == 0, x, NX - 1 - x) > 0

        def send_edge(i, side):
            @pl.when(has(side))
            def _():
                for j in range(2):
                    edge[side, i, j] = scaled(3 * side, row_of(i), j).astype(BF16)
                send(
                    edge.at[side, i], came.at[1 - side, i], edge_send.at[side], edge_sem.at[1 - side, i],
                    jnp.where(side == 0, low_seat, high_seat), m,
                )

        def finish(i, side):
            row = row_of(i)

            @pl.when(has(side))
            def _():
                wait_for(came.at[side, i], edge_sem.at[side, i])
                for j in range(2):
                    total[side, i, j] = (scaled(1 + side, row, j) + came[side, i, j].astype(F32)).astype(BF16)

            @pl.when(jnp.logical_not(has(side)))
            def _():
                for j in range(2):
                    total[side, i, j] = scaled(1 + side, row, j).astype(BF16)

            @pl.when(jnp.logical_and(i == 0, side == z // 4))
            def _():
                seat, m0 = seat_of(side, row - 1)

                def send_tile(j, carry):
                    src = total.at[side, i, :, j // 2, tile_rows(lax.rem(j, 2)), :]
                    dst = extra.at[:, :, columns]
                    here = jnp.logical_and(two, m0 + j == m)

                    @pl.when(here)
                    def _():
                        pltpu.make_async_copy(src, dst, extra_sem).start()

                    @pl.when(jnp.logical_not(here))
                    def _():
                        send(src, dst, near_send, extra_sem, seat, m0 + j)

                    return carry

                lax.fori_loop(0, TW, send_tile, 0)

            @pl.when(jnp.logical_and(i == 0, side != z // 4))
            def _():
                send(
                    total.at[side, i], passed.at[side],
                    part_send.at[side], part_sem.at[side], other_seat, m,
                )

            @pl.when(jnp.logical_and(i == 1, side != other_z // 4))
            def _():
                wait_for(passed.at[side], part_sem.at[side])
                total[side, i] = (total[side, i].astype(F32) + passed[side].astype(F32)).astype(BF16)

            @pl.when(i > 0)
            def _():
                seat, m0 = seat_of(side, row - 1)

                def send_tile(j, carry):
                    send(
                        total.at[side, i, :, j // 2, tile_rows(lax.rem(j, 2)), :],
                        tokens.at[pl.ds(2, 2), :, columns],
                        total_send, token_sem.at[1], seat, m0 + j,
                    )
                    return carry

                lax.fori_loop(0, TW, send_tile, 0)

        def step(i, carry):
            r = jnp.where(part == 0, 3 - i, i)

            def one(layer, carry):
                strip(layer, r)
                send_edge(i, layer)

                @pl.when(i == 3)
                def _():
                    send_edge(4, layer)

                send_strip(layer, r)

                @pl.when(jnp.logical_and(i > 0, layer == 0))
                def _():
                    finish(i - 1, 1)
                    finish(i - 1, 0)

                return carry

            return lax.fori_loop(0, 2, one, carry)

        lax.fori_loop(0, 4, step, 0)

        def last(n, carry):
            finish(3 + lax.rem(n, 2), 1 - n // 2)
            return carry

        lax.fori_loop(0, 4, last, 0)

        @pl.when(two)
        def _():
            wait_for(out.at[0, 0, :, pl.ds(0, 3 * TILE), :], near_send)

        @pl.when(jnp.logical_not(two))
        def _():
            wait_for(out.at[0, 0], near_send)

        wait_for(out, out_send)
        wait_for(total.at[:, pl.ds(1, 4)], total_send)
        for side in range(2):

            @pl.when(other_z // 4 != side)
            def _():
                wait_for(pool.at[0, 0], zsend.at[side])


            @pl.when(z // 4 != side)
            def _():
                wait_for(total.at[side, 0], part_send.at[side])


            @pl.when(has_high if side else has_low)
            def _():
                wait_for(pool.at[0, pl.ds(0, 5)], xsend.at[side])
                wait_for(edge.at[side], edge_send.at[side])

    pl.when(active)(work)

    for i, ref in enumerate((k_ref, v_ref, q_ref, g_ref)):
        wait_for(ref, send_sem.at[i])
    for i, ref in enumerate((k_ref, v_ref)):
        @pl.when(jnp.logical_and(two, active))
        def _():
            wait_for(ref.at[:, : (HEADS // 2 - 1) * HEAD_DIM], border_send.at[i])

        @pl.when(jnp.logical_and(two, jnp.logical_not(active)))
        def _():
            wait_for(ref.at[:, : HEADS // 2 * HEAD_DIM], border_send.at[i])

    for i in range(WAVES):
        wait_for(flag_mine, flag_send.at[i])
    for i in range(2):
        wait_for(tokens.at[pl.ds(2 * i, 2)], token_sem.at[i])

    @pl.when(two)
    def _():
        wait_for(extra.at[:, :, : HEADS // 2 * HEAD_DIM], extra_sem)


def relay_kernel(tokens, extra, a, b, c, d, held, more, load_sem, more_sem, store_sem):
    x, z, m = place()
    h = 2 * lax.rem(z, 4) + m // 4
    two = jnp.logical_or(h == 3, h == 4)
    loads = [pltpu.make_async_copy(tokens.at[i], held.at[i], load_sem.at[i]) for i in range(4)]
    stores = [pltpu.make_async_copy(held.at[i], ref, store_sem.at[i]) for i, ref in enumerate((a, b, c, d))]
    extras = pltpu.make_async_copy(extra, more, more_sem)

    @pl.when(two)
    def _():
        extras.start()

    for copy in loads[2:] + loads[:2]:
        copy.start()
    for i in (2, 3):
        loads[i].wait()

    @pl.when(two)
    def _():
        extras.wait()
        for head in range(HEADS):
            columns = slice(head * HEAD_DIM, (head + 1) * HEAD_DIM)

            @pl.when(worker_z(jnp.where(h == 4, 0, 1), head // 3, head % 3) // 4 == z // 4)
            def _():
                both = held[2:, :, columns].astype(F32) + more[:, :, columns].astype(F32)
                held[2:, :, columns] = both.astype(BF16)

    for i in (2, 3):
        stores[i].start()
    for i in (0, 1):
        loads[i].wait()
        stores[i].start()
    for copy in stores:
        copy.wait()


def on_device(queries, keys, values, out_grad, window_lists, valid_counts):
    any_space = pl.BlockSpec(memory_space=pl.ANY)
    dma = pltpu.SemaphoreType.DMA
    row = (2, 2, 2 * TILE, HEAD_DIM)
    tokens, extra = pl.pallas_call(
        kernel,
        out_shape=(jax.ShapeDtypeStruct((4, TILE, D), BF16), jax.ShapeDtypeStruct((2, TILE, D), BF16)),
        in_specs=[any_space] * 4
        + [pl.BlockSpec(memory_space=pltpu.VMEM), pl.BlockSpec(memory_space=pltpu.SMEM)],
        out_specs=(any_space,) * 2,
        scratch_shapes=[
            pltpu.VMEM((4, 6) + row, BF16),
            pltpu.VMEM((2, 4, 2, TW * TILE, HEAD_DIM), BF16),
            pltpu.VMEM((2, 4, 2, TW * TILE, HEAD_DIM), BF16),
            pltpu.VMEM((4, 6) + row, F32),
            pltpu.VMEM((2, 5) + row, BF16),
            pltpu.VMEM((2, 5) + row, BF16),
            pltpu.VMEM((2,) + row, BF16),
            pltpu.VMEM((2, 5) + row, BF16),
            pltpu.VMEM((8, 128), F32),
            pltpu.VMEM((2, 2, 8, 128), F32),
            pltpu.VMEM((2, 128, KEYS), BF16),
            pltpu.VMEM((4, 6, 2, 128), F32),
            pltpu.VMEM((2, 4, 2, 4, KEYS), F32),
            dma((4,)), dma((2, 4)), dma((2, 4)), dma((WAVES,)), dma((2, 2)),
            dma((2,)), dma((2, 6)), dma((2,)), dma((2,)),
            dma, dma((2,)), dma((2,)), dma((2, 5)), dma((2,)), dma((2,)), dma, dma((2,)),
            dma, dma,
        ],
        compiler_params=pltpu.CompilerParams(
            collective_id=0, has_side_effects=True, vmem_limit_bytes=56 * 1024 * 1024
        ),
        cost_estimate=pl.CostEstimate(flops=5_400_000_000, bytes_accessed=6_000_000, transcendentals=3_600_000),
        name="window_attention",
    )(queries, keys, values, out_grad, window_lists, valid_counts)

    return pl.pallas_call(
        relay_kernel,
        out_shape=(jax.ShapeDtypeStruct((TILE, D), BF16),) * 4,
        in_specs=[any_space] * 2,
        out_specs=(any_space,) * 4,
        scratch_shapes=[
            pltpu.VMEM((4, TILE, D), BF16), pltpu.VMEM((2, TILE, D), BF16), dma((4,)), dma, dma((4,)),
        ],
        name="relay",
    )(tokens, extra)


def solution(mesh):
    rows = P(("seq", "mp"), None)
    return jax.shard_map(
        on_device,
        mesh=mesh,
        in_specs=(rows, rows, rows, rows, P("seq", None), P()),
        out_specs=(rows, rows, rows, rows),
        check_vma=False,
    )
```

```python
import math

import jax
import jax.numpy as jnp
from jax import lax
from jax.experimental import pallas as pl
from jax.experimental.pallas import tpu as pltpu
from jax.sharding import PartitionSpec as P

HEADS = 24
HEAD_DIM = 128
D = HEADS * HEAD_DIM
TILE = 64
WINDOW = 27
TLAYERS = 8
NH = 8
TW = 4
TILES = TLAYERS * NH * TW
NX = 4
NZ = 8
NM = 8
WAVES = 3
KEYS = 9 * 2 * TILE
BIG = 1e30
SCALE = 1.0 / math.sqrt(HEAD_DIM)
EXP2_SCALE = SCALE / math.log(2.0)
MESH = pl.DeviceIdType.MESH
BF16 = jnp.bfloat16
F32 = jnp.float32


def place():
    seat = lax.axis_index("seq")
    m = lax.axis_index("mp")
    return seat // NZ, lax.rem(seat, NZ), m


def worker_z(part, m, wave):
    u = lax.rem(wave + 1, 2)
    v = lax.rem(m + wave // 2, 2)
    return jnp.where(part == 0, 3 - u + 4 * v, lax.rem(4 - 3 * u + 4 * v, NZ))


def work_of(z, m):
    zq = lax.rem(z, 4)
    zh = z // 4
    part = jnp.where(zq >= 2, 0, 1)
    u = jnp.where(part == 0, 3 - zq, zq)
    v = jnp.where(jnp.logical_and(part == 1, u == 0), 1 - zh, zh)
    same_v = v == lax.rem(m, 2)
    same_u = u == 1
    wave = jnp.where(same_u, jnp.where(same_v, 0, 2), 1)
    return part, wave, jnp.logical_or(same_u, same_v)


def greet(x, z, m, part, wave, active, two):
    barrier = pltpu.get_barrier_semaphore()

    def signal(seat, mm):
        pl.semaphore_signal(barrier, inc=1, device_id=(seat, mm), device_id_type=MESH)

    @pl.when(active)
    def _():
        def owner(d, carry):
            zz = 2 * part + lax.rem(d // NM, 2) + 4 * (d // (2 * NM))
            signal(x * NZ + zz, lax.rem(m + d, NM))
            return carry

        lax.fori_loop(0, 4 * NM, owner, 0)
        signal(x * NZ + worker_z(1 - part, m, wave), m)

        def border(d, carry):
            zz = 2 - part + 4 * (z // 4)
            mm = 4 * part + d

            @pl.when(jnp.logical_or(zz != z, mm != m))
            def _():
                signal(x * NZ + zz, mm)

            return carry

        lax.fori_loop(0, TW, border, 0)

        @pl.when(x > 0)
        def _():
            signal((x - 1) * NZ + z, m)

        @pl.when(x < NX - 1)
        def _():
            signal((x + 1) * NZ + z, m)

    near = 1 + jnp.where(x > 0, 1, 0) + jnp.where(x < NX - 1, 1, 0)
    others = jnp.where(two, jnp.where(active, HEADS // 2 - 1, HEADS // 2), 0)
    pl.semaphore_wait(barrier, HEADS + others + jnp.where(active, near, 0))


def wait_for(ref, sem):
    pltpu.make_async_copy(ref, ref, sem).wait()


def send(src, dst, send_sem, recv_sem, seat, m):
    pltpu.make_async_remote_copy(
        src_ref=src, dst_ref=dst, send_sem=send_sem, recv_sem=recv_sem,
        device_id=(seat, m), device_id_type=MESH,
    ).start()


def dot(a, b, dims):
    return lax.dot_general(a, b, (dims, ((), ())), preferred_element_type=F32)


def tile_rows(w):
    return pl.ds(pl.multiple_of(w * TILE, TILE), TILE)


def head_columns(head):
    return pl.ds(pl.multiple_of(head * HEAD_DIM, HEAD_DIM), HEAD_DIM)


def kernel(
    q_ref, k_ref, v_ref, g_ref, list_ref, count_ref,
    tokens, extra,
    pool, qg, out, acc, edge, came, passed, total, flag_mine, flag_all, places, valid, bias,
    send_sem, kv_sem, qg_sem, flag_send, flag_sem, xsend, xsem, zsend, zsem,
    out_send, token_sem, edge_send, edge_sem, part_send, part_sem, total_send, border_send, near_send, extra_sem,
):
    x, z, m = place()
    zh = z // 4
    zl = lax.rem(z, 4)
    h = 2 * zl + m // 4
    w = lax.rem(m, 4)
    t = 2 * x + zh
    own = zl // 2
    part, wave, active = work_of(z, m)
    head = 3 * m + wave
    has_low = x > 0
    has_high = x < NX - 1
    low_seat = (x - 1) * NZ + z
    high_seat = (x + 1) * NZ + z
    other_z = worker_z(1 - part, m, wave)
    other_seat = x * NZ + other_z
    two = jnp.logical_or(h == 3, h == 4)

    spot = lax.broadcasted_iota(jnp.int32, (8, 128), 1)
    mine = lax.broadcasted_iota(jnp.int32, (8, 128), 0)
    near_t = t + spot // 12 - 1
    near_h = 2 * zl + mine // 4 + lax.rem(spot // 4, 3) - 1
    near = (near_t * NH + near_h) * TW + lax.rem(spot, 4)
    inside = (spot < 36) & (near_t >= 0) & (near_t < TLAYERS) & (near_h >= 0) & (near_h < NH)
    near = jnp.where(inside, near, -2)
    listed = jnp.zeros((8, 128), F32)
    for j in range(WINDOW):
        listed = jnp.where(list_ref[:, j : j + 1] == near, 1.0, listed)
    flag_mine[...] = listed
    pool[...] = jnp.zeros_like(pool)
    greet(x, z, m, part, wave, active, two)

    my_rows = tile_rows(lax.rem(w, 2))

    def send_kv(number, start, stop):
        def one(j, carry):
            wm = lax.rem(j + m + z, NM)
            seat = x * NZ + worker_z(own, wm, number)
            columns = head_columns(3 * wm + number)
            row = lax.rem(h, 4)
            for i, ref in ((0, k_ref), (1, v_ref)):
                send(
                    ref.at[:, columns], pool.at[1 + zh, 1 + row, i, w // 2, my_rows, :],
                    send_sem.at[i], kv_sem.at[zh, row], seat, wm,
                )

            oz = worker_z(1 - own, wm, number)
            near = jnp.logical_and(two, oz // 4 == zh)
            here = jnp.logical_and(oz == z, wm == m)
            border = [pool.at[1 + zh, jnp.where(own == 0, 0, 5), i, w // 2, my_rows, :] for i in range(2)]

            @pl.when(jnp.logical_and(near, jnp.logical_not(here)))
            def _():
                for i, ref in ((0, k_ref), (1, v_ref)):
                    send(ref.at[:, columns], border[i], border_send.at[i], zsem.at[zh], x * NZ + oz, wm)

            @pl.when(jnp.logical_and(near, here))
            def _():
                for i, ref in ((0, k_ref), (1, v_ref)):
                    pltpu.make_async_copy(ref.at[:, columns], border[i], zsem.at[zh]).start()

            return carry

        lax.fori_loop(start, stop, one, 0)

    def send_flags(number):
        send(
            flag_mine, flag_all.at[zh, lax.rem(zl, 2)],
            flag_send.at[number], flag_sem.at[zh, lax.rem(zl, 2)],
            x * NZ + worker_z(own, m, number), m,
        )

    def send_qg(number, start, stop):
        def one(j, carry):
            wm = lax.rem(j + m + z, NM)
            seat = x * NZ + worker_z(own, wm, number)
            columns = head_columns(3 * wm + number)
            row = lax.rem(h, 4)
            for i, ref in ((0, q_ref), (1, g_ref)):
                send(
                    ref.at[:, columns], qg.at[zh, row, i, tile_rows(w), :],
                    send_sem.at[2 + i], qg_sem.at[zh, row], seat, wm,
                )
            return carry

        lax.fori_loop(start, stop, one, 0)

    def row_of(i):
        return jnp.where(part == 0, 5 - i, i)

    def forward(i, carry):
        row = row_of(i)
        for side in range(2):
            wait_for(pool.at[1 + side, row], kv_sem.at[side, row - 1])

            @pl.when(jnp.logical_and(i == 1, other_z // 4 != side))
            def _():
                send(
                    pool.at[1 + side, row], pool.at[1 + side, jnp.where(part == 0, 0, 5)],
                    zsend.at[side], zsem.at[side], other_seat, m,
                )

        @pl.when(has_low)
        def _():
            send(pool.at[1, row], pool.at[3, row], xsend.at[0], xsem.at[1, row], low_seat, m)

        @pl.when(has_high)
        def _():
            send(pool.at[2, row], pool.at[0, row], xsend.at[1], xsem.at[0, row], high_seat, m)

        return carry

    def forward_border(side):
        row = row_of(0)
        wait_for(pool.at[1 + side, row], zsem.at[side])

        @pl.when(jnp.where(side == 0, x, NX - 1 - x) > 0)
        def _():
            send(
                pool.at[1 + side, row], pool.at[3 - 3 * side, row], xsend.at[side], xsem.at[1 - side, row],
                jnp.where(side == 0, low_seat, high_seat), m,
            )

    def forward_own(number):
        @pl.when(jnp.logical_and(active, wave == number))
        def _():
            lax.fori_loop(1, 5, forward, 0)
            forward_border(z // 4)

    def forward_other(number):
        @pl.when(jnp.logical_and(active, wave == number))
        def _():
            forward_border(1 - z // 4)

    send_flags(0)
    send_kv(0, 0, 8)
    send_flags(1)
    send_kv(1, 0, 8)
    send_flags(2)
    send_kv(2, 0, 4)
    forward_own(0)
    send_kv(2, 4, 8)
    send_qg(0, 0, 4)
    forward_own(1)
    send_qg(0, 4, 8)
    forward_other(0)
    forward_own(2)
    send_qg(1, 0, 4)
    forward_other(1)
    send_qg(1, 4, 8)
    forward_other(2)
    send_qg(2, 0, 8)

    def work():
        acc[...] = jnp.zeros_like(acc)
        lane = lax.broadcasted_iota(jnp.int32, (1, 128), 1)

        def mark(i, carry):
            layer = i // 6
            row = lax.rem(i, 6)
            key_t = 2 * x - 1 + layer
            key_h = 4 * part - 1 + row
            real = (key_t >= 0) & (key_t < TLAYERS) & (key_h >= 0) & (key_h < NH)
            first = jnp.where(real, (key_t * NH + key_h) * TW, 0)
            for pair in range(2):
                counts = [jnp.where(real, count_ref[first + 2 * pair + j], 0) for j in range(2)]
                until = jnp.where(lane < TILE, counts[0], counts[1] + TILE)
                valid[layer, row, pair : pair + 1, :] = jnp.where(lane < until, 1.0, 0.0)
            return carry

        lax.fori_loop(0, 24, mark, 0)

        key = lax.broadcasted_iota(jnp.int32, (128, KEYS), 1)
        flag = lax.broadcasted_iota(jnp.int32, (128, KEYS), 0)
        for pair in range(2):
            wanted = key // 128 * 4 + pair * 2 + lax.rem(key, 128) // TILE
            places[pair] = jnp.where(wanted == flag, 1.0, 0.0).astype(BF16)

        def make_bias(layer, carry):
            for a in range(2):
                wait_for(flag_all.at[layer, a], flag_sem.at[layer, a])
            for pair in range(2):
                for r in range(4):
                    if r % 2 == 0:
                        live = dot(flag_all[layer, r // 2].astype(BF16), places[pair], ((1,), (0,)))
                    ok = jnp.concatenate(
                        [valid[layer + a, r + b, pair : pair + 1, :] for a in range(3) for b in range(3)], axis=1
                    )
                    tiles = live[(r % 2) * 4 : (r % 2) * 4 + 4]
                    bias[layer, r, pair, 0:4, :] = (tiles * ok - 1.0) * BIG
            return carry

        lax.fori_loop(0, 2, make_bias, 0)

        def arrive(i, carry):
            row = row_of(i)

            @pl.when(has_low)
            def _():
                wait_for(pool.at[0, row], xsem.at[0, row])

            @pl.when(has_high)
            def _():
                wait_for(pool.at[3, row], xsem.at[1, row])

            return carry

        lax.fori_loop(0, 5, arrive, 0)

        position = lax.broadcasted_iota(jnp.int32, (TILE, HEAD_DIM), 0)

        def strip(layer, r):
            wait_for(qg.at[layer, r], qg_sem.at[layer, r])
            tile0 = ((2 * x + layer) * NH + 4 * part + r) * TW
            token_ok = jnp.concatenate([position < count_ref[tile0 + j] for j in range(TW)], axis=0)
            q = qg[layer, r, 0]
            g = qg[layer, r, 1]
            g = jnp.where(token_ok, g.astype(F32), 0.0).astype(BF16)
            scores, keys, values = [], [], []
            for pair in range(2):
                rows = slice(pair * TILE, pair * TILE + 3 * TILE)
                key = [pool[layer + a, pl.ds(r, 3), 0, pair].reshape(384, HEAD_DIM) for a in range(3)]
                value = [pool[layer + a, pl.ds(r, 3), 1, pair].reshape(384, HEAD_DIM) for a in range(3)]
                keys.append(jnp.concatenate(key, axis=0))
                values.append(jnp.concatenate(value, axis=0))
                out_of = jnp.concatenate(
                    [
                        jnp.broadcast_to(bias[layer, r, pair, pair + j : pair + j + 1, :], (TILE, KEYS))
                        for j in range(3)
                    ],
                    axis=0,
                )
                scores.append(dot(q[rows], keys[pair], ((1,), (1,))) + out_of)
            tops = [jnp.max(sc, axis=1, keepdims=True) for sc in scores]
            middle = jnp.maximum(tops[0][TILE:], tops[1][: 2 * TILE])
            top0 = jnp.concatenate([tops[0][:TILE], middle], axis=0)
            top1 = jnp.concatenate([middle, tops[1][2 * TILE :]], axis=0)
            expo = [jnp.exp2((sc - top) * EXP2_SCALE) for sc, top in zip(scores, (top0, top1))]
            sums = [jnp.sum(e, axis=1, keepdims=True) for e in expo]
            middle = sums[0][TILE:] + sums[1][: 2 * TILE]
            inv0 = 1.0 / jnp.concatenate([sums[0][:TILE], middle], axis=0)
            inv1 = 1.0 / jnp.concatenate([middle, sums[1][2 * TILE :]], axis=0)
            probs = [expo[0] * inv0, expo[1] * inv1]
            low = [p.astype(BF16) for p in probs]

            def join(a, b):
                return jnp.concatenate([a[:TILE], a[TILE:] + b[: 2 * TILE], b[2 * TILE :]], axis=0)

            attended = join(*[dot(low[i], values[i], ((1,), (0,))) for i in range(2)])
            attended = jnp.where(token_ok, attended, 0.0).astype(BF16)
            out[layer, r, 0] = attended
            delta = jnp.sum(g.astype(F32) * attended.astype(F32), axis=1, keepdims=True)
            grads = []
            for pair in range(2):
                rows = slice(pair * TILE, pair * TILE + 3 * TILE)
                dprobs = dot(g[rows], values[pair], ((1,), (1,)))
                dscores = (probs[pair] * (dprobs - delta[rows])).astype(BF16)
                grads.append(dot(dscores, keys[pair], ((1,), (0,))))
                grad_k = dot(dscores, q[rows], ((0,), (0,))).reshape(3, 3, 2 * TILE, HEAD_DIM)
                grad_v = dot(low[pair], g[rows], ((0,), (0,))).reshape(3, 3, 2 * TILE, HEAD_DIM)
                for a in range(3):
                    acc[layer + a, pl.ds(r, 3), 0, pair] += grad_k[a]
                    acc[layer + a, pl.ds(r, 3), 1, pair] += grad_v[a]
            out[layer, r, 1] = (join(*grads) * SCALE).astype(BF16)

        columns = head_columns(head)

        def seat_of(layer, row):
            there = 4 * part + row
            return x * NZ + layer * 4 + there // 2, lax.rem(there, 2) * 4

        def send_strip(layer, r):
            seat, m0 = seat_of(layer, r)

            def send_tile(j, carry):
                send(
                    out.at[layer, r, :, tile_rows(j), :], tokens.at[pl.ds(0, 2), :, columns],
                    out_send, token_sem.at[0], seat, m0 + j,
                )
                return carry

            lax.fori_loop(0, TW, send_tile, 0)

        def scaled(layer, row, i):
            return acc[layer, row, i] * (SCALE if i == 0 else 1.0)

        def has(side):
            return jnp.where(side == 0, x, NX - 1 - x) > 0

        def send_edge(i, side):
            @pl.when(has(side))
            def _():
                for j in range(2):
                    edge[side, i, j] = scaled(3 * side, row_of(i), j).astype(BF16)
                send(
                    edge.at[side, i], came.at[1 - side, i], edge_send.at[side], edge_sem.at[1 - side, i],
                    jnp.where(side == 0, low_seat, high_seat), m,
                )

        def finish(i, side):
            row = row_of(i)

            @pl.when(has(side))
            def _():
                wait_for(came.at[side, i], edge_sem.at[side, i])
                for j in range(2):
                    total[side, i, j] = (scaled(1 + side, row, j) + came[side, i, j].astype(F32)).astype(BF16)

            @pl.when(jnp.logical_not(has(side)))
            def _():
                for j in range(2):
                    total[side, i, j] = scaled(1 + side, row, j).astype(BF16)

            @pl.when(jnp.logical_and(i == 0, side == z // 4))
            def _():
                seat, m0 = seat_of(side, row - 1)

                def send_tile(j, carry):
                    src = total.at[side, i, :, j // 2, tile_rows(lax.rem(j, 2)), :]
                    dst = extra.at[:, :, columns]
                    here = jnp.logical_and(two, m0 + j == m)

                    @pl.when(here)
                    def _():
                        pltpu.make_async_copy(src, dst, extra_sem).start()

                    @pl.when(jnp.logical_not(here))
                    def _():
                        send(src, dst, near_send, extra_sem, seat, m0 + j)

                    return carry

                lax.fori_loop(0, TW, send_tile, 0)

            @pl.when(jnp.logical_and(i == 0, side != z // 4))
            def _():
                send(
                    total.at[side, i], passed.at[side],
                    part_send.at[side], part_sem.at[side], other_seat, m,
                )

            @pl.when(jnp.logical_and(i == 1, side != other_z // 4))
            def _():
                wait_for(passed.at[side], part_sem.at[side])
                total[side, i] = (total[side, i].astype(F32) + passed[side].astype(F32)).astype(BF16)

            @pl.when(i > 0)
            def _():
                seat, m0 = seat_of(side, row - 1)

                def send_tile(j, carry):
                    send(
                        total.at[side, i, :, j // 2, tile_rows(lax.rem(j, 2)), :],
                        tokens.at[pl.ds(2, 2), :, columns],
                        total_send, token_sem.at[1], seat, m0 + j,
                    )
                    return carry

                lax.fori_loop(0, TW, send_tile, 0)

        def step(i, carry):
            r = jnp.where(part == 0, 3 - i, i)

            def one(layer, carry):
                strip(layer, r)
                send_edge(i, layer)

                @pl.when(i == 3)
                def _():
                    send_edge(4, layer)

                send_strip(layer, r)

                @pl.when(jnp.logical_and(i > 0, layer == 0))
                def _():
                    finish(i - 1, 1)
                    finish(i - 1, 0)

                return carry

            return lax.fori_loop(0, 2, one, carry)

        lax.fori_loop(0, 4, step, 0)

        def last(n, carry):
            finish(3 + lax.rem(n, 2), 1 - n // 2)
            return carry

        lax.fori_loop(0, 4, last, 0)

        @pl.when(two)
        def _():
            wait_for(out.at[0, 0, :, pl.ds(0, 3 * TILE), :], near_send)

        @pl.when(jnp.logical_not(two))
        def _():
            wait_for(out.at[0, 0], near_send)

        wait_for(out, out_send)
        wait_for(total.at[:, pl.ds(1, 4)], total_send)
        for side in range(2):

            @pl.when(other_z // 4 != side)
            def _():
                wait_for(pool.at[0, 0], zsend.at[side])


            @pl.when(z // 4 != side)
            def _():
                wait_for(total.at[side, 0], part_send.at[side])


            @pl.when(has_high if side else has_low)
            def _():
                wait_for(pool.at[0, pl.ds(0, 5)], xsend.at[side])
                wait_for(edge.at[side], edge_send.at[side])

    pl.when(active)(work)

    for i, ref in enumerate((k_ref, v_ref, q_ref, g_ref)):
        wait_for(ref, send_sem.at[i])
    for i, ref in enumerate((k_ref, v_ref)):
        @pl.when(jnp.logical_and(two, active))
        def _():
            wait_for(ref.at[:, : (HEADS // 2 - 1) * HEAD_DIM], border_send.at[i])

        @pl.when(jnp.logical_and(two, jnp.logical_not(active)))
        def _():
            wait_for(ref.at[:, : HEADS // 2 * HEAD_DIM], border_send.at[i])

    for i in range(WAVES):
        wait_for(flag_mine, flag_send.at[i])
    for i in range(2):
        wait_for(tokens.at[pl.ds(2 * i, 2)], token_sem.at[i])

    @pl.when(two)
    def _():
        wait_for(extra.at[:, :, : HEADS // 2 * HEAD_DIM], extra_sem)


def relay_kernel(tokens, extra, a, b, c, d, held, more, load_sem, more_sem, store_sem):
    x, z, m = place()
    h = 2 * lax.rem(z, 4) + m // 4
    two = jnp.logical_or(h == 3, h == 4)
    loads = [pltpu.make_async_copy(tokens.at[i], held.at[i], load_sem.at[i]) for i in range(4)]
    stores = [pltpu.make_async_copy(held.at[i], ref, store_sem.at[i]) for i, ref in enumerate((a, b, c, d))]
    extras = pltpu.make_async_copy(extra, more, more_sem)

    @pl.when(two)
    def _():
        extras.start()

    for copy in loads[2:] + loads[:2]:
        copy.start()
    for i in (2, 3):
        loads[i].wait()

    @pl.when(two)
    def _():
        extras.wait()
        for head in range(HEADS):
            columns = slice(head * HEAD_DIM, (head + 1) * HEAD_DIM)

            @pl.when(worker_z(jnp.where(h == 4, 0, 1), head // 3, head % 3) // 4 == z // 4)
            def _():
                both = held[2:, :, columns].astype(F32) + more[:, :, columns].astype(F32)
                held[2:, :, columns] = both.astype(BF16)

    for i in (2, 3):
        stores[i].start()
    for i in (0, 1):
        loads[i].wait()
        stores[i].start()
    for copy in stores:
        copy.wait()


def on_device(queries, keys, values, out_grad, window_lists, valid_counts):
    any_space = pl.BlockSpec(memory_space=pl.ANY)
    dma = pltpu.SemaphoreType.DMA
    row = (2, 2, 2 * TILE, HEAD_DIM)
    tokens, extra = pl.pallas_call(
        kernel,
        out_shape=(jax.ShapeDtypeStruct((4, TILE, D), BF16), jax.ShapeDtypeStruct((2, TILE, D), BF16)),
        in_specs=[any_space] * 4
        + [pl.BlockSpec(memory_space=pltpu.VMEM), pl.BlockSpec(memory_space=pltpu.SMEM)],
        out_specs=(any_space,) * 2,
        scratch_shapes=[
            pltpu.VMEM((4, 6) + row, BF16),
            pltpu.VMEM((2, 4, 2, TW * TILE, HEAD_DIM), BF16),
            pltpu.VMEM((2, 4, 2, TW * TILE, HEAD_DIM), BF16),
            pltpu.VMEM((4, 6) + row, F32),
            pltpu.VMEM((2, 5) + row, BF16),
            pltpu.VMEM((2, 5) + row, BF16),
            pltpu.VMEM((2,) + row, BF16),
            pltpu.VMEM((2, 5) + row, BF16),
            pltpu.VMEM((8, 128), F32),
            pltpu.VMEM((2, 2, 8, 128), F32),
            pltpu.VMEM((2, 128, KEYS), BF16),
            pltpu.VMEM((4, 6, 2, 128), F32),
            pltpu.VMEM((2, 4, 2, 4, KEYS), F32),
            dma((4,)), dma((2, 4)), dma((2, 4)), dma((WAVES,)), dma((2, 2)),
            dma((2,)), dma((2, 6)), dma((2,)), dma((2,)),
            dma, dma((2,)), dma((2,)), dma((2, 5)), dma((2,)), dma((2,)), dma, dma((2,)),
            dma, dma,
        ],
        compiler_params=pltpu.CompilerParams(
            collective_id=0, has_side_effects=True, vmem_limit_bytes=56 * 1024 * 1024
        ),
        cost_estimate=pl.CostEstimate(flops=5_400_000_000, bytes_accessed=6_000_000, transcendentals=3_600_000),
        name="window_attention",
    )(queries, keys, values, out_grad, window_lists, valid_counts)

    return pl.pallas_call(
        relay_kernel,
        out_shape=(jax.ShapeDtypeStruct((TILE, D), BF16),) * 4,
        in_specs=[any_space] * 2,
        out_specs=(any_space,) * 4,
        scratch_shapes=[
            pltpu.VMEM((4, TILE, D), BF16), pltpu.VMEM((2, TILE, D), BF16), dma((4,)), dma, dma((4,)),
        ],
        name="relay",
    )(tokens, extra)


def solution(mesh):
    rows = P(("seq", "mp"), None)
    return jax.shard_map(
        on_device,
        mesh=mesh,
        in_specs=(rows, rows, rows, rows, P("seq", None), P()),
        out_specs=(rows, rows, rows, rows),
        check_vma=False,
    )
```
